32 devices in a mesh: dp: 8 (over z, x), ctx: 2 (over core), tp: 2 (over y).
Axes of the slice: x: 2, y: 2, z: 4, core: 2. Of those that a mesh axis runs over, the one named last changes fastest.
Arguments:
- tokens: bfloat16 [32, 512, 1024], P('dp', 'ctx'), may hold values from -6 to 6
- segments: int32 [32, 512], P('dp'), may hold values from 0 to 6, as said below
- query_weight: float32 [1024, 1024], P(('dp', 'ctx'), 'tp'), may hold values from -0.1875 to 0.1875
- key_weight: float32 [1024, 1024], P(('dp', 'ctx'), 'tp'), may hold values from -0.1875 to 0.1875
- value_weight: float32 [1024, 1024], P(('dp', 'ctx'), 'tp'), may hold values from -0.1875 to 0.1875
- out_weight: float32 [1024, 1024], P('tp', ('dp', 'ctx')), may hold values from -0.75 to 0.75
- up_weight: float32 [1024, 4096], P(('dp', 'ctx'), 'tp'), may hold values from -0.1875 to 0.1875
- down_weight: float32 [4096, 1024], P('tp', ('dp', 'ctx')), may hold values from -0.125 to 0.125
- query_bias: float32 [1024], P('tp'), may hold values from -3 to 3
- value_bias: float32 [1024], P('tp'), may hold values from -3 to 3
- out_bias: float32 [1024], replicated, may hold values from -3 to 3
- up_bias: float32 [4096], P('tp'), may hold values from -3 to 3
- down_bias: float32 [1024], replicated, may hold values from -3 to 3
- attn_gain: float32 [1024], replicated, may hold values from 0.5 to 1.5
- attn_shift: float32 [1024], replicated, may hold values from -3 to 3
- mlp_gain: float32 [1024], replicated, may hold values from 0.5 to 1.5
- mlp_shift: float32 [1024], replicated, may hold values from -3 to 3
- cotangent: bfloat16 [32, 512, 1024], P('dp', 'ctx'), may hold values from -6 to 6
Outputs:
- layer_out: bfloat16 [32, 512, 1024], P('dp', 'ctx')
- input_grad: bfloat16 [32, 512, 1024], P('dp', 'ctx')
- query_grad: float32 [1024, 1024], P(('dp', 'ctx'), 'tp')
- key_grad: float32 [1024, 1024], P(('dp', 'ctx'), 'tp')
- value_grad: float32 [1024, 1024], P(('dp', 'ctx'), 'tp')
- out_grad: float32 [1024, 1024], P('tp', ('dp', 'ctx'))
- up_grad: float32 [1024, 4096], P(('dp', 'ctx'), 'tp')
- down_grad: float32 [4096, 1024], P('tp', ('dp', 'ctx'))
- query_bias_grad: float32 [1024], P('tp')
- value_bias_grad: float32 [1024], P('tp')
- out_bias_grad: float32 [1024], replicated
- up_bias_grad: float32 [4096], P('tp')
- down_bias_grad: float32 [1024], replicated
- attn_gain_grad: float32 [1024], replicated
- attn_shift_grad: float32 [1024], replicated
- mlp_gain_grad: float32 [1024], replicated
- mlp_shift_grad: float32 [1024], replicated
The draws below stay inside these ranges and needn't reach their ends.
Inputs may be any that keep to these rules, and one draw needn't show every extreme that they name: `segments`: segment numbers never fall along a sequence; every sequence holds a document that covers positions 128 to 384.
All inputs are finite; a program needn't handle non-finite values.
Results may differ from the reference program's by a relative error of at most 0.018.
Values may be sent and summed in bfloat16 or wider, within the bound.
No kernel may reach another device: no remote copies, remote signals or barrier semaphores. Data moves between devices by JAX's collectives and lax.ppermute only.
A program may use at most 192 MiB of HBM per device.

```python
import math
import jax
import jax.numpy as jnp
from jax import lax

D = 1024
HEADS = 16
HEAD_DIM = 64
FF = 4096
LEN = 512
CUTS = 6
SEQS = 32


def draw_segments(key, part):
    key = jax.random.fold_in(key, 11)
    first_key, second_key = jax.random.split(key)
    lower = jax.random.randint(first_key, (SEQS, CUTS // 2), 1, LEN // 4)
    upper = jax.random.randint(second_key, (SEQS, CUTS - CUTS // 2), 3 * LEN // 4 + 1, LEN)
    boundary = jnp.concatenate([lower, upper], axis=1).astype(jnp.int32)
    position = jnp.arange(LEN, dtype=jnp.int32)
    return jnp.sum((boundary[:, None, :] <= position[None, :, None]).astype(jnp.int32), axis=2)


def block_levels(own_key, extent, pieces, least, high):
    level, own = 1.0, jax.random.fold_in(own_key, 6)
    for axis_at, shards_of in pieces:
        heights = jnp.exp(jax.random.uniform(jax.random.fold_in(own, axis_at), (shards_of,), jnp.float32, least / len(pieces), high / len(pieces)))
        level = level * jnp.repeat(heights, extent[axis_at] // shards_of).reshape([-1 if axis == axis_at else 1 for axis in range(len(extent))])
    return level


def noise(stream_key, extent, width, limit, shards=(), kind=jnp.bfloat16):
    drawn = width * jax.random.normal(stream_key, extent, jnp.float32)
    if shards:
        drawn = drawn * block_levels(stream_key, extent, shards, -0.22, 0.18)
    return jnp.clip(drawn, -limit, limit).astype(kind)


def setup_inputs(seed: int = 0) -> dict:
    arg_keys = jax.random.split(jax.random.key(seed), 19)
    return {
        "tokens": noise(arg_keys[0], (SEQS, LEN, D), 1.0, 6.0, ((0, 8), (1, 2))),
        "segments": draw_segments(jax.random.fold_in(arg_keys[18], 71), 0),
        "query_weight": noise(arg_keys[2], (D, D), D ** -0.5, 0.1875, ((0, 16), (1, 2)), jnp.float32),
        "key_weight": noise(arg_keys[3], (D, D), D ** -0.5, 0.1875, ((0, 16), (1, 2)), jnp.float32),
        "value_weight": noise(arg_keys[4], (D, D), D ** -0.5, 0.1875, ((0, 16), (1, 2)), jnp.float32),
        "out_weight": noise(arg_keys[5], (D, D), (D // 16) ** -0.5, 0.75, ((0, 2), (1, 16)), jnp.float32),
        "up_weight": noise(arg_keys[6], (D, FF), D ** -0.5, 0.1875, ((0, 16), (1, 2)), jnp.float32),
        "down_weight": noise(arg_keys[7], (FF, D), (FF // 2) ** -0.5, 0.125, ((0, 2), (1, 16)), jnp.float32),
        "query_bias": noise(arg_keys[8], (D,), 0.5, 3.0, ((0, 2),), jnp.float32),
        "value_bias": noise(arg_keys[9], (D,), 0.5, 3.0, ((0, 2),), jnp.float32),
        "out_bias": noise(arg_keys[10], (D,), 0.5, 3.0, (), jnp.float32),
        "up_bias": noise(arg_keys[11], (FF,), 0.5, 3.0, ((0, 2),), jnp.float32),
        "down_bias": noise(arg_keys[12], (D,), 0.5, 3.0, (), jnp.float32),
        "attn_gain": jnp.clip(1.0 + 0.1 * jax.random.normal(arg_keys[13], (D,), jnp.float32), 0.5, 1.5),
        "attn_shift": noise(arg_keys[14], (D,), 0.5, 3.0, (), jnp.float32),
        "mlp_gain": jnp.clip(1.0 + 0.1 * jax.random.normal(arg_keys[15], (D,), jnp.float32), 0.5, 1.5),
        "mlp_shift": noise(arg_keys[16], (D,), 0.5, 3.0, (), jnp.float32),
        "cotangent": noise(arg_keys[17], (SEQS, LEN, D), 1.0, 6.0, ((0, 8), (1, 2))),
    }


epsilon = 1e-12
root_half = 0.7071067811865476

@jax.custom_vjp
def low(v):
    return lax.optimization_barrier(v.astype(jnp.bfloat16)).astype(jnp.float32)

@jax.custom_vjp
def low_back(v):
    return v

def low_keep(v):
    return (low(v), None)

def low_pass(kept, grad):
    return (grad,)

def back_keep(v):
    return (v, None)

def back_low(kept, grad):
    return (low(grad),)
low.defvjp(low_keep, low_pass)
low_back.defvjp(back_keep, back_low)

def product(left, right):
    return jnp.dot(left, right, precision=lax.Precision.HIGHEST)

def layer_norm(values, gain, shift):
    centre = values - lax.optimization_barrier(jnp.mean(values, axis=-1, keepdims=True))
    spread = lax.optimization_barrier(jnp.mean(centre * centre, axis=-1, keepdims=True))
    return centre * lax.rsqrt(spread + epsilon) * gain + shift

def group_layer(inputs, segment_ids, params):
    query_weight, key_weight, value_weight, out_weight, up_weight, down_weight, query_bias, value_bias, out_bias, up_bias, down_bias, attn_gain, attn_shift, mlp_gain, mlp_shift = params
    group_seqs = inputs.shape[0]
    flat_rows = inputs.reshape(group_seqs * LEN, D)
    queries = low(low_back(product(flat_rows, low(query_weight)) + query_bias))
    keys = low(low_back(product(flat_rows, low(key_weight))))
    values = low(low_back(product(flat_rows, low(value_weight)) + value_bias))
    head_shape = (group_seqs, LEN, HEADS, HEAD_DIM)
    scores = jnp.einsum('gqhd,gkhd->ghqk', queries.reshape(head_shape), keys.reshape(head_shape), precision=lax.Precision.HIGHEST)
    scores = low_back(scores * HEAD_DIM ** (-0.5))
    allowed = segment_ids[:, None, :, None] == segment_ids[:, None, None, :]
    scores = jnp.where(allowed, scores, -1000000000.0)
    largest = lax.optimization_barrier(jnp.max(scores, axis=-1, keepdims=True))
    raised = jnp.exp(scores - largest)
    attention = raised / lax.optimization_barrier(jnp.sum(raised, axis=-1, keepdims=True))
    context = jnp.einsum('ghqk,gkhd->gqhd', low(attention), values.reshape(head_shape), precision=lax.Precision.HIGHEST).reshape(group_seqs * LEN, D)
    context = low(low_back(context))
    attended = low_back(product(context, low(out_weight))) + out_bias
    normed_one = layer_norm(flat_rows + attended, attn_gain, attn_shift)
    hidden_pre = low_back(product(low(normed_one), low(up_weight)) + up_bias)
    hidden_act = low(0.5 * hidden_pre * (1.0 + lax.erf(hidden_pre * root_half)))
    mixed = low_back(product(hidden_act, low(down_weight))) + down_bias
    result = layer_norm(normed_one + mixed, mlp_gain, mlp_shift)
    return result.reshape(group_seqs, LEN, D)

def reference(tokens, segments, query_weight, key_weight, value_weight, out_weight, up_weight, down_weight, query_bias, value_bias, out_bias, up_bias, down_bias, attn_gain, attn_shift, mlp_gain, mlp_shift, cotangent):
    params = tuple((member.astype(jnp.float32) for member in (query_weight, key_weight, value_weight, out_weight, up_weight, down_weight, query_bias, value_bias, out_bias, up_bias, down_bias, attn_gain, attn_shift, mlp_gain, mlp_shift)))
    group_size = math.gcd(SEQS, 8)
    groups = SEQS // group_size

    def forward(inputs, weights):
        shaped = inputs.reshape(groups, group_size, LEN, D)
        seg_groups = segments.reshape(groups, group_size, LEN)

        def one_group(grouped):
            return group_layer(grouped[0], grouped[1], weights)
        return lax.map(jax.checkpoint(one_group), (shaped, seg_groups)).reshape(SEQS, LEN, D)
    result, pullback = jax.vjp(forward, tokens.astype(jnp.float32), params)
    token_grad, grads = pullback(cotangent.astype(jnp.float32))
    query_grad, key_grad, value_grad, out_grad, up_grad, down_grad, query_bias_grad, value_bias_grad, out_bias_grad, up_bias_grad, down_bias_grad, attn_gain_grad, attn_shift_grad, mlp_gain_grad, mlp_shift_grad = grads
    return (result.astype(jnp.bfloat16), token_grad.astype(jnp.bfloat16), query_grad, key_grad, value_grad, out_grad, up_grad, down_grad, query_bias_grad, value_bias_grad, out_bias_grad, up_bias_grad, down_bias_grad, attn_gain_grad, attn_shift_grad, mlp_gain_grad, mlp_shift_grad)
```

```python
import jax
import jax.numpy as jnp
from jax import lax
from jax.sharding import PartitionSpec as P

HEAD_DIM = 64

epsilon = 1e-12
root_half = 0.7071067811865476
inv_root_two_pi = 0.3989422804014327
bf16 = jnp.bfloat16
f32 = jnp.float32


def matmul(left, right):
    return jnp.dot(left, right, preferred_element_type=f32)


def rows_product(left, right):
    return lax.dot_general(left, right, (((0,), (0,)), ((), ())), preferred_element_type=f32)


def cols_product(left, right):
    return lax.dot_general(left, right, (((1,), (1,)), ((), ())), preferred_element_type=f32)


def norm_forward(values, gain, shift):
    centre = values - jnp.mean(values, axis=-1, keepdims=True)
    inverse = lax.rsqrt(jnp.mean(centre * centre, axis=-1, keepdims=True) + epsilon)
    normed = centre * inverse
    return (normed * gain + shift, normed, inverse)


def norm_backward(upstream, normed, inverse, gain):
    scaled = upstream * gain
    inner = scaled - jnp.mean(scaled, axis=-1, keepdims=True)
    inner = inner - normed * jnp.mean(scaled * normed, axis=-1, keepdims=True)
    return (inner * inverse, jnp.sum(upstream * normed, axis=0), jnp.sum(upstream, axis=0))


def swap(values, axis):
    return lax.ppermute(values, axis, [(0, 1), (1, 0)])


def take(values, index, axis):
    return lax.dynamic_index_in_dim(values, index, axis, keepdims=False)


def add(left, right):
    return (left.astype(f32) + right.astype(f32)).astype(bf16)


def gather_all(shard):
    full = lax.all_gather(shard, ("tp", "dp", "ctx"), axis=0, tiled=True)
    return full.reshape(2, -1, shard.shape[-1])


def scatter_sum(grad, dp_count):
    rows, _, cols = grad.shape
    t = lax.axis_index("tp")
    if dp_count != 8:
        mine = lax.psum_scatter(grad, "tp", scatter_dimension=1, tiled=True)
        mine = mine.reshape(rows, cols)
        return lax.psum_scatter(mine, "dp", scatter_dimension=0, tiled=True).astype(f32)
    d = lax.axis_index("dp")
    x, z = d % 2, d // 2
    piece = rows // 8
    blocks = grad.reshape(2, 2, 2, piece, 2, cols)
    over_x = [(i, i ^ 1) for i in range(8)]
    first, second = blocks[0], blocks[1]
    got = swap(take(first, 1 - t, 3), "tp")
    got_b = lax.ppermute(take(second, 1 - x, 1), "dp", over_x)
    first = add(take(first, t, 3), got)
    second = add(take(second, x, 1), got_b)
    got = lax.ppermute(take(first, 1 - x, 1), "dp", over_x)
    got_b = swap(take(second, 1 - t, 2), "tp")
    first = add(take(first, x, 1), got)
    second = add(take(second, t, 2), got_b)
    line = jnp.concatenate([first, second], axis=0)
    total = take(line, z, 0).astype(f32)
    for step in range(1, 4):
        pairs = [(i, (i + 2 * step) % 8) for i in range(8)]
        got = lax.ppermute(take(line, (z + step) % 4, 0), "dp", pairs)
        total = total + got.astype(f32)
    return total


def to_shard(total, c):
    halves = total.reshape(2, total.shape[0] // 2, total.shape[1])
    mine = take(halves, c, 0)
    other = swap(take(halves, 1 - c, 0), "ctx")
    ordered = jnp.where(c == 0, jnp.stack([mine, other], 1), jnp.stack([other, mine], 1))
    return ordered


def body(dp_count, tokens, segments, query_weight, key_weight, value_weight, out_weight, up_weight, down_weight, query_bias, value_bias, out_bias, up_bias, down_bias, attn_gain, attn_shift, mlp_gain, mlp_shift, cotangent):
    c = lax.axis_index("ctx")
    t = lax.axis_index("tp")
    half, width = tokens.shape[1], tokens.shape[2]
    rows = 2 * half
    factor = HEAD_DIM ** (-0.5)
    heads = 2 * query_bias.shape[0] // HEAD_DIM
    ff = 2 * up_bias.shape[0]
    inner = heads * HEAD_DIM

    shard_one = jnp.concatenate([query_weight, key_weight, value_weight, out_weight.T], 1).astype(bf16)
    full_one = gather_all(shard_one)
    full_up = gather_all(up_weight.astype(bf16))
    full_down = gather_all(down_weight.T.astype(bf16))
    hin = inner // 2

    seq = 2 * t + c
    other_seq = 2 * t + 1 - c
    mine_pair = jnp.stack([take(tokens, seq, 0), take(cotangent, seq, 0)])
    send_pair = jnp.stack([take(tokens, other_seq, 0), take(cotangent, other_seq, 0)])
    got_pair = swap(send_pair, "ctx")
    flat = jnp.concatenate([mine_pair[0], got_pair[0]], 0)
    grad_output = jnp.concatenate([mine_pair[1], got_pair[1]], 0).astype(f32)
    seg = take(segments, seq, 0)
    seg = jnp.where(c == 0, seg, jnp.roll(seg, half))
    allowed = seg[:, None] == seg[None, :]

    bias_q = lax.all_gather(query_bias, "tp", axis=0, tiled=True)
    bias_v = lax.all_gather(value_bias, "tp", axis=0, tiled=True)
    bias_up = lax.all_gather(up_bias, "tp", axis=0, tiled=True)

    def whole(part):
        return jnp.concatenate([part[0], part[1]], axis=1)

    w_q = whole(full_one[:, :, :hin])
    w_k = whole(full_one[:, :, hin : 2 * hin])
    w_v = whole(full_one[:, :, 2 * hin : 3 * hin])
    w_ot = whole(full_one[:, :, 3 * hin :])
    w_up = whole(full_up)
    w_dt = whole(full_down)

    queries = (matmul(flat, w_q) + bias_q).astype(bf16)
    keys = matmul(flat, w_k).astype(bf16)
    values = (matmul(flat, w_v) + bias_v).astype(bf16)
    qh = queries.reshape(rows, heads, HEAD_DIM)
    kh = keys.reshape(rows, heads, HEAD_DIM)
    vh = values.reshape(rows, heads, HEAD_DIM)
    scores = jnp.einsum("qhd,khd->hqk", qh, kh, preferred_element_type=f32)
    scores = jnp.where(allowed, scores * factor, -1000000000.0)
    raised = jnp.exp(scores - jnp.max(scores, axis=-1, keepdims=True))
    probs = (raised / jnp.sum(raised, axis=-1, keepdims=True)).astype(bf16)
    context = jnp.einsum("hqk,khd->qhd", probs, vh, preferred_element_type=f32)
    context = context.reshape(rows, -1).astype(bf16)
    resid_one = flat.astype(f32) + cols_product(context, w_ot) + out_bias
    normed_one, unit_one, inverse_one = norm_forward(resid_one, attn_gain, attn_shift)
    normed_low = normed_one.astype(bf16)
    hidden_pre = matmul(normed_low, w_up) + bias_up
    erf_part = lax.erf(hidden_pre * root_half)
    hidden_act = (0.5 * hidden_pre * (1.0 + erf_part)).astype(bf16)
    slope = (0.5 * (1.0 + erf_part) + hidden_pre * jnp.exp(-0.5 * hidden_pre * hidden_pre) * inv_root_two_pi)
    resid_two = normed_one + cols_product(hidden_act, w_dt) + down_bias
    output, unit_two, inverse_two = norm_forward(resid_two, mlp_gain, mlp_shift)
    grad_two, mlp_gain_term, mlp_shift_term = norm_backward(grad_output, unit_two, inverse_two, mlp_gain)
    grad_mixed = grad_two.astype(bf16)
    down_bias_term = jnp.sum(grad_two, axis=0)
    grad_pre = (matmul(grad_mixed, w_dt) * slope).astype(bf16)
    up_bias_term = jnp.sum(grad_pre.astype(f32), axis=0)

    def both(values):
        return jnp.concatenate([values, swap(values, "ctx")], 0)

    def halves(values):
        parts = values.reshape(rows, 2, 2, -1)
        return jnp.concatenate([take(parts, c, 2), swap(take(parts, 1 - c, 2), "ctx")], 0)

    def grads(left, right):
        out = rows_product(left, right.reshape(2 * rows, -1)).astype(bf16)
        return out.reshape(width, 2, -1)

    down_total = scatter_sum(grads(both(grad_mixed), halves(hidden_act)), dp_count)
    up_total = scatter_sum(grads(both(normed_low), halves(grad_pre)), dp_count)

    grad_normed = grad_two + cols_product(grad_pre, w_up)
    grad_one, attn_gain_term, attn_shift_term = norm_backward(grad_normed, unit_one, inverse_one, attn_gain)
    grad_attended = grad_one.astype(bf16)
    out_bias_term = jnp.sum(grad_one, axis=0)
    grad_context = matmul(grad_attended, w_ot).astype(bf16).reshape(rows, heads, HEAD_DIM)
    grad_probs = jnp.einsum("qhd,khd->hqk", grad_context, vh, preferred_element_type=f32)
    probs_wide = probs.astype(f32)
    row_inner = jnp.sum(probs_wide * grad_probs, axis=-1, keepdims=True)
    grad_scores = (probs_wide * (grad_probs - row_inner)).astype(bf16)
    grad_q = jnp.einsum("hqk,khd->qhd", grad_scores, kh, preferred_element_type=f32) * factor
    grad_k = jnp.einsum("hqk,qhd->khd", grad_scores, qh, preferred_element_type=f32) * factor
    grad_v = jnp.einsum("hqk,qhd->khd", probs, grad_context, preferred_element_type=f32)
    grad_q = grad_q.reshape(rows, -1).astype(bf16)
    grad_k = grad_k.reshape(rows, -1).astype(bf16)
    grad_v = grad_v.reshape(rows, -1).astype(bf16)
    query_bias_term = jnp.sum(grad_q.astype(f32), axis=0)
    value_bias_term = jnp.sum(grad_v.astype(f32), axis=0)
    sent_back = cols_product(grad_q, w_q) + cols_product(grad_k, w_k) + cols_product(grad_v, w_v)
    input_grad = (grad_one + sent_back).astype(bf16)

    both_x = both(flat)
    one_grad = jnp.concatenate(
        [grads(both_x, halves(grad_q)), grads(both_x, halves(grad_k)), grads(both_x, halves(grad_v)), grads(both(grad_attended), halves(context))],
        axis=2,
    )
    one_total = scatter_sum(one_grad, dp_count)

    small = jnp.concatenate(
        [query_bias_term, value_bias_term, up_bias_term, out_bias_term, down_bias_term, attn_gain_term, attn_shift_term, mlp_gain_term, mlp_shift_term]
    )
    small = lax.psum(small.reshape(-1, 128), ("dp", "ctx", "tp")).reshape(-1)

    def cut(start, size):
        return lax.slice_in_dim(small, start, start + size)

    def cut_tp(start, size):
        return lax.dynamic_slice_in_dim(small, start + t * (size // 2), size // 2)

    at = 2 * inner + ff
    vectors = [cut(at + i * width, width) for i in range(6)]

    def spread(values):
        mine, theirs = values[:half], values[half:]
        got = swap(theirs, "ctx")
        pair = jnp.where(c == 0, jnp.stack([mine, got]), jnp.stack([got, mine]))
        far = swap(pair, "tp")
        return jnp.where(t == 0, jnp.concatenate([pair, far]), jnp.concatenate([far, pair]))

    one_shard = to_shard(one_total, c)
    r = one_shard.shape[0]
    one_shard = one_shard.reshape(r, 2, 4, -1).transpose(2, 0, 1, 3).reshape(4, r, -1)
    up_shard = to_shard(up_total, c).reshape(r, -1)
    down_shard = to_shard(down_total, c).reshape(r, -1).T
    return (
        spread(output.astype(bf16)),
        spread(input_grad),
        one_shard[0],
        one_shard[1],
        one_shard[2],
        one_shard[3].T,
        up_shard,
        down_shard,
        cut_tp(0, inner),
        cut_tp(inner, inner),
        vectors[0],
        cut_tp(2 * inner, ff),
        *vectors[1:],
    )


def solution(mesh):
    weight_in, weight_out = P(("dp", "ctx"), "tp"), P("tp", ("dp", "ctx"))
    rows = P("dp", "ctx", None)
    weights = (weight_in, weight_in, weight_in, weight_out, weight_in, weight_out)
    vectors = (P("tp"), P("tp"), P(), P("tp"), P(), P(), P(), P(), P())
    dp_count = mesh.shape["dp"]

    def run(*args):
        return body(dp_count, *args)

    return jax.shard_map(
        run,
        mesh=mesh,
        in_specs=(rows, P("dp", None), *weights, *vectors, rows),
        out_specs=(rows, rows, *weights, *vectors),
        check_vma=False,
    )
```

```python
import functools

import jax
import jax.numpy as jnp
from jax import lax
from jax.experimental import pallas as pl
from jax.experimental.pallas import tpu as pltpu
from jax.sharding import PartitionSpec as P

HEAD_DIM = 64
LANES = 2 * HEAD_DIM

epsilon = 1e-12
root_half = 0.7071067811865476
inv_root_two_pi = 0.3989422804014327
bf16 = jnp.bfloat16
f32 = jnp.float32


def dot(left, right, left_dim, right_dim):
    return lax.dot_general(left, right, (((left_dim,), (right_dim,)), ((), ())), preferred_element_type=f32)


def norm_forward(values, gain, shift):
    centre = values - jnp.mean(values, axis=-1, keepdims=True)
    inverse = lax.rsqrt(jnp.mean(centre * centre, axis=-1, keepdims=True) + epsilon)
    normed = centre * inverse
    return (normed * gain + shift, normed, inverse)


def norm_backward(upstream, normed, inverse, gain):
    scaled = upstream * gain
    inner = scaled - jnp.mean(scaled, axis=-1, keepdims=True)
    inner = inner - normed * jnp.mean(scaled * normed, axis=-1, keepdims=True)
    return (inner * inverse, jnp.sum(upstream * normed, axis=0), jnp.sum(upstream, axis=0))


def swap(values, axis):
    return lax.ppermute(values, axis, [(0, 1), (1, 0)])


def swap_x(values):
    return lax.ppermute(values, "dp", [(i, i ^ 1) for i in range(8)])


def shift_z(values, step):
    return lax.ppermute(values, "dp", [(i, (i + 2 * step) % 8) for i in range(8)])


def take(values, index, axis=0):
    return lax.dynamic_index_in_dim(values, index, axis, keepdims=False)


def add(left, right):
    return (left.astype(f32) + right.astype(f32)).astype(bf16)


def order(index, mine, other, axis):
    return jnp.where(index == 0, jnp.concatenate([mine, other], axis), jnp.concatenate([other, mine], axis))


def assemble_kernel(cuts, place, one, one_y, two, two_x, *rest):
    outs, sems = rest[: len(cuts)], rest[len(cuts)]
    z, x = place[0], place[1]
    rows = one.shape[2]
    for k in range(4):
        for far_x in range(2):
            block = lax.rem(z + 4 - k, 4) * 2 + lax.rem(x + far_x, 2)
            at = pl.ds(pl.multiple_of(block * rows, rows), rows)
            for far_t in range(2):
                if k < 2:
                    source = (one_y if far_t else one).at[far_x, k]
                else:
                    source = (two_x if far_x else two).at[far_t, k - 2]
                for n, (start, size) in enumerate(cuts):
                    pltpu.make_async_copy(
                        source.at[:, start : start + size],
                        outs[n].at[at, far_t * size : far_t * size + size],
                        sems.at[n],
                    ).start()
    for n in range(len(cuts)):
        pltpu.make_async_copy(outs[n], outs[n], sems.at[n]).wait()


def gather_weights(piece, cuts, place, dp_count):
    rows, cols = piece.shape
    total = dp_count * rows
    if dp_count != 8:
        t = lax.axis_index("tp")
        both = lax.all_gather(piece, ("tp", "dp"), axis=0, tiled=True).reshape(2, total, cols)
        first, second = take(both, t), take(both, 1 - t)
        return [
            jnp.concatenate([first[:, s : s + n], second[:, s : s + n]], 1) for s, n in cuts
        ]
    line = [piece] + [shift_z(piece, k) for k in range(1, 4)]
    one, two = jnp.stack(line[:2]), jnp.stack(line[2:])
    one_x, two_y = swap_x(one), swap(two, "tp")
    one, two = jnp.stack([one, one_x]), jnp.stack([two, two_y])
    one_y, two_x = swap(one, "tp"), swap_x(two)
    anyspace = pl.BlockSpec(memory_space=pl.ANY)


    return pl.pallas_call(
        functools.partial(assemble_kernel, cuts),
        out_shape=[jax.ShapeDtypeStruct((total, 2 * n), bf16) for _, n in cuts],
        in_specs=[pl.BlockSpec(memory_space=pltpu.SMEM)] + [anyspace] * 4,
        out_specs=[anyspace] * len(cuts),
        scratch_shapes=[pltpu.SemaphoreType.DMA((len(cuts),))],
        name="assemble",
    )(place, one, one_y, two, two_x)


def attend_kernel(qkv, seg_keys, seg_queries, context, probs, bias):
    quarter = qkv.shape[1] // 3

    @pl.when(pl.program_id(0) == 0)
    def _():
        bias[...] = jnp.where(seg_keys[...] == seg_queries[...], 0.0, -1000000000.0)

    low = lax.broadcasted_iota(jnp.int32, (1, LANES), 1) < HEAD_DIM
    for pair in range(quarter // LANES):
        cols = slice(pair * LANES, pair * LANES + LANES)
        query = qkv[:, cols] * 0.125
        key = qkv[:, quarter + pair * LANES : quarter + pair * LANES + LANES]
        value_t = qkv[:, 2 * quarter + pair * LANES : 2 * quarter + pair * LANES + LANES].T
        parts = []
        for h in range(2):
            mine = jnp.where(low if h == 0 else ~low, query, jnp.zeros_like(query))
            scores = dot(key, mine, 1, 1) + bias[...]
            raised = jnp.exp(scores - jnp.max(scores, axis=0, keepdims=True))
            prob = (raised * (1.0 / jnp.sum(raised, axis=0, keepdims=True))).astype(bf16)
            probs[2 * pair + h] = prob
            parts.append(dot(value_t[h * HEAD_DIM : (h + 1) * HEAD_DIM], prob, 1, 0))
        context[:, cols] = jnp.concatenate(parts, 0).T.astype(bf16)


def attend(qkv, seg):
    rows, cols = qkv.shape
    half = cols // 2
    quarter = half // 3
    heads = quarter // HEAD_DIM
    return pl.pallas_call(
        attend_kernel,
        grid=(2,),
        out_shape=[jax.ShapeDtypeStruct((rows, 2 * quarter), bf16), jax.ShapeDtypeStruct((2 * heads, rows, rows), bf16)],
        in_specs=[
            pl.BlockSpec((rows, half), lambda i: (0, i)),
            pl.BlockSpec((rows, 1), lambda i: (0, 0)),
            pl.BlockSpec((1, rows), lambda i: (0, 0)),
        ],
        out_specs=[pl.BlockSpec((rows, quarter), lambda i: (0, i)), pl.BlockSpec((heads, rows, rows), lambda i: (i, 0, 0))],
        scratch_shapes=[pltpu.VMEM((rows, rows), f32)],
        compiler_params=pltpu.CompilerParams(vmem_limit_bytes=48 << 20),
        cost_estimate=pl.CostEstimate(flops=12_000_000_000, bytes_accessed=8 << 20, transcendentals=2 << 20),
        name="attend",
    )(qkv, seg.reshape(rows, 1), seg.reshape(1, rows))


def attend_back_kernel(qkv, probs, upstream, grads, sums):
    quarter = qkv.shape[1] // 3
    low = lax.broadcasted_iota(jnp.int32, (1, LANES), 1) < HEAD_DIM
    for pair in range(quarter // LANES):
        cols = [slice(n * quarter + pair * LANES, n * quarter + pair * LANES + LANES) for n in range(3)]
        query, key, value = (qkv[:, c] for c in cols)
        key_t = key.T
        above = upstream[:, cols[0]]
        grad_q, grad_k, grad_v = [], [], []
        for h in range(2):
            mine = jnp.where(low if h == 0 else ~low, above, jnp.zeros_like(above))
            grad_p = dot(value, mine, 1, 1)
            prob_low = probs[2 * pair + h]
            prob = prob_low.astype(f32)
            weighted = prob * grad_p
            inner = jnp.sum(weighted, axis=0, keepdims=True)
            grad_s = (weighted - prob * inner).astype(bf16)
            grad_k.append(dot(grad_s, query, 1, 0))
            grad_v.append(dot(prob_low, above, 1, 0))
            grad_q.append(dot(key_t[h * HEAD_DIM : (h + 1) * HEAD_DIM], grad_s, 1, 0))
        out_q = (jnp.concatenate(grad_q, 0) * 0.125).T.astype(bf16)
        out_v = jnp.where(low, grad_v[0], grad_v[1]).astype(bf16)
        grads[:, cols[0]] = out_q
        grads[:, cols[1]] = (jnp.where(low, grad_k[0], grad_k[1]) * 0.125).astype(bf16)
        grads[:, cols[2]] = out_v
        for n, out in ((0, out_q), (1, out_v)):
            total = jnp.sum(out.astype(f32), axis=0, keepdims=True)
            sums[0, n, :, cols[0]] = jnp.broadcast_to(total, (8, LANES))


def attend_back(qkv, probs, upstream):
    rows, cols = qkv.shape
    half = cols // 2
    quarter = half // 3
    heads = quarter // HEAD_DIM
    return pl.pallas_call(
        attend_back_kernel,
        grid=(2,),
        out_shape=[jax.ShapeDtypeStruct((rows, cols), bf16), jax.ShapeDtypeStruct((2, 2, 8, quarter), f32)],
        in_specs=[
            pl.BlockSpec((rows, half), lambda i: (0, i)),
            pl.BlockSpec((heads, rows, rows), lambda i: (i, 0, 0)),
            pl.BlockSpec((rows, quarter), lambda i: (0, i)),
        ],
        out_specs=[pl.BlockSpec((rows, half), lambda i: (0, i)), pl.BlockSpec((1, 2, 8, quarter), lambda i: (i, 0, 0, 0))],
        compiler_params=pltpu.CompilerParams(vmem_limit_bytes=48 << 20),
        cost_estimate=pl.CostEstimate(flops=20_000_000_000, bytes_accessed=8 << 20, transcendentals=0),
        name="attend_back",
    )(qkv, probs, upstream)


def scatter_sum(grad, dp_count):
    rows, _, cols = grad.shape
    if dp_count != 8:
        t = lax.axis_index("tp")
        mine = add(grad[:, 0], swap(grad[:, 1], "tp"))
        return lax.psum_scatter(mine, "dp", scatter_dimension=0, tiled=True).astype(f32)
    d = lax.axis_index("dp")
    x, z = d % 2, d // 2
    blocks = grad.reshape(2, 2, 2, rows // 8, 2, cols)
    first, second = blocks[0], blocks[1]
    got = swap(first[:, :, :, 1], "tp")
    got_b = swap_x(take(second, 1 - x, 1))
    first = add(first[:, :, :, 0], got)
    second = add(take(second, x, 1), got_b)
    got = swap_x(take(first, 1 - x, 1))
    got_b = swap(second[:, :, 1], "tp")
    first = add(take(first, x, 1), got)
    second = add(second[:, :, 0], got_b)
    line = jnp.concatenate([first, second], axis=0)
    total = take(line, z).astype(f32)
    for step in range(1, 4):
        total = total + shift_z(take(line, (z + step) % 4), step).astype(f32)
    return total


def body(dp_count, tokens, segments, query_weight, key_weight, value_weight, out_weight, up_weight, down_weight, query_bias, value_bias, out_bias, up_bias, down_bias, attn_gain, attn_shift, mlp_gain, mlp_shift, cotangent):
    c = lax.axis_index("ctx")
    t = lax.axis_index("tp")
    d = lax.axis_index("dp")
    place = jnp.stack([d // 2, d % 2]).astype(jnp.int32)
    half, width = tokens.shape[1], tokens.shape[2]
    rows = 2 * half
    inner = 2 * query_bias.shape[0]
    ff = 2 * up_bias.shape[0]
    piece_rows = query_weight.shape[0]

    one = jnp.stack([query_weight, key_weight, value_weight, out_weight.T], 1)
    one = one.reshape(piece_rows, 4, 2, -1).transpose(2, 0, 1, 3).reshape(2, piece_rows, -1)
    up = up_weight.reshape(piece_rows, 2, -1).transpose(1, 0, 2)
    down = down_weight.T.reshape(piece_rows, 2, -1).transpose(1, 0, 2)
    packed = jnp.stack([one, up, down], 1).astype(bf16)
    pieces = order(c, take(packed, c), swap(take(packed, 1 - c), "ctx"), 1)
    unit = pieces.shape[2]
    quarter = unit // 4
    whole = ((0, unit),)
    qkv_mine, out_mine = gather_weights(pieces[0], ((0, 3 * quarter), (3 * quarter, quarter)), place, dp_count)
    w_qkv = (qkv_mine, swap(qkv_mine, "ctx"))
    w_out = (out_mine, swap(out_mine, "ctx"))
    (up_mine,) = gather_weights(pieces[1], whole, place, dp_count)
    w_up = (up_mine, swap(up_mine, "ctx"))
    (down_mine,) = gather_weights(pieces[2], whole, place, dp_count)
    w_down = (down_mine, swap(down_mine, "ctx"))

    biases = jnp.concatenate([query_bias, value_bias, up_bias])
    biases = jnp.stack([biases, swap(biases, "tp")])
    hin = inner // 2

    def near(values):
        values = values.reshape(2, 2, -1).transpose(1, 0, 2)
        return jnp.where(c == 0, values, values[::-1])

    bias_q, bias_v, bias_up = near(biases[:, :hin]), near(biases[:, hin : 2 * hin]), near(biases[:, 2 * hin :])
    bias_qkv = jnp.stack([bias_q, jnp.zeros_like(bias_q), bias_v], 2).reshape(2, -1)
    bias_up = bias_up.reshape(2, -1)

    seq = 2 * t + c
    other_seq = 2 * t + 1 - c
    pair_mine = jnp.stack([take(tokens, seq), take(cotangent, seq), take(tokens, other_seq)])
    pair_send = jnp.stack([take(tokens, other_seq), take(cotangent, other_seq), take(tokens, seq)])
    got = swap(pair_send, "ctx")
    flat = jnp.concatenate([pair_mine[0], got[0]], 0)
    flat_far = jnp.concatenate([got[2], pair_mine[2]], 0)
    grad_output = jnp.concatenate([pair_mine[1], got[1]], 0).astype(f32)
    seg = take(segments, seq)
    seg = jnp.where(c == 0, seg, jnp.roll(seg, half))

    qkv = [(dot(flat, w_qkv[r], 1, 0) + bias_qkv[r]).astype(bf16) for r in range(2)]
    attended = [attend(qkv[r], seg) for r in range(2)]
    context = [a[0] for a in attended]
    probs = [a[1] for a in attended]
    resid_one = flat.astype(f32) + dot(context[0], w_out[0], 1, 1) + dot(context[1], w_out[1], 1, 1) + out_bias
    normed_one, unit_one, inverse_one = norm_forward(resid_one, attn_gain, attn_shift)
    normed_low = normed_one.astype(bf16)
    hidden, slope = [], []
    for r in range(2):
        pre = dot(normed_low, w_up[r], 1, 0) + bias_up[r]
        erf_part = lax.erf(pre * root_half)
        hidden.append((0.5 * pre * (1.0 + erf_part)).astype(bf16))
        slope.append((0.5 * (1.0 + erf_part) + pre * jnp.exp(-0.5 * pre * pre) * inv_root_two_pi).astype(bf16))
    mixed = dot(hidden[0], w_down[0], 1, 1) + dot(hidden[1], w_down[1], 1, 1)
    resid_two = normed_one + mixed + down_bias
    output, unit_two, inverse_two = norm_forward(resid_two, mlp_gain, mlp_shift)
    grad_two, mlp_gain_term, mlp_shift_term = norm_backward(grad_output, unit_two, inverse_two, mlp_gain)
    grad_mixed = grad_two.astype(bf16)
    down_bias_term = jnp.sum(grad_two, axis=0)
    grad_pre = [(dot(grad_mixed, w_down[r], 1, 0) * slope[r].astype(f32)).astype(bf16) for r in range(2)]
    up_bias_term = jnp.stack([jnp.sum(g.astype(f32), axis=0) for g in grad_pre])

    def far(values):
        return jnp.concatenate([values, swap(values, "ctx")], 0)

    def mine_and_far(pair):
        return jnp.concatenate([pair[0], swap(pair[1], "ctx")], 0)

    def grads(left, right):
        return dot(left, right, 0, 0).astype(bf16)

    down_grad = grads(far(grad_mixed), mine_and_far(hidden)).reshape(width, 2, -1)
    up_grad = grads(far(normed_low), mine_and_far(grad_pre)).reshape(width, 2, -1)
    down_total = scatter_sum(down_grad, dp_count)
    up_total = scatter_sum(up_grad, dp_count)

    grad_normed = grad_two + dot(grad_pre[0], w_up[0], 1, 1) + dot(grad_pre[1], w_up[1], 1, 1)
    grad_one, attn_gain_term, attn_shift_term = norm_backward(grad_normed, unit_one, inverse_one, attn_gain)
    grad_attended = grad_one.astype(bf16)
    out_bias_term = jnp.sum(grad_one, axis=0)
    grad_attended, down_grad, up_grad = lax.optimization_barrier((grad_attended, down_grad, up_grad))
    grad_context = [dot(grad_attended, w_out[r], 1, 0).astype(bf16) for r in range(2)]
    back = [attend_back(qkv[r], probs[r], grad_context[r]) for r in range(2)]
    grad_qkv = [b[0] for b in back]
    sums = jnp.stack([b[1] for b in back])[:, :, :, 0]
    sent_back = dot(grad_qkv[0], w_qkv[0], 1, 1) + dot(grad_qkv[1], w_qkv[1], 1, 1)
    input_grad = (grad_one + sent_back).astype(bf16)

    qkv_grad = grads(jnp.concatenate([flat, flat_far], 0), mine_and_far(grad_qkv)).reshape(width, 2, -1)
    out_grad = grads(far(grad_attended), mine_and_far(context)).reshape(width, 2, -1)
    one_total = scatter_sum(jnp.concatenate([qkv_grad, out_grad], 2), dp_count)

    def settle(values):
        values = jnp.where(c == 0, values, values[::-1])
        values = jnp.where(t == 0, values, values[:, ::-1])
        return values.transpose(1, 0, 2).reshape(-1)

    small = jnp.concatenate(
        [settle(sums[:, :, 0]), settle(sums[:, :, 1]), settle(up_bias_term.reshape(2, 2, -1)), out_bias_term, down_bias_term, attn_gain_term, attn_shift_term, mlp_gain_term, mlp_shift_term]
    )
    small = lax.all_gather(small.reshape(-1, 128), ("dp", "ctx", "tp"), axis=0, tiled=False)
    small = jnp.sum(small, axis=0).reshape(-1)

    def cut_tp(start, size):
        return lax.dynamic_slice_in_dim(small, start + t * (size // 2), size // 2)

    at = 2 * inner + ff
    vectors = [lax.slice_in_dim(small, at + i * width, at + (i + 1) * width) for i in range(6)]

    def spread(values):
        got = swap(values[half:], "ctx")
        pair = order(c, values[None, :half], got[None], 0)
        return order(t, pair, swap(pair, "tp"), 0)

    totals = jnp.stack([one_total, up_total, down_total])
    totals = totals.reshape(3, 2, piece_rows, unit)
    shards = order(c, take(totals, c, 1)[None], swap(take(totals, 1 - c, 1), "ctx")[None], 0)
    one_shard = shards[:, 0].reshape(2, piece_rows, 4, -1).transpose(2, 1, 0, 3).reshape(4, piece_rows, -1)
    up_shard = shards[:, 1].transpose(1, 0, 2).reshape(piece_rows, -1)
    down_shard = shards[:, 2].transpose(1, 0, 2).reshape(piece_rows, -1).T
    return (
        spread(output.astype(bf16)),
        spread(input_grad),
        one_shard[0],
        one_shard[1],
        one_shard[2],
        one_shard[3].T,
        up_shard,
        down_shard,
        cut_tp(0, inner),
        cut_tp(inner, inner),
        vectors[0],
        cut_tp(2 * inner, ff),
        *vectors[1:],
    )


def solution(mesh):
    weight_in, weight_out = P(("dp", "ctx"), "tp"), P("tp", ("dp", "ctx"))
    rows = P("dp", "ctx", None)
    weights = (weight_in, weight_in, weight_in, weight_out, weight_in, weight_out)
    vectors = (P("tp"), P("tp"), P(), P("tp"), P(), P(), P(), P(), P())
    dp_count = mesh.shape["dp"]

    def run(*args):
        return body(dp_count, *args)

    return jax.shard_map(
        run,
        mesh=mesh,
        in_specs=(rows, P("dp", None), *weights, *vectors, rows),
        out_specs=(rows, rows, *weights, *vectors),
        check_vma=False,
    )
```

```python
import functools

import jax
import jax.numpy as jnp
from jax import lax
from jax.experimental import pallas as pl
from jax.experimental.pallas import tpu as pltpu
from jax.sharding import PartitionSpec as P

HEAD_DIM = 64
LANES = 2 * HEAD_DIM

epsilon = 1e-12
root_half = 0.7071067811865476
inv_root_two_pi = 0.3989422804014327
bf16 = jnp.bfloat16
f32 = jnp.float32


def dot(left, right, left_dim, right_dim):
    return lax.dot_general(left, right, (((left_dim,), (right_dim,)), ((), ())), preferred_element_type=f32)


def norm_forward(values, gain, shift):
    centre = values - jnp.mean(values, axis=-1, keepdims=True)
    inverse = lax.rsqrt(jnp.mean(centre * centre, axis=-1, keepdims=True) + epsilon)
    normed = centre * inverse
    return (normed * gain + shift, normed, inverse)


def norm_backward(upstream, normed, inverse, gain):
    scaled = upstream * gain
    inner = scaled - jnp.mean(scaled, axis=-1, keepdims=True)
    inner = inner - normed * jnp.mean(scaled * normed, axis=-1, keepdims=True)
    return (inner * inverse, jnp.sum(upstream * normed, axis=0), jnp.sum(upstream, axis=0))


def swap(values, axis):
    return lax.ppermute(values, axis, [(0, 1), (1, 0)])


def swap_x(values):
    return lax.ppermute(values, "dp", [(i, i ^ 1) for i in range(8)])


def shift_z(values, step):
    return lax.ppermute(values, "dp", [(i, (i + 2 * step) % 8) for i in range(8)])


def take(values, index, axis=0):
    return lax.dynamic_index_in_dim(values, index, axis, keepdims=False)


def add(left, right):
    return (left.astype(f32) + right.astype(f32)).astype(bf16)


def order(index, mine, other, axis):
    return jnp.where(index == 0, jnp.concatenate([mine, other], axis), jnp.concatenate([other, mine], axis))


def assemble_kernel(cuts, place, one, one_y, two, two_x, *rest):
    outs, sems = rest[: len(cuts)], rest[len(cuts)]
    z, x = place[0], place[1]
    rows = one.shape[2]
    copies = []
    for k in range(4):
        for far_x in range(2):
            block = lax.rem(z + 4 - k, 4) * 2 + lax.rem(x + far_x, 2)
            at = pl.ds(pl.multiple_of(block * rows, rows), rows)
            for far_t in range(2):
                if k < 2:
                    source = (one_y if far_t else one).at[far_x, k]
                else:
                    source = (two_x if far_x else two).at[far_t, k - 2]
                for n, (start, size) in enumerate(cuts):
                    copies.append(
                        pltpu.make_async_copy(
                            source.at[:, start : start + size],
                            outs[n].at[at, far_t * size : far_t * size + size],
                            sems.at[len(copies)],
                        )
                    )
                    copies[-1].start()
    for copy in copies:
        copy.wait()


def gather_weights(piece, cuts, place, dp_count):
    rows, cols = piece.shape
    total = dp_count * rows
    if dp_count != 8:
        t = lax.axis_index("tp")
        both = lax.all_gather(piece, ("tp", "dp"), axis=0, tiled=True).reshape(2, total, cols)
        first, second = take(both, t), take(both, 1 - t)
        return [
            jnp.concatenate([first[:, s : s + n], second[:, s : s + n]], 1) for s, n in cuts
        ]
    line = [piece] + [shift_z(piece, k) for k in range(1, 4)]
    one, two = jnp.stack(line[:2]), jnp.stack(line[2:])
    one_x, two_y = swap_x(one), swap(two, "tp")
    one, two = jnp.stack([one, one_x]), jnp.stack([two, two_y])
    one_y, two_x = swap(one, "tp"), swap_x(two)
    anyspace = pl.BlockSpec(memory_space=pl.ANY)


    return pl.pallas_call(
        functools.partial(assemble_kernel, cuts),
        out_shape=[jax.ShapeDtypeStruct((total, 2 * n), bf16) for _, n in cuts],
        in_specs=[pl.BlockSpec(memory_space=pltpu.SMEM)] + [anyspace] * 4,
        out_specs=[pl.BlockSpec(memory_space=pltpu.VMEM)] * len(cuts),
        scratch_shapes=[pltpu.SemaphoreType.DMA((16 * len(cuts),))],
        compiler_params=pltpu.CompilerParams(vmem_limit_bytes=24 << 20),
        name="assemble",
    )(place, one, one_y, two, two_x)


def attend_kernel(qkv, seg_keys, seg_queries, context, probs, bias):
    quarter = qkv.shape[1] // 3

    @pl.when(pl.program_id(0) == 0)
    def _():
        bias[...] = jnp.where(seg_keys[...] == seg_queries[...], 0.0, -1000000000.0)

    low = lax.broadcasted_iota(jnp.int32, (1, LANES), 1) < HEAD_DIM
    for pair in range(quarter // LANES):
        cols = slice(pair * LANES, pair * LANES + LANES)
        query = qkv[:, cols] * 0.125
        key = qkv[:, quarter + pair * LANES : quarter + pair * LANES + LANES]
        value_t = qkv[:, 2 * quarter + pair * LANES : 2 * quarter + pair * LANES + LANES].T
        parts = []
        for h in range(2):
            mine = jnp.where(low if h == 0 else ~low, query, jnp.zeros_like(query))
            scores = dot(key, mine, 1, 1) + bias[...]
            raised = jnp.exp(scores - jnp.max(scores, axis=0, keepdims=True))
            prob = (raised * (1.0 / jnp.sum(raised, axis=0, keepdims=True))).astype(bf16)
            probs[2 * pair + h] = prob
            parts.append(dot(value_t[h * HEAD_DIM : (h + 1) * HEAD_DIM], prob, 1, 0))
        context[:, cols] = jnp.concatenate(parts, 0).T.astype(bf16)


def attend(qkv, seg):
    rows, cols = qkv.shape
    half = cols // 2
    quarter = half // 3
    heads = quarter // HEAD_DIM
    return pl.pallas_call(
        attend_kernel,
        grid=(2,),
        out_shape=[jax.ShapeDtypeStruct((rows, 2 * quarter), bf16), jax.ShapeDtypeStruct((2 * heads, rows, rows), bf16)],
        in_specs=[
            pl.BlockSpec((rows, half), lambda i: (0, i)),
            pl.BlockSpec((rows, 1), lambda i: (0, 0)),
            pl.BlockSpec((1, rows), lambda i: (0, 0)),
        ],
        out_specs=[pl.BlockSpec((rows, quarter), lambda i: (0, i)), pl.BlockSpec((heads, rows, rows), lambda i: (i, 0, 0))],
        scratch_shapes=[pltpu.VMEM((rows, rows), f32)],
        compiler_params=pltpu.CompilerParams(vmem_limit_bytes=48 << 20),
        cost_estimate=pl.CostEstimate(flops=12_000_000_000, bytes_accessed=8 << 20, transcendentals=2 << 20),
        name="attend",
    )(qkv, seg.reshape(rows, 1), seg.reshape(1, rows))


def attend_back_kernel(qkv, probs, upstream, *rest):
    grads, sums = rest[-2:]
    quarter = qkv.shape[1] // 3
    low = lax.broadcasted_iota(jnp.int32, (1, LANES), 1) < HEAD_DIM
    for pair in range(quarter // LANES):
        cols = [slice(n * quarter + pair * LANES, n * quarter + pair * LANES + LANES) for n in range(3)]
        query, key, value = (qkv[:, c] for c in cols)
        key_t = key.T
        above = upstream[:, cols[0]]
        grad_q, grad_k, grad_v = [], [], []
        for h in range(2):
            mine = jnp.where(low if h == 0 else ~low, above, jnp.zeros_like(above))
            grad_p = dot(value, mine, 1, 1)
            prob_low = probs[2 * pair + h]
            prob = prob_low.astype(f32)
            weighted = prob * grad_p
            inner = jnp.sum(weighted, axis=0, keepdims=True)
            grad_s = (weighted - prob * inner).astype(bf16)
            grad_k.append(dot(grad_s, query, 1, 0))
            grad_v.append(dot(prob_low, above, 1, 0))
            grad_q.append(dot(key_t[h * HEAD_DIM : (h + 1) * HEAD_DIM], grad_s, 1, 0))
        out_q = (jnp.concatenate(grad_q, 0) * 0.125).T.astype(bf16)
        out_v = jnp.where(low, grad_v[0], grad_v[1]).astype(bf16)
        grads[:, cols[0]] = out_q
        grads[:, cols[1]] = (jnp.where(low, grad_k[0], grad_k[1]) * 0.125).astype(bf16)
        grads[:, cols[2]] = out_v
        for n, out in ((0, out_q), (1, out_v)):
            total = jnp.sum(out.astype(f32), axis=0, keepdims=True)
            sums[0, n, :, cols[0]] = jnp.broadcast_to(total, (8, LANES))


def attend_back(qkv, probs, upstream, after):
    rows, cols = qkv.shape
    half = cols // 2
    quarter = half // 3
    heads = quarter // HEAD_DIM
    return pl.pallas_call(
        attend_back_kernel,
        grid=(2,),
        out_shape=[jax.ShapeDtypeStruct((rows, cols), bf16), jax.ShapeDtypeStruct((2, 2, 8, quarter), f32)],
        in_specs=[
            pl.BlockSpec((rows, half), lambda i: (0, i)),
            pl.BlockSpec((heads, rows, rows), lambda i: (i, 0, 0)),
            pl.BlockSpec((rows, quarter), lambda i: (0, i)),
        ]
        + [pl.BlockSpec(memory_space=pl.ANY)] * len(after),
        out_specs=[pl.BlockSpec((rows, half), lambda i: (0, i)), pl.BlockSpec((1, 2, 8, quarter), lambda i: (i, 0, 0, 0))],
        compiler_params=pltpu.CompilerParams(vmem_limit_bytes=48 << 20),
        cost_estimate=pl.CostEstimate(flops=20_000_000_000, bytes_accessed=8 << 20, transcendentals=0),
        name="attend_back",
    )(qkv, probs, upstream, *after)


def grad_kernel(lefts, place, *refs):
    sources = refs[: 2 * lefts]
    rights = refs[2 * lefts : 4 * lefts]
    outs = refs[-4 - lefts : -lefts]
    turned = refs[-lefts:]
    i = pl.program_id(0)
    x = place[1]
    rows, width = sources[0].shape
    piece = width // 8

    @pl.when(i == 0)
    def _():
        for n in range(lefts):
            for at in range(8):
                high, far_x, low = at // 4, (at // 2) % 2, at % 2
                block = (2 * high + low) * 2 + lax.rem(x + far_x, 2)
                cols = pl.ds(pl.multiple_of(block * piece, piece), piece)
                for far in range(2):
                    turned[n][at * piece : (at + 1) * piece, far * rows : (far + 1) * rows] = sources[2 * n + far][:, cols].T

    def work(n):
        right = jnp.concatenate([rights[2 * n][...], rights[2 * n + 1][...]], 0)
        out = dot(turned[n][...], right, 1, 0).astype(bf16)
        out = out.reshape(8, piece, out.shape[1])

        @pl.when(i < 4)
        def _():
            outs[0][...] = out[:4]

        @pl.when(i >= 4)
        def _():
            outs[1][...] = out[:4]

        outs[2][0] = out[4:6]
        outs[3][0] = out[6:]

    if lefts == 1:
        work(0)
    else:
        last = lax.rem(i, 4) == 3
        pl.when(jnp.logical_not(last))(lambda: work(0))
        pl.when(last)(lambda: work(1))


def weight_grad(place, pairs):
    rows, width = pairs[0][0].shape
    piece = width // 8
    whole = pl.BlockSpec((rows, width), lambda i: (0, 0))
    if len(pairs) == 1:
        maps = [lambda i: (0, i)]
    else:
        maps = [lambda i: (0, (i // 4) * 3 + jnp.minimum(i % 4, 2)), lambda i: (0, i // 4)]
    right_specs = [pl.BlockSpec((rows, 256), m) for m in maps for _ in range(2)]
    lefts = [v for p in pairs for v in p[:2]]
    rights = [v for p in pairs for v in p[2:]]
    out_specs = [
        pl.BlockSpec((4, piece, 256), lambda i: (0, 0, jnp.minimum(i, 3))),
        pl.BlockSpec((4, piece, 256), lambda i: (0, 0, jnp.maximum(i, 4) - 4)),
        pl.BlockSpec((1, 2, piece, 256), lambda i: (i // 4, 0, 0, i % 4)),
        pl.BlockSpec((1, 2, piece, 256), lambda i: (i // 4, 0, 0, i % 4)),
    ]
    return pl.pallas_call(
        functools.partial(grad_kernel, len(pairs)),
        grid=(8,),
        out_shape=[jax.ShapeDtypeStruct((4, piece, 1024), bf16)] * 2 + [jax.ShapeDtypeStruct((2, 2, piece, 1024), bf16)] * 2,
        in_specs=[pl.BlockSpec(memory_space=pltpu.SMEM)] + [whole] * len(lefts) + right_specs,
        out_specs=out_specs,
        scratch_shapes=[pltpu.VMEM((width, 2 * rows), bf16)] * len(pairs),
        compiler_params=pltpu.CompilerParams(vmem_limit_bytes=40 << 20),
        cost_estimate=pl.CostEstimate(flops=4 << 30, bytes_accessed=12 << 20, transcendentals=0),
        name="weight_grad",
    )(place, *lefts, *rights)


def sum_one_kernel(one, got_one, two, got_two, keep_one, send_one, keep_two, send_two):
    for mine, got, keep, send in ((one, got_one, keep_one, send_one), (two, got_two, keep_two, send_two)):
        keep[...] = add(mine[0], got[0])
        send[...] = add(mine[1], got[1])


def sum_one(one, got_one, two, got_two):
    _, piece, cols = one.shape
    four = (2, 2, piece, cols)
    block = pl.BlockSpec((2, 2, piece, 256), lambda i: (0, 0, 0, i))
    return pl.pallas_call(
        sum_one_kernel,
        grid=(cols // 256,),
        out_shape=[jax.ShapeDtypeStruct(four[1:], bf16)] * 4,
        in_specs=[block] * 4,
        out_specs=[pl.BlockSpec((2, piece, 256), lambda i: (0, 0, i))] * 4,
        compiler_params=pltpu.CompilerParams(vmem_limit_bytes=24 << 20),
        cost_estimate=pl.CostEstimate(flops=1 << 20, bytes_accessed=6 << 20, transcendentals=0),
        name="sum_one",
    )(one.reshape(four), got_one.reshape(four), two, got_two)


def sum_two_kernel(place, one, got_one, two, got_two, own, *rest):
    sends, line = rest[:3], rest[3]
    line[:2] = add(one[...], got_one[...])
    line[2:] = add(two[...], got_two[...])
    own[...] = line[place[0]]
    for k in range(1, 4):
        sends[k - 1][...] = line[lax.rem(place[0] + k, 4)]


def sum_two(place, one, got_one, two, got_two):
    _, piece, cols = one.shape
    block = pl.BlockSpec((2, piece, 256), lambda i: (0, 0, i))
    return pl.pallas_call(
        sum_two_kernel,
        grid=(cols // 256,),
        out_shape=[jax.ShapeDtypeStruct((piece, cols), bf16)] * 4,
        in_specs=[pl.BlockSpec(memory_space=pltpu.SMEM)] + [block] * 4,
        out_specs=[pl.BlockSpec((piece, 256), lambda i: (0, i))] * 4,
        scratch_shapes=[pltpu.VMEM((4, piece, 256), bf16)],
        compiler_params=pltpu.CompilerParams(vmem_limit_bytes=24 << 20),
        cost_estimate=pl.CostEstimate(flops=1 << 20, bytes_accessed=3 << 20, transcendentals=0),
        name="sum_two",
    )(place, one, got_one, two, got_two)


def first_sends(place, pairs, dp_count):
    if dp_count != 8:
        grads = []
        for left, left_far, right, right_far in pairs:
            both = dot(jnp.concatenate([left, left_far], 0), jnp.concatenate([right, right_far], 0), 0, 0)
            grads.append(both.astype(bf16).reshape(both.shape[0], 2, -1))
        return (jnp.concatenate(grads, 2),)
    keep_one, send_one, keep_two, send_two = weight_grad(place, pairs)
    return (keep_one, send_one, keep_two, send_two)


def scatter_sum(place, parts, dp_count):
    if dp_count != 8:
        (grad,) = parts
        mine = add(grad[:, 0], swap(grad[:, 1], "tp"))
        return lax.psum_scatter(mine, "dp", scatter_dimension=0, tiled=True).astype(f32)
    keep_one, send_one, keep_two, send_two = parts
    keep_one, send_one, keep_two, send_two = sum_one(keep_one, swap(send_one, "tp"), keep_two, swap_x(send_two))
    own, *sends = sum_two(place, keep_one, swap_x(send_one), keep_two, swap(send_two, "tp"))
    total = own.astype(f32)
    for k in range(1, 4):
        total = total + shift_z(sends[k - 1], k).astype(f32)
    return total


def body(dp_count, tokens, segments, query_weight, key_weight, value_weight, out_weight, up_weight, down_weight, query_bias, value_bias, out_bias, up_bias, down_bias, attn_gain, attn_shift, mlp_gain, mlp_shift, cotangent):
    c = lax.axis_index("ctx")
    t = lax.axis_index("tp")
    d = lax.axis_index("dp")
    place = jnp.stack([d // 2, d % 2]).astype(jnp.int32)
    half, width = tokens.shape[1], tokens.shape[2]
    rows = 2 * half
    inner = 2 * query_bias.shape[0]
    ff = 2 * up_bias.shape[0]
    piece_rows = query_weight.shape[0]

    one = jnp.stack([query_weight, key_weight, value_weight, out_weight.T], 1)
    one = one.reshape(piece_rows, 4, 2, -1).transpose(2, 0, 1, 3).reshape(2, piece_rows, -1)
    one = one.astype(bf16)
    piece = order(c, take(one, c), swap(take(one, 1 - c), "ctx"), 0)
    unit = piece.shape[1]
    quarter = unit // 4
    qkv_mine, out_mine = gather_weights(piece, ((0, 3 * quarter), (3 * quarter, quarter)), place, dp_count)
    w_qkv = (qkv_mine, swap(qkv_mine, "ctx"))
    w_out = (out_mine, swap(out_mine, "ctx"))
    rest = jnp.concatenate([up_weight.astype(bf16), down_weight.T.astype(bf16)], 1)
    rest = lax.all_gather(rest, ("tp", "dp", "ctx"), axis=0, tiled=True).reshape(2, width, 2, 2, unit)

    def columns(group, core):
        parts = [lax.dynamic_slice(rest, (tp, 0, group, core, 0), (1, width, 1, 1, unit)).reshape(width, unit) for tp in (t, 1 - t)]
        return jnp.concatenate(parts, 1)

    w_up = (columns(0, c), columns(0, 1 - c))
    w_down = (columns(1, c), columns(1, 1 - c))

    biases = jnp.concatenate([query_bias, value_bias, up_bias])
    biases = jnp.stack([biases, swap(biases, "tp")])
    hin = inner // 2

    def near(values):
        values = values.reshape(2, 2, -1).transpose(1, 0, 2)
        return jnp.where(c == 0, values, values[::-1])

    bias_q, bias_v, bias_up = near(biases[:, :hin]), near(biases[:, hin : 2 * hin]), near(biases[:, 2 * hin :])
    bias_qkv = jnp.stack([bias_q, jnp.zeros_like(bias_q), bias_v], 2).reshape(2, -1)
    bias_up = bias_up.reshape(2, -1)

    seq = 2 * t + c
    other_seq = 2 * t + 1 - c
    pair_mine = jnp.stack([take(tokens, seq), take(cotangent, seq), take(tokens, other_seq)])
    pair_send = jnp.stack([take(tokens, other_seq), take(cotangent, other_seq), take(tokens, seq)])
    got = swap(pair_send, "ctx")
    flat = jnp.concatenate([pair_mine[0], got[0]], 0)
    flat_far = jnp.concatenate([got[2], pair_mine[2]], 0)
    grad_output = jnp.concatenate([pair_mine[1], got[1]], 0).astype(f32)
    seg = take(segments, seq)
    seg = jnp.where(c == 0, seg, jnp.roll(seg, half))

    qkv = [(dot(flat, w_qkv[r], 1, 0) + bias_qkv[r]).astype(bf16) for r in range(2)]
    attended = [attend(qkv[r], seg) for r in range(2)]
    context = [a[0] for a in attended]
    probs = [a[1] for a in attended]
    resid_one = flat.astype(f32) + dot(context[0], w_out[0], 1, 1) + dot(context[1], w_out[1], 1, 1) + out_bias
    normed_one, unit_one, inverse_one = norm_forward(resid_one, attn_gain, attn_shift)
    normed_low = normed_one.astype(bf16)
    hidden, slope = [], []
    for r in range(2):
        pre = dot(normed_low, w_up[r], 1, 0) + bias_up[r]
        erf_part = lax.erf(pre * root_half)
        hidden.append((0.5 * pre * (1.0 + erf_part)).astype(bf16))
        slope.append((0.5 * (1.0 + erf_part) + pre * jnp.exp(-0.5 * pre * pre) * inv_root_two_pi).astype(bf16))
    mixed = dot(hidden[0], w_down[0], 1, 1) + dot(hidden[1], w_down[1], 1, 1)
    resid_two = normed_one + mixed + down_bias
    output, unit_two, inverse_two = norm_forward(resid_two, mlp_gain, mlp_shift)
    grad_two, mlp_gain_term, mlp_shift_term = norm_backward(grad_output, unit_two, inverse_two, mlp_gain)
    grad_mixed = grad_two.astype(bf16)
    down_bias_term = jnp.sum(grad_two, axis=0)
    grad_pre = [(dot(grad_mixed, w_down[r], 1, 0) * slope[r].astype(f32)).astype(bf16) for r in range(2)]
    up_bias_term = jnp.stack([jnp.sum(g.astype(f32), axis=0) for g in grad_pre])

    def far(values):
        return swap(values, "ctx")

    down_parts = first_sends(place, [(grad_mixed, far(grad_mixed), hidden[0], far(hidden[1]))], dp_count)
    up_parts = first_sends(place, [(normed_low, far(normed_low), grad_pre[0], far(grad_pre[1]))], dp_count)
    down_total = scatter_sum(place, down_parts, dp_count)
    up_total = scatter_sum(place, up_parts, dp_count)

    grad_normed = grad_two + dot(grad_pre[0], w_up[0], 1, 1) + dot(grad_pre[1], w_up[1], 1, 1)
    grad_one, attn_gain_term, attn_shift_term = norm_backward(grad_normed, unit_one, inverse_one, attn_gain)
    grad_attended = grad_one.astype(bf16)
    out_bias_term = jnp.sum(grad_one, axis=0)
    grad_context = [dot(grad_attended, w_out[r], 1, 0).astype(bf16) for r in range(2)]
    back = [attend_back(qkv[r], probs[r], grad_context[r], (down_parts[-1], up_parts[-1])) for r in range(2)]
    grad_qkv = [b[0] for b in back]
    sums = jnp.stack([b[1] for b in back])[:, :, :, 0]
    sent_back = dot(grad_qkv[0], w_qkv[0], 1, 1) + dot(grad_qkv[1], w_qkv[1], 1, 1)
    input_grad = (grad_one + sent_back).astype(bf16)

    one_parts = first_sends(
        place,
        [(flat, flat_far, grad_qkv[0], far(grad_qkv[1])), (grad_attended, far(grad_attended), context[0], far(context[1]))],
        dp_count,
    )
    one_total = scatter_sum(place, one_parts, dp_count)

    def settle(values):
        values = jnp.where(c == 0, values, values[::-1])
        values = jnp.where(t == 0, values, values[:, ::-1])
        return values.transpose(1, 0, 2).reshape(-1)

    small = jnp.concatenate(
        [settle(sums[:, :, 0]), settle(sums[:, :, 1]), settle(up_bias_term.reshape(2, 2, -1)), out_bias_term, down_bias_term, attn_gain_term, attn_shift_term, mlp_gain_term, mlp_shift_term]
    )
    small = lax.all_gather(small.reshape(-1, 128), ("dp", "ctx", "tp"), axis=0, tiled=False)
    small = jnp.sum(small, axis=0).reshape(-1)

    def cut_tp(start, size):
        return lax.dynamic_slice_in_dim(small, start + t * (size // 2), size // 2)

    at = 2 * inner + ff
    vectors = [lax.slice_in_dim(small, at + i * width, at + (i + 1) * width) for i in range(6)]

    def spread(values):
        got = swap(values[half:], "ctx")
        pair = order(c, values[None, :half], got[None], 0)
        return order(t, pair, swap(pair, "tp"), 0)

    totals = jnp.stack([one_total, up_total, down_total])
    totals = totals.reshape(3, 2, piece_rows, unit)
    shards = order(c, take(totals, c, 1)[None], swap(take(totals, 1 - c, 1), "ctx")[None], 0)
    one_shard = shards[:, 0].reshape(2, piece_rows, 4, -1).transpose(2, 1, 0, 3).reshape(4, piece_rows, -1)
    up_shard = shards[:, 1].transpose(1, 0, 2).reshape(piece_rows, -1)
    down_shard = shards[:, 2].transpose(1, 0, 2).reshape(piece_rows, -1).T
    return (
        spread(output.astype(bf16)),
        spread(input_grad),
        one_shard[0],
        one_shard[1],
        one_shard[2],
        one_shard[3].T,
        up_shard,
        down_shard,
        cut_tp(0, inner),
        cut_tp(inner, inner),
        vectors[0],
        cut_tp(2 * inner, ff),
        *vectors[1:],
    )


def solution(mesh):
    weight_in, weight_out = P(("dp", "ctx"), "tp"), P("tp", ("dp", "ctx"))
    rows = P("dp", "ctx", None)
    weights = (weight_in, weight_in, weight_in, weight_out, weight_in, weight_out)
    vectors = (P("tp"), P("tp"), P(), P("tp"), P(), P(), P(), P(), P())
    dp_count = mesh.shape["dp"]

    def run(*args):
        return body(dp_count, *args)

    return jax.shard_map(
        run,
        mesh=mesh,
        in_specs=(rows, P("dp", None), *weights, *vectors, rows),
        out_specs=(rows, rows, *weights, *vectors),
        check_vma=False,
    )
```

```python
import functools

import jax
import jax.numpy as jnp
from jax import lax
from jax.experimental import pallas as pl
from jax.experimental.pallas import tpu as pltpu
from jax.sharding import PartitionSpec as P

HEAD_DIM = 64
LANES = 2 * HEAD_DIM

epsilon = 1e-12
root_half = 0.7071067811865476
inv_root_two_pi = 0.3989422804014327
bf16 = jnp.bfloat16
f32 = jnp.float32


def dot(left, right, left_dim, right_dim):
    return lax.dot_general(left, right, (((left_dim,), (right_dim,)), ((), ())), preferred_element_type=f32)


def norm_forward(values, gain, shift):
    centre = values - jnp.mean(values, axis=-1, keepdims=True)
    inverse = lax.rsqrt(jnp.mean(centre * centre, axis=-1, keepdims=True) + epsilon)
    normed = centre * inverse
    return (normed * gain + shift, normed, inverse)


def swap(values, axis):
    return lax.ppermute(values, axis, [(0, 1), (1, 0)])


def swap_x(values):
    return lax.ppermute(values, "dp", [(i, i ^ 1) for i in range(8)])


def shift_z(values, step):
    return lax.ppermute(values, "dp", [(i, (i + 2 * step) % 8) for i in range(8)])


def take(values, index, axis=0):
    return lax.dynamic_index_in_dim(values, index, axis, keepdims=False)


def add(left, right):
    return (left.astype(f32) + right.astype(f32)).astype(bf16)


def order(index, mine, other, axis):
    return jnp.where(index == 0, jnp.concatenate([mine, other], axis), jnp.concatenate([other, mine], axis))


def assemble_kernel(cuts, place, one, one_y, two, two_x, *rest):
    outs, sems = rest[: len(cuts)], rest[len(cuts)]
    z, x = place[0], place[1]
    rows = one.shape[2]
    copies = []
    for k in range(4):
        for far_x in range(2):
            block = lax.rem(z + 4 - k, 4) * 2 + lax.rem(x + far_x, 2)
            at = pl.ds(pl.multiple_of(block * rows, rows), rows)
            for far_t in range(2):
                if k < 2:
                    source = (one_y if far_t else one).at[far_x, k]
                else:
                    source = (two_x if far_x else two).at[far_t, k - 2]
                for n, (start, size) in enumerate(cuts):
                    copies.append(
                        pltpu.make_async_copy(
                            source.at[:, start : start + size],
                            outs[n].at[at, far_t * size : far_t * size + size],
                            sems.at[len(copies)],
                        )
                    )
                    copies[-1].start()
    for copy in copies:
        copy.wait()


def gather_weights(piece, cuts, place, dp_count):
    rows, cols = piece.shape
    total = dp_count * rows
    if dp_count != 8:
        t = lax.axis_index("tp")
        both = lax.all_gather(piece, ("tp", "dp"), axis=0, tiled=True).reshape(2, total, cols)
        first, second = take(both, t), take(both, 1 - t)
        return [
            jnp.concatenate([first[:, s : s + n], second[:, s : s + n]], 1) for s, n in cuts
        ]
    line = [piece] + [shift_z(piece, k) for k in range(1, 4)]
    one, two = jnp.stack(line[:2]), jnp.stack(line[2:])
    one_x, two_y = swap_x(one), swap(two, "tp")
    one, two = jnp.stack([one, one_x]), jnp.stack([two, two_y])
    one_y, two_x = swap(one, "tp"), swap_x(two)
    anyspace = pl.BlockSpec(memory_space=pl.ANY)


    return pl.pallas_call(
        functools.partial(assemble_kernel, cuts),
        out_shape=[jax.ShapeDtypeStruct((total, 2 * n), bf16) for _, n in cuts],
        in_specs=[pl.BlockSpec(memory_space=pltpu.SMEM)] + [anyspace] * 4,
        out_specs=[pl.BlockSpec(memory_space=pltpu.VMEM)] * len(cuts),
        scratch_shapes=[pltpu.SemaphoreType.DMA((16 * len(cuts),))],
        compiler_params=pltpu.CompilerParams(vmem_limit_bytes=24 << 20),
        name="assemble",
    )(place, one, one_y, two, two_x)


def tie_kernel(*refs):
    pass


def tie(value, *after):
    anyspace = pl.BlockSpec(memory_space=pl.ANY)
    return pl.pallas_call(
        tie_kernel,
        out_shape=jax.ShapeDtypeStruct(value.shape, value.dtype),
        in_specs=[anyspace] * (1 + len(after)),
        out_specs=anyspace,
        input_output_aliases={0: 0},
        name="tie",
    )(value, *after)


def attend_kernel(qkv, seg_keys, seg_queries, context, probs, bias):
    quarter = qkv.shape[1] // 3

    @pl.when(pl.program_id(0) == 0)
    def _():
        bias[...] = jnp.where(seg_keys[...] == seg_queries[...], 0.0, -1000000000.0)

    low = lax.broadcasted_iota(jnp.int32, (1, LANES), 1) < HEAD_DIM
    for pair in range(quarter // LANES):
        cols = slice(pair * LANES, pair * LANES + LANES)
        query = qkv[:, cols] * 0.125
        key = qkv[:, quarter + pair * LANES : quarter + pair * LANES + LANES]
        value_t = qkv[:, 2 * quarter + pair * LANES : 2 * quarter + pair * LANES + LANES].T
        parts = []
        for h in range(2):
            mine = jnp.where(low if h == 0 else ~low, query, jnp.zeros_like(query))
            scores = dot(key, mine, 1, 1) + bias[...]
            raised = jnp.exp(scores - jnp.max(scores, axis=0, keepdims=True))
            prob = (raised * (1.0 / jnp.sum(raised, axis=0, keepdims=True))).astype(bf16)
            probs[2 * pair + h] = prob
            parts.append(dot(value_t[h * HEAD_DIM : (h + 1) * HEAD_DIM], prob, 1, 0))
        context[:, cols] = jnp.concatenate(parts, 0).T.astype(bf16)


def attend(qkv, seg):
    rows, cols = qkv.shape
    half = cols // 2
    quarter = half // 3
    heads = quarter // HEAD_DIM
    return pl.pallas_call(
        attend_kernel,
        grid=(2,),
        out_shape=[jax.ShapeDtypeStruct((rows, 2 * quarter), bf16), jax.ShapeDtypeStruct((2 * heads, rows, rows), bf16)],
        in_specs=[
            pl.BlockSpec((rows, half), lambda i: (0, i)),
            pl.BlockSpec((rows, 1), lambda i: (0, 0)),
            pl.BlockSpec((1, rows), lambda i: (0, 0)),
        ],
        out_specs=[pl.BlockSpec((rows, quarter), lambda i: (0, i)), pl.BlockSpec((heads, rows, rows), lambda i: (i, 0, 0))],
        scratch_shapes=[pltpu.VMEM((rows, rows), f32)],
        compiler_params=pltpu.CompilerParams(vmem_limit_bytes=48 << 20),
        cost_estimate=pl.CostEstimate(flops=1024, bytes_accessed=1024, transcendentals=0),
        name="attend",
    )(qkv, seg.reshape(rows, 1), seg.reshape(1, rows))


def attend_back_kernel(qkv, probs, upstream, *rest):
    grads, sums = rest[-2:]
    quarter = qkv.shape[1] // 3
    low = lax.broadcasted_iota(jnp.int32, (1, LANES), 1) < HEAD_DIM
    for pair in range(quarter // LANES):
        cols = [slice(n * quarter + pair * LANES, n * quarter + pair * LANES + LANES) for n in range(3)]
        query, key, value = (qkv[:, c] for c in cols)
        key_t = key.T
        above = upstream[:, cols[0]]
        grad_q, grad_k, grad_v = [], [], []
        for h in range(2):
            mine = jnp.where(low if h == 0 else ~low, above, jnp.zeros_like(above))
            grad_p = dot(value, mine, 1, 1)
            prob_low = probs[2 * pair + h]
            prob = prob_low.astype(f32)
            weighted = prob * grad_p
            inner = jnp.sum(weighted, axis=0, keepdims=True)
            grad_s = (weighted - prob * inner).astype(bf16)
            grad_k.append(dot(grad_s, query, 1, 0))
            grad_v.append(dot(prob_low, above, 1, 0))
            grad_q.append(dot(key_t[h * HEAD_DIM : (h + 1) * HEAD_DIM], grad_s, 1, 0))
        out_q = (jnp.concatenate(grad_q, 0) * 0.125).T.astype(bf16)
        out_v = jnp.where(low, grad_v[0], grad_v[1]).astype(bf16)
        grads[:, cols[0]] = out_q
        grads[:, cols[1]] = (jnp.where(low, grad_k[0], grad_k[1]) * 0.125).astype(bf16)
        grads[:, cols[2]] = out_v
        for n, out in ((0, out_q), (1, out_v)):
            total = jnp.sum(out.astype(f32), axis=0, keepdims=True)
            sums[0, n, :, cols[0]] = jnp.broadcast_to(total, (8, LANES))


def attend_back(qkv, probs, upstream, after):
    rows, cols = qkv.shape
    half = cols // 2
    quarter = half // 3
    heads = quarter // HEAD_DIM
    return pl.pallas_call(
        attend_back_kernel,
        grid=(2,),
        out_shape=[jax.ShapeDtypeStruct((rows, cols), bf16), jax.ShapeDtypeStruct((2, 2, 8, quarter), f32)],
        in_specs=[
            pl.BlockSpec((rows, half), lambda i: (0, i)),
            pl.BlockSpec((heads, rows, rows), lambda i: (i, 0, 0)),
            pl.BlockSpec((rows, quarter), lambda i: (0, i)),
        ]
        + [pl.BlockSpec(memory_space=pl.ANY)] * len(after),
        out_specs=[pl.BlockSpec((rows, half), lambda i: (0, i)), pl.BlockSpec((1, 2, 8, quarter), lambda i: (i, 0, 0, 0))],
        compiler_params=pltpu.CompilerParams(vmem_limit_bytes=48 << 20),
        cost_estimate=pl.CostEstimate(flops=1024, bytes_accessed=1024, transcendentals=0),
        name="attend_back",
    )(qkv, probs, upstream, *after)


CHUNK = 32


def cheap():
    return pl.CostEstimate(flops=1024, bytes_accessed=1024, transcendentals=0)


def clamp(i, low, count):
    return jnp.clip(i - low, 0, count - 1)


def put(near, far, i, steps, value):
    @pl.when(i < steps)
    def _():
        near[0] = value

    @pl.when(i >= steps)
    def _():
        far[0] = value


def halves_of(group, width, unit):
    core = lambda i, p: lax.rem(p[2] + i // 4, 2)
    return pl.BlockSpec((1, width, unit // 2), lambda i, p: (group, (i // 2) % 2, core(i, p) * 2 + i % 2))


def blocks_of(group, width, unit):
    return pl.BlockSpec((1, width, unit), lambda i, p: (group, lax.rem(p[3] + i % 2, 2), lax.rem(p[2] + i // 2, 2)))


def half_outs(rows, unit):
    return [pl.BlockSpec((1, rows, unit // 2), lambda i, p, n=n: (clamp(i, n, 4) // 2, 0, clamp(i, n, 4) % 2)) for n in (0, 4)]


def block_ins(rows, unit):
    return [pl.BlockSpec((1, rows, unit), lambda i, p, n=n: (clamp(i, n, 2), 0, 0)) for n in (0, 2)]


def fixed(*shape):
    return pl.BlockSpec(shape, lambda i, p: (0,) * len(shape))


def call(kernel, place, grid, ins, in_specs, outs, out_specs, scratch, name):
    return pl.pallas_call(
        kernel,
        grid_spec=pltpu.PrefetchScalarGridSpec(num_scalar_prefetch=1, grid=(grid,), in_specs=in_specs, out_specs=out_specs, scratch_shapes=scratch),
        out_shape=[jax.ShapeDtypeStruct(*o) for o in outs],
        compiler_params=pltpu.CompilerParams(vmem_limit_bytes=48 << 20),
        cost_estimate=cheap(),
        name=name,
    )(place, *ins)


def mean(values):
    return jnp.sum(values, axis=-1, keepdims=True) * (1.0 / values.shape[-1])


def fold(values):
    return jnp.sum(values.reshape(-1, 8, values.shape[-1]), axis=0)


def mlp_kernel(place, low, up_weight, down_weight, up_bias, normed, above, bias, gain, shift, near, far, out, grad, grad_low, pre_near, pre_far, sums, up_sums, units, slope, down, total):
    i = pl.program_id(0)
    rows, width = low.shape
    cols = up_weight.shape[2]
    tile = cols // 4

    def up(out_ref):
        for n in range(4):
            at = slice(n * tile, n * tile + tile)
            pre = dot(low[...], up_weight[0, :, at], 1, 0) + up_bias[0, :, at]
            half = 0.5 * (1.0 + lax.erf(pre * root_half))
            value = (pre * half).astype(bf16)
            out_ref[0, :, at] = value
            units[i, :, at] = value
            slope[i, :, at] = (half + pre * jnp.exp(-0.5 * pre * pre) * inv_root_two_pi).astype(bf16)

    pl.when(i < 2)(lambda: up(near))
    pl.when(jnp.logical_and(i >= 2, i < 4))(lambda: up(far))

    @pl.when(i == 4)
    def _():
        total[...] = normed[...] + bias[...]

    @pl.when(jnp.logical_and(i >= 4, i < 8))
    def _():
        down[i - 4] = down_weight[0]
        total[...] += dot(units[i - 4], down_weight[0], 1, 1)

    @pl.when(i == 7)
    def _():
        def step(k, carry):
            at = pl.ds(pl.multiple_of(k * CHUNK, CHUNK), CHUNK)
            centre = total[at] - mean(total[at])
            inverse = lax.rsqrt(mean(centre * centre) + epsilon)
            unit = centre * inverse
            out[at] = (unit * gain[...] + shift[...]).astype(bf16)
            upper = above[at].astype(f32)
            scaled = upper * gain[...]
            lower = inverse * (scaled - mean(scaled) - unit * mean(scaled * unit))
            grad[at] = lower
            grad_low[at] = lower.astype(bf16)
            return tuple(c + fold(v) for c, v in zip(carry, (upper * unit, upper, lower)))

        zero = jnp.zeros((8, width), f32)
        done = lax.fori_loop(0, rows // CHUNK, step, (zero,) * 3)
        for n in range(3):
            sums[n] = done[n]

    def pre(out_ref):
        for n in range(4):
            at = slice(n * tile, n * tile + tile)
            value = (dot(grad_low[...], down[i - 8, :, at], 1, 0) * slope[i - 8, :, at].astype(f32)).astype(bf16)
            out_ref[0, :, at] = value
            up_sums[0, :, at] = fold(value.astype(f32))

    pl.when(jnp.logical_and(i >= 8, i < 10))(lambda: pre(pre_near))
    pl.when(i >= 10)(lambda: pre(pre_far))


def mlp(place, low, weights, up_bias, normed, above, bias, gain, shift):
    rows, width = low.shape
    unit = weights.shape[2] // 2

    def still(*shape):
        return pl.BlockSpec(shape, lambda i, p: (0,) * len(shape), pipeline_mode=pl.Buffered(1))

    def block(group, first):
        def index(i, p):
            j = clamp(i, first, 4)
            return (group, lax.rem(p[3] + j % 2, 2), lax.rem(p[2] + j // 2, 2))

        return pl.BlockSpec((1, width, unit), index)

    def outs(first):
        return [pl.BlockSpec((1, rows, unit), lambda i, p, n=n: (clamp(i, n, 2), 0, 0)) for n in (first, first + 2)]

    def bias_index(i, p):
        j = clamp(i, 0, 4)
        return (lax.rem(p[3] + j % 2, 2) * 2 + lax.rem(p[2] + j // 2, 2), 0, 0)

    one, vector = still(rows, width), still(1, width)
    return pl.pallas_call(
        mlp_kernel,
        grid_spec=pltpu.PrefetchScalarGridSpec(
            num_scalar_prefetch=1,
            grid=(12,),
            in_specs=[one, block(0, 0), block(1, 4), pl.BlockSpec((1, 1, unit), bias_index), one, one, vector, vector, vector],
            out_specs=outs(0) + [one, one, one] + outs(8) + [still(3, 8, width), pl.BlockSpec((1, 8, unit), lambda i, p: (clamp(i, 8, 4), 0, 0))],
            scratch_shapes=[pltpu.VMEM((4, rows, unit), bf16)] * 2 + [pltpu.VMEM((4, width, unit), bf16), pltpu.VMEM((rows, width), f32)],
        ),
        out_shape=[jax.ShapeDtypeStruct(*o) for o in (
            [((2, rows, unit), bf16)] * 2
            + [((rows, width), bf16), ((rows, width), f32), ((rows, width), bf16)]
            + [((2, rows, unit), bf16)] * 2
            + [((3, 8, width), f32), ((4, 8, unit), f32)]
        )],
        compiler_params=pltpu.CompilerParams(vmem_limit_bytes=60 << 20),
        cost_estimate=cheap(),
        name="mlp",
    )(place, low, weights, weights, up_bias.reshape(4, 1, unit), normed, above, bias[None], gain[None], shift[None])


def mlp_back_kernel(place, near, far, weight, grad_two, unit_one, inverse, gain, out_near, out_far, grad, grad_low, near_context, far_context, sums, total):
    i = pl.program_id(0)

    @pl.when(i == 0)
    def _():
        total[...] = grad_two[...] + dot(near[0], weight[0], 1, 1)

    @pl.when(i == 1)
    def _():
        total[...] += dot(near[0], weight[0], 1, 1)

    @pl.when(i >= 2)
    def _():
        total[...] += dot(far[0], weight[0], 1, 1)

    @pl.when(i == 3)
    def _():
        def step(k, carry):
            at = pl.ds(pl.multiple_of(k * CHUNK, CHUNK), CHUNK)
            upper = total[at]
            unit = unit_one[at]
            scaled = upper * gain[...]
            down = inverse[at] * (scaled - mean(scaled) - unit * mean(scaled * unit))
            grad[at] = down
            grad_low[at] = down.astype(bf16)
            return tuple(c + fold(v) for c, v in zip(carry, (upper * unit, upper, down)))

        zero = jnp.zeros((8, grad.shape[1]), f32)
        done = lax.fori_loop(0, grad.shape[0] // CHUNK, step, (zero,) * 3)
        for n in range(3):
            sums[n] = done[n]
        near_context[...] = dot(grad_low[...], out_near[...], 1, 0).astype(bf16)
        far_context[...] = dot(grad_low[...], out_far[...], 1, 0).astype(bf16)


def mlp_back(place, near, far, weights, grad_two, unit_one, inverse, gain, out_near, out_far, after):
    rows, width = grad_two.shape
    unit = weights.shape[2] // 2
    part = out_near.shape[1]
    one = fixed(rows, width)

    def kernel(*refs):
        mlp_back_kernel(*refs[:10], *refs[10 + len(after) :])

    return call(
        kernel,
        place,
        4,
        (near, far, weights, grad_two, unit_one, inverse, gain[None], out_near, out_far, *after),
        block_ins(rows, unit) + [blocks_of(0, width, unit), one, one, fixed(rows, 1), fixed(1, width)] + [fixed(width, part)] * 2 + [pl.BlockSpec(memory_space=pl.ANY)] * len(after),
        [((rows, width), f32), ((rows, width), bf16)] + [((rows, part), bf16)] * 2 + [((3, 8, width), f32)],
        [one, one] + [fixed(rows, part)] * 2 + [fixed(3, 8, width)],
        [pltpu.VMEM((rows, width), f32)],
        "mlp_back",
    )


def over(axis, values):
    if axis == "t":
        return swap(values, "tp")
    if axis == "x":
        return swap_x(values)
    flip = 2 if axis == "l" else 4
    return lax.ppermute(values, "dp", [(i, i ^ flip) for i in range(8)])


def grad_kernel(kind, place, *refs):
    lefts = 2 if kind == "one" else 1
    sources = refs[: 2 * lefts]
    rights = refs[2 * lefts : 4 * lefts]
    outs = refs[4 * lefts : -lefts]
    turned = refs[-lefts:]
    i = pl.program_id(0)
    z, x = place[0], place[1]
    rows, width = sources[0].shape
    piece = width // 8

    @pl.when(i == 0)
    def _():
        for at in range(8):
            a, b, c = at // 4, (at // 2) % 2, at % 2
            far_x, low, high = (b, a, c) if kind == "one" else (a, b, c)
            block = (2 * lax.rem(z // 2 + high, 2) + lax.rem(z + low, 2)) * 2 + lax.rem(x + far_x, 2)
            cols = pl.ds(pl.multiple_of(block * piece, piece), piece)
            for n in range(lefts):
                for far in range(2):
                    turned[n][at * piece : (at + 1) * piece, far * rows : (far + 1) * rows] = sources[2 * n + far][:, cols].T

    def work(n):
        near, away = rights[2 * n], rights[2 * n + 1]
        pick = (lambda r: r[...]) if kind == "one" else (lambda r: r[0])
        out = dot(turned[n][...], jnp.concatenate([pick(near), pick(away)], 0), 1, 0).astype(bf16)
        if kind == "tp":
            out = out.reshape(2, 4 * piece, out.shape[1])
            pl.when(i < 4)(lambda: outs[0].__setitem__(..., out))
            pl.when(i >= 4)(lambda: outs[1].__setitem__(..., out))
        elif kind == "x":
            out = out.reshape(2, 2, 2, piece, out.shape[1])
            outs[0][:, :, 0] = out[0]
            outs[1][:, :, 0] = out[1]
        else:
            out = out.reshape(2, 2, 2 * piece, out.shape[1])
            pl.when(i < 4)(lambda: outs[0].__setitem__(..., out[0]))
            pl.when(i >= 4)(lambda: outs[1].__setitem__(..., out[0]))
            outs[2][0] = out[1, 0]
            outs[3][0] = out[1, 1]

    if lefts == 1:
        work(0)
    else:
        last = lax.rem(i, 4) == 3
        pl.when(jnp.logical_not(last))(lambda: work(0))
        pl.when(last)(lambda: work(1))


def weight_grad(place, pairs, kind):
    rows, width = pairs[0][0].shape
    piece = width // 8
    whole = pl.BlockSpec((rows, width), lambda i, p: (0, 0))
    first = lambda i: jnp.minimum(i, 3)
    second = lambda i: jnp.maximum(i, 4) - 4
    if kind == "one":
        maps = [lambda i, p: (0, (i // 4) * 3 + jnp.minimum(i % 4, 2)), lambda i, p: (0, i // 4)]
        right_specs = [pl.BlockSpec((rows, 256), m) for m in maps for _ in range(2)]
        shapes = [(2, 2 * piece, 1024)] * 4
        out_specs = [
            pl.BlockSpec((2, 2 * piece, 256), lambda i, p: (0, 0, first(i))),
            pl.BlockSpec((2, 2 * piece, 256), lambda i, p: (0, 0, second(i))),
        ] + [pl.BlockSpec((1, 2 * piece, 256), lambda i, p: (i // 4, 0, i % 4))] * 2
    else:
        right_specs = [pl.BlockSpec((1, rows, 256), lambda i, p: (i // 4, 0, i % 4))] * 2
        if kind == "tp":
            shapes = [(2, 4 * piece, 1024)] * 2
            out_specs = [
                pl.BlockSpec((2, 4 * piece, 256), lambda i, p: (0, 0, first(i))),
                pl.BlockSpec((2, 4 * piece, 256), lambda i, p: (0, 0, second(i))),
            ]
        else:
            shapes = [(2, 2, 2, piece, 1024)] * 2
            out_specs = [pl.BlockSpec((2, 2, 1, piece, 256), lambda i, p: (0, 0, i // 4, 0, i % 4))] * 2
    lefts = [v for p in pairs for v in p[:2]]
    rights = [v for p in pairs for v in p[2:]]
    outs = pl.pallas_call(
        functools.partial(grad_kernel, kind),
        grid_spec=pltpu.PrefetchScalarGridSpec(
            num_scalar_prefetch=1,
            grid=(8,),
            in_specs=[whole] * len(lefts) + right_specs,
            out_specs=out_specs,
            scratch_shapes=[pltpu.VMEM((width, 2 * rows), bf16)] * len(pairs),
        ),
        out_shape=[jax.ShapeDtypeStruct(shape, bf16) for shape in shapes],
        compiler_params=pltpu.CompilerParams(vmem_limit_bytes=40 << 20),
        cost_estimate=cheap(),
        name="weight_grad_" + kind,
    )(place, *lefts, *rights)
    return [v.reshape(2, -1, 1024) for v in outs]


def halve_kernel(count, *refs):
    total = refs[0][...].astype(f32)
    for part in refs[1:count]:
        total += part[...].astype(f32)
    total = total.astype(bf16)
    if len(refs) == count + 1:
        refs[count][...] = total
    else:
        refs[count][...] = total[0]
        refs[count + 1][...] = total[1]


def halve(*parts, split=True):
    _, rows, cols = parts[0].shape
    tile = min(rows, 128)
    block = pl.BlockSpec((2, tile, cols), lambda i: (0, i, 0))
    half = pl.BlockSpec((tile, cols), lambda i: (i, 0))
    outs = pl.pallas_call(
        functools.partial(halve_kernel, len(parts)),
        grid=(rows // tile,),
        out_shape=[jax.ShapeDtypeStruct((rows, cols), bf16)] * 2 if split else [jax.ShapeDtypeStruct((2, rows, cols), bf16)],
        in_specs=[block] * len(parts),
        out_specs=[half] * 2 if split else [block],
        cost_estimate=cheap(),
        name="halve",
    )(*parts)
    if not split:
        return outs[0]
    if rows == tile:
        return outs
    return [v.reshape(2, rows // 2, cols) for v in outs]


def plain_sum(pairs):
    grads = []
    for left, left_far, right, right_far in pairs:
        both = jnp.concatenate([right, right_far], -2)
        if both.ndim == 3:
            both = jnp.concatenate([both[0], both[1]], 1)
        both = dot(jnp.concatenate([left, left_far], 0), both, 0, 0)
        grads.append(both.astype(bf16).reshape(both.shape[0], 2, -1))
    grads = jnp.concatenate(grads, 2)
    mine = add(grads[:, 0], swap(grads[:, 1], "tp"))
    return [lax.psum_scatter(mine, "dp", scatter_dimension=0, tiled=True)]


def close_kernel(place, *refs):
    parts, (mine, send) = refs[:-2], refs[-2:]
    total = parts[0][...].astype(f32)
    for part in parts[1:]:
        total += part[...].astype(f32)
    rows = mine.shape[0]
    for core in range(2):

        @pl.when(place[2] == core)
        def _(core=core):
            mine[...] = total[core * rows : (core + 1) * rows]
            send[...] = total[(1 - core) * rows : (2 - core) * rows]


def close(place, parts):
    rows, cols = parts[0].shape
    return pl.pallas_call(
        close_kernel,
        out_shape=[jax.ShapeDtypeStruct((rows // 2, cols), f32)] * 2,
        in_specs=[pl.BlockSpec(memory_space=pltpu.SMEM)] + [pl.BlockSpec(memory_space=pltpu.VMEM)] * len(parts),
        out_specs=[pl.BlockSpec(memory_space=pltpu.VMEM)] * 2,
        cost_estimate=cheap(),
        name="close",
    )(place, *parts)


def settle_kernel(turns, place, mine, other, *outs):
    size = mine.shape[1] // len(turns)
    for core in range(2):

        @pl.when(place[2] == core)
        def _(core=core):
            for n, turn in enumerate(turns):
                for part, at in ((mine, core), (other, 1 - core)):
                    value = part[:, n * size : (n + 1) * size]
                    if turn:
                        outs[n][at * size : (at + 1) * size, :] = value.T
                    else:
                        outs[n][:, at * size : (at + 1) * size] = value


def settle_columns(place, mine, turns):
    mine, send = mine
    other = swap(send, "ctx")
    rows, cols = mine.shape
    size = 2 * cols // len(turns)
    return pl.pallas_call(
        functools.partial(settle_kernel, turns),
        out_shape=[jax.ShapeDtypeStruct((size, rows) if turn else (rows, size), f32) for turn in turns],
        in_specs=[pl.BlockSpec(memory_space=pltpu.SMEM)] + [pl.BlockSpec(memory_space=pltpu.VMEM)] * 2,
        out_specs=[pl.BlockSpec(memory_space=pltpu.VMEM)] * len(turns),
        cost_estimate=cheap(),
        name="settle_columns",
    )(place, mine, other)


def body(dp_count, tokens, segments, query_weight, key_weight, value_weight, out_weight, up_weight, down_weight, query_bias, value_bias, out_bias, up_bias, down_bias, attn_gain, attn_shift, mlp_gain, mlp_shift, cotangent):
    c = lax.axis_index("ctx")
    t = lax.axis_index("tp")
    d = lax.axis_index("dp")
    place = jnp.stack([d // 2, d % 2, c, t]).astype(jnp.int32)
    half, width = tokens.shape[1], tokens.shape[2]
    rows = 2 * half
    inner = 2 * query_bias.shape[0]
    ff = 2 * up_bias.shape[0]
    piece_rows = query_weight.shape[0]

    one = jnp.stack([query_weight, key_weight, value_weight, out_weight.T], 1)
    one = one.reshape(piece_rows, 4, 2, -1).transpose(2, 0, 1, 3).reshape(2, piece_rows, -1)
    one = one.astype(bf16)
    piece = order(c, take(one, c), swap(take(one, 1 - c), "ctx"), 0)
    unit = piece.shape[1]
    quarter = unit // 4
    qkv_mine, out_mine = gather_weights(piece, ((0, 3 * quarter), (3 * quarter, quarter)), place, dp_count)
    w_qkv = (qkv_mine, swap(qkv_mine, "ctx"))
    w_out = (out_mine, swap(out_mine, "ctx"))
    rest = jnp.stack([up_weight.astype(bf16), down_weight.T.astype(bf16)])
    rest = lax.all_gather(rest, ("tp", "dp", "ctx"), axis=1, tiled=True)

    biases = jnp.concatenate([query_bias, value_bias, up_bias])
    biases = jnp.stack([biases, swap(biases, "tp")])
    hin = inner // 2

    def near(values):
        values = values.reshape(2, 2, -1).transpose(1, 0, 2)
        return jnp.where(c == 0, values, values[::-1])

    bias_q, bias_v = near(biases[:, :hin]), near(biases[:, hin : 2 * hin])
    bias_up = jnp.where(t == 0, biases[:, 2 * hin :], biases[::-1, 2 * hin :])
    bias_qkv = jnp.stack([bias_q, jnp.zeros_like(bias_q), bias_v], 2).reshape(2, -1)

    seq = 2 * t + c
    other_seq = 2 * t + 1 - c
    pair_mine = jnp.stack([take(tokens, seq), take(cotangent, seq), take(tokens, other_seq)])
    pair_send = jnp.stack([take(tokens, other_seq), take(cotangent, other_seq), take(tokens, seq)])
    got = swap(pair_send, "ctx")
    flat = order(c, pair_mine[0], got[0], 0)
    flat_far = order(c, pair_mine[2], got[2], 0)
    grad_output = order(c, pair_mine[1], got[1], 0)
    flat = tie(flat, flat_far, grad_output)
    seg = take(segments, seq)

    def far(values):
        return swap(values, "ctx")

    qkv = [(dot(flat, w_qkv[r], 1, 0) + bias_qkv[r]).astype(bf16) for r in range(2)]
    attended = [attend(qkv[r], seg) for r in range(2)]
    context = [a[0] for a in attended]
    probs = [a[1] for a in attended]
    resid_one = flat.astype(f32) + dot(context[0], w_out[0], 1, 1) + dot(context[1], w_out[1], 1, 1) + out_bias
    normed_one, unit_one, inverse_one = norm_forward(resid_one, attn_gain, attn_shift)
    normed_low = normed_one.astype(bf16)
    normed_far, context_far = far(normed_low), far(context[1])
    normed_low = tie(normed_low, normed_far, context_far)
    hidden_near, hidden_far, output, grad_two, grad_mixed, pre_near, pre_far, sums_two, sums_pre = mlp(
        place, normed_low, rest, bias_up, normed_one, grad_output, down_bias, mlp_gain, mlp_shift
    )
    hidden_far, pre_got, grad_mixed_far = far(hidden_far), far(pre_far), far(grad_mixed)

    layer_out = lax.all_gather(output, ("tp", "ctx"), axis=0, tiled=False)
    layer_out = lax.dynamic_slice_in_dim(layer_out, c * half, half, 1)
    grad_one, grad_attended, *grad_context, sums_one = mlp_back(
        place, pre_near, pre_far, rest, grad_two, unit_one, inverse_one, attn_gain, *w_out, ()
    )
    quick = dp_count == 8
    down_pairs = [(tie(grad_mixed, grad_attended), grad_mixed_far, hidden_near, hidden_far)]
    up_pairs = [(normed_low, normed_far, pre_near, pre_got)]
    if quick:
        down_keep, down_send = weight_grad(place, down_pairs, "x")
        up_keep, up_send = weight_grad(place, up_pairs, "tp")
        sent = (down_send, up_send)
    else:
        down_last, up_last, sent = plain_sum(down_pairs), plain_sum(up_pairs), ()
    back = [attend_back(qkv[r], probs[r], grad_context[r], sent) for r in range(2)]
    grad_qkv = [b[0] for b in back]
    sums = jnp.stack([b[1] for b in back])[:, :, :, 0]
    grad_qkv_far = far(grad_qkv[1])
    attended_far = far(grad_attended)
    one_pairs = [(flat, flat_far, grad_qkv[0], grad_qkv_far), (grad_attended, attended_far, context[0], context_far)]
    if quick:
        one_keep, one_send, two_keep, two_send = weight_grad(place, one_pairs, "one")
        down_keep, down_send = halve(tie(down_keep, one_send), over("x", down_send))
        up_keep, up_send = halve(tie(up_keep, one_send), over("t", up_send))
        up_got = over("x", up_send)
        down_got = over("l", down_send)
    else:
        one_last = plain_sum(one_pairs)
    sent_back = dot(grad_qkv[0], w_qkv[0], 1, 1) + dot(grad_qkv[1], w_qkv[1], 1, 1)
    input_grad = (grad_one + sent_back).astype(bf16).reshape(2, half, width)
    got = swap(take(input_grad, 1 - c), "ctx")
    input_grad = order(c, take(input_grad, c)[None], got[None], 0)
    if quick:
        small_after = one_send
        one_got, two_got = over("t", one_send), over("x", two_send)
        two_keep, two_send = halve(tie(two_keep, down_got), two_got)
        one_keep, one_send = halve(one_keep, one_got)
        two_got, one_got = over("t", two_send), over("x", one_send)
        down_keep, down_send = halve(down_keep, down_got)
        down_got = over("h", down_send)
        low_got = over("l", halve(tie(two_keep, up_got), two_got, split=False))
        up_keep, up_send = halve(up_keep, up_got)
        up_got = over("l", up_send)
        down_keep, down_send = halve(down_keep, down_got)
        one_keep, one_send = halve(tie(one_keep, up_got), one_got, low_got)
        up_keep, up_send = halve(up_keep, up_got)
        up_last = (up_keep, over("h", up_send))
        down_last = (down_keep, over("t", down_send))
        one_last = (one_keep, over("h", one_send))
        sums_one, sums_two, sums_pre = (tie(v, small_after) for v in (sums_one, sums_two, sums_pre))
    input_grad = order(t, input_grad, swap(input_grad, "tp"), 0)
    (down_shard,) = settle_columns(place, close(place, down_last), (True,))
    (up_shard,) = settle_columns(place, close(place, up_last), (False,))
    one_shard = settle_columns(place, close(place, one_last), (False, False, False, True))

    sums_one, sums_two = jnp.sum(sums_one, 1), jnp.sum(sums_two, 1)

    def settle(values):
        values = jnp.where(c == 0, values, values[::-1])
        values = jnp.where(t == 0, values, values[:, ::-1])
        return values.transpose(1, 0, 2).reshape(-1)

    small = jnp.concatenate(
        [settle(sums[:, :, 0]), settle(sums[:, :, 1]), settle(jnp.sum(sums_pre, 1).reshape(2, 2, -1)), sums_one[2], sums_two[2], sums_one[0], sums_one[1], sums_two[0], sums_two[1]]
    )
    small = tie(small.reshape(-1, 128), layer_out)
    small = lax.all_gather(small, ("dp", "ctx", "tp"), axis=0, tiled=False)
    small = jnp.sum(small, axis=0).reshape(-1)

    def cut_tp(start, size):
        return lax.dynamic_slice_in_dim(small, start + t * (size // 2), size // 2)

    at = 2 * inner + ff
    vectors = [lax.slice_in_dim(small, at + i * width, at + (i + 1) * width) for i in range(6)]

    return (
        layer_out,
        input_grad,
        *one_shard,
        up_shard,
        down_shard,
        cut_tp(0, inner),
        cut_tp(inner, inner),
        vectors[0],
        cut_tp(2 * inner, ff),
        *vectors[1:],
    )


def solution(mesh):
    weight_in, weight_out = P(("dp", "ctx"), "tp"), P("tp", ("dp", "ctx"))
    rows = P("dp", "ctx", None)
    weights = (weight_in, weight_in, weight_in, weight_out, weight_in, weight_out)
    vectors = (P("tp"), P("tp"), P(), P("tp"), P(), P(), P(), P(), P())
    dp_count = mesh.shape["dp"]

    def run(*args):
        return body(dp_count, *args)

    return jax.shard_map(
        run,
        mesh=mesh,
        in_specs=(rows, P("dp", None), *weights, *vectors, rows),
        out_specs=(rows, rows, *weights, *vectors),
        check_vma=False,
    )
```

```python
import functools

import jax
import jax.numpy as jnp
from jax import lax
from jax.experimental import pallas as pl
from jax.experimental.pallas import tpu as pltpu
from jax.sharding import PartitionSpec as P

HEAD_DIM = 64
LANES = 2 * HEAD_DIM

epsilon = 1e-12
root_half = 0.7071067811865476
inv_root_two_pi = 0.3989422804014327
bf16 = jnp.bfloat16
f32 = jnp.float32


def dot(left, right, left_dim, right_dim):
    return lax.dot_general(left, right, (((left_dim,), (right_dim,)), ((), ())), preferred_element_type=f32)


def norm_forward(values, gain, shift):
    centre = values - jnp.mean(values, axis=-1, keepdims=True)
    inverse = lax.rsqrt(jnp.mean(centre * centre, axis=-1, keepdims=True) + epsilon)
    normed = centre * inverse
    return (normed * gain + shift, normed, inverse)


def swap(values, axis):
    return lax.ppermute(values, axis, [(0, 1), (1, 0)])


def swap_x(values):
    return lax.ppermute(values, "dp", [(i, i ^ 1) for i in range(8)])


def shift_z(values, step):
    return lax.ppermute(values, "dp", [(i, (i + 2 * step) % 8) for i in range(8)])


def take(values, index, axis=0):
    return lax.dynamic_index_in_dim(values, index, axis, keepdims=False)


def add(left, right):
    return (left.astype(f32) + right.astype(f32)).astype(bf16)


def order(index, mine, other, axis):
    return jnp.where(index == 0, jnp.concatenate([mine, other], axis), jnp.concatenate([other, mine], axis))


def assemble_kernel(cuts, place, one, one_y, two, two_x, *rest):
    outs, sems = rest[: len(cuts)], rest[len(cuts)]
    z, x = place[0], place[1]
    rows = one.shape[2]
    copies = []
    for k in range(4):
        for far_x in range(2):
            block = lax.rem(z + 4 - k, 4) * 2 + lax.rem(x + far_x, 2)
            at = pl.ds(pl.multiple_of(block * rows, rows), rows)
            for far_t in range(2):
                if k < 2:
                    source = (one_y if far_t else one).at[far_x, k]
                else:
                    source = (two_x if far_x else two).at[far_t, k - 2]
                for n, (start, size) in enumerate(cuts):
                    copies.append(
                        pltpu.make_async_copy(
                            source.at[:, start : start + size],
                            outs[n].at[at, far_t * size : far_t * size + size],
                            sems.at[len(copies)],
                        )
                    )
                    copies[-1].start()
    for copy in copies:
        copy.wait()


def gather_weights(piece, cuts, place, dp_count):
    rows, cols = piece.shape
    total = dp_count * rows
    if dp_count != 8:
        t = lax.axis_index("tp")
        both = lax.all_gather(piece, ("tp", "dp"), axis=0, tiled=True).reshape(2, total, cols)
        first, second = take(both, t), take(both, 1 - t)
        return [
            jnp.concatenate([first[:, s : s + n], second[:, s : s + n]], 1) for s, n in cuts
        ]
    line = [piece] + [shift_z(piece, k) for k in range(1, 4)]
    one, two = jnp.stack(line[:2]), jnp.stack(line[2:])
    one_x, two_y = swap_x(one), swap(two, "tp")
    one, two = jnp.stack([one, one_x]), jnp.stack([two, two_y])
    one_y, two_x = swap(one, "tp"), swap_x(two)
    anyspace = pl.BlockSpec(memory_space=pl.ANY)


    return pl.pallas_call(
        functools.partial(assemble_kernel, cuts),
        out_shape=[jax.ShapeDtypeStruct((total, 2 * n), bf16) for _, n in cuts],
        in_specs=[pl.BlockSpec(memory_space=pltpu.SMEM)] + [anyspace] * 4,
        out_specs=[pl.BlockSpec(memory_space=pltpu.VMEM)] * len(cuts),
        scratch_shapes=[pltpu.SemaphoreType.DMA((16 * len(cuts),))],
        compiler_params=pltpu.CompilerParams(vmem_limit_bytes=24 << 20),
        name="assemble",
    )(place, one, one_y, two, two_x)


def tie_kernel(*refs):
    pass


def tie(value, *after):
    anyspace = pl.BlockSpec(memory_space=pl.ANY)
    return pl.pallas_call(
        tie_kernel,
        out_shape=jax.ShapeDtypeStruct(value.shape, value.dtype),
        in_specs=[anyspace] * (1 + len(after)),
        out_specs=anyspace,
        input_output_aliases={0: 0},
        name="tie",
    )(value, *after)


def attend_kernel(qkv, seg_keys, seg_queries, context, probs, bias):
    quarter = qkv.shape[1] // 3

    @pl.when(pl.program_id(0) == 0)
    def _():
        bias[...] = jnp.where(seg_keys[...] == seg_queries[...], 0.0, -1000000000.0)

    low = lax.broadcasted_iota(jnp.int32, (1, LANES), 1) < HEAD_DIM
    for pair in range(quarter // LANES):
        cols = slice(pair * LANES, pair * LANES + LANES)
        query = qkv[:, cols] * 0.125
        key = qkv[:, quarter + pair * LANES : quarter + pair * LANES + LANES]
        value_t = qkv[:, 2 * quarter + pair * LANES : 2 * quarter + pair * LANES + LANES].T
        parts = []
        for h in range(2):
            mine = jnp.where(low if h == 0 else ~low, query, jnp.zeros_like(query))
            scores = dot(key, mine, 1, 1) + bias[...]
            raised = jnp.exp(scores - jnp.max(scores, axis=0, keepdims=True))
            prob = (raised * (1.0 / jnp.sum(raised, axis=0, keepdims=True))).astype(bf16)
            probs[2 * pair + h] = prob
            parts.append(dot(value_t[h * HEAD_DIM : (h + 1) * HEAD_DIM], prob, 1, 0))
        context[:, cols] = jnp.concatenate(parts, 0).T.astype(bf16)


def attend(qkv, seg):
    rows, cols = qkv.shape
    half = cols // 2
    quarter = half // 3
    heads = quarter // HEAD_DIM
    return pl.pallas_call(
        attend_kernel,
        grid=(2,),
        out_shape=[jax.ShapeDtypeStruct((rows, 2 * quarter), bf16), jax.ShapeDtypeStruct((2 * heads, rows, rows), bf16)],
        in_specs=[
            pl.BlockSpec((rows, half), lambda i: (0, i)),
            pl.BlockSpec((rows, 1), lambda i: (0, 0)),
            pl.BlockSpec((1, rows), lambda i: (0, 0)),
        ],
        out_specs=[pl.BlockSpec((rows, quarter), lambda i: (0, i)), pl.BlockSpec((heads, rows, rows), lambda i: (i, 0, 0))],
        scratch_shapes=[pltpu.VMEM((rows, rows), f32)],
        compiler_params=pltpu.CompilerParams(vmem_limit_bytes=48 << 20),
        cost_estimate=pl.CostEstimate(flops=1024, bytes_accessed=1024, transcendentals=0),
        name="attend",
    )(qkv, seg.reshape(rows, 1), seg.reshape(1, rows))


def attend_back_kernel(qkv, probs, upstream, *rest):
    grads, sums = rest[-2:]
    quarter = qkv.shape[1] // 3
    low = lax.broadcasted_iota(jnp.int32, (1, LANES), 1) < HEAD_DIM
    for pair in range(quarter // LANES):
        cols = [slice(n * quarter + pair * LANES, n * quarter + pair * LANES + LANES) for n in range(3)]
        query, key, value = (qkv[:, c] for c in cols)
        key_t = key.T
        above = upstream[:, cols[0]]
        grad_q, grad_k, grad_v = [], [], []
        for h in range(2):
            mine = jnp.where(low if h == 0 else ~low, above, jnp.zeros_like(above))
            grad_p = dot(value, mine, 1, 1)
            prob_low = probs[2 * pair + h]
            prob = prob_low.astype(f32)
            weighted = prob * grad_p
            inner = jnp.sum(weighted, axis=0, keepdims=True)
            grad_s = (weighted - prob * inner).astype(bf16)
            grad_k.append(dot(grad_s, query, 1, 0))
            grad_v.append(dot(prob_low, above, 1, 0))
            grad_q.append(dot(key_t[h * HEAD_DIM : (h + 1) * HEAD_DIM], grad_s, 1, 0))
        out_q = (jnp.concatenate(grad_q, 0) * 0.125).T.astype(bf16)
        out_v = jnp.where(low, grad_v[0], grad_v[1]).astype(bf16)
        grads[:, cols[0]] = out_q
        grads[:, cols[1]] = (jnp.where(low, grad_k[0], grad_k[1]) * 0.125).astype(bf16)
        grads[:, cols[2]] = out_v
        for n, out in ((0, out_q), (1, out_v)):
            total = jnp.sum(out.astype(f32), axis=0, keepdims=True)
            sums[0, n, :, cols[0]] = jnp.broadcast_to(total, (8, LANES))


def attend_back(qkv, probs, upstream, after):
    rows, cols = qkv.shape
    half = cols // 2
    quarter = half // 3
    heads = quarter // HEAD_DIM
    return pl.pallas_call(
        attend_back_kernel,
        grid=(2,),
        out_shape=[jax.ShapeDtypeStruct((rows, cols), bf16), jax.ShapeDtypeStruct((2, 2, 8, quarter), f32)],
        in_specs=[
            pl.BlockSpec((rows, half), lambda i: (0, i)),
            pl.BlockSpec((heads, rows, rows), lambda i: (i, 0, 0)),
            pl.BlockSpec((rows, quarter), lambda i: (0, i)),
        ]
        + [pl.BlockSpec(memory_space=pl.ANY)] * len(after),
        out_specs=[pl.BlockSpec((rows, half), lambda i: (0, i)), pl.BlockSpec((1, 2, 8, quarter), lambda i: (i, 0, 0, 0))],
        compiler_params=pltpu.CompilerParams(vmem_limit_bytes=48 << 20),
        cost_estimate=pl.CostEstimate(flops=1024, bytes_accessed=1024, transcendentals=0),
        name="attend_back",
    )(qkv, probs, upstream, *after)


CHUNK = 32


def cheap():
    return pl.CostEstimate(flops=1024, bytes_accessed=1024, transcendentals=0)


def clamp(i, low, count):
    return jnp.clip(i - low, 0, count - 1)


def put(near, far, i, steps, value):
    @pl.when(i < steps)
    def _():
        near[0] = value

    @pl.when(i >= steps)
    def _():
        far[0] = value


def halves_of(group, width, unit):
    core = lambda i, p: lax.rem(p[2] + i // 4, 2)
    return pl.BlockSpec((1, width, unit // 2), lambda i, p: (group, (i // 2) % 2, core(i, p) * 2 + i % 2))


def blocks_of(group, width, unit):
    return pl.BlockSpec((1, width, unit), lambda i, p: (group, lax.rem(p[3] + i % 2, 2), lax.rem(p[2] + i // 2, 2)))


def half_outs(rows, unit):
    return [pl.BlockSpec((1, rows, unit // 2), lambda i, p, n=n: (clamp(i, n, 4) // 2, 0, clamp(i, n, 4) % 2)) for n in (0, 4)]


def block_ins(rows, unit):
    return [pl.BlockSpec((1, rows, unit), lambda i, p, n=n: (clamp(i, n, 2), 0, 0)) for n in (0, 2)]


def fixed(*shape):
    return pl.BlockSpec(shape, lambda i, p: (0,) * len(shape))


def call(kernel, place, grid, ins, in_specs, outs, out_specs, scratch, name):
    return pl.pallas_call(
        kernel,
        grid_spec=pltpu.PrefetchScalarGridSpec(num_scalar_prefetch=1, grid=(grid,), in_specs=in_specs, out_specs=out_specs, scratch_shapes=scratch),
        out_shape=[jax.ShapeDtypeStruct(*o) for o in outs],
        compiler_params=pltpu.CompilerParams(vmem_limit_bytes=48 << 20),
        cost_estimate=cheap(),
        name=name,
    )(place, *ins)


def mean(values):
    return jnp.sum(values, axis=-1, keepdims=True) * (1.0 / values.shape[-1])


def fold(values):
    return jnp.sum(values.reshape(-1, 8, values.shape[-1]), axis=0)


def mlp_kernel(place, low, up_weight, down_weight, up_bias, normed, above, bias, gain, shift, near, far, out, grad, grad_low, pre_near, pre_far, sums, up_sums, units, slope, down, total):
    i = pl.program_id(0)
    rows, width = low.shape
    cols = up_weight.shape[2]
    tile = cols // 4

    def up(out_ref):
        for n in range(4):
            at = slice(n * tile, n * tile + tile)
            pre = dot(low[...], up_weight[0, :, at], 1, 0) + up_bias[0, :, at]
            half = 0.5 * (1.0 + lax.erf(pre * root_half))
            value = (pre * half).astype(bf16)
            out_ref[0, :, at] = value
            units[i, :, at] = value
            slope[i, :, at] = (half + pre * jnp.exp(-0.5 * pre * pre) * inv_root_two_pi).astype(bf16)

    pl.when(i < 2)(lambda: up(near))
    pl.when(jnp.logical_and(i >= 2, i < 4))(lambda: up(far))

    @pl.when(i == 4)
    def _():
        total[...] = normed[...] + bias[...]

    @pl.when(jnp.logical_and(i >= 4, i < 8))
    def _():
        down[i - 4] = down_weight[0]
        total[...] += dot(units[i - 4], down_weight[0], 1, 1)

    @pl.when(i == 7)
    def _():
        def step(k, carry):
            at = pl.ds(pl.multiple_of(k * CHUNK, CHUNK), CHUNK)
            centre = total[at] - mean(total[at])
            inverse = lax.rsqrt(mean(centre * centre) + epsilon)
            unit = centre * inverse
            out[at] = (unit * gain[...] + shift[...]).astype(bf16)
            upper = above[at].astype(f32)
            scaled = upper * gain[...]
            lower = inverse * (scaled - mean(scaled) - unit * mean(scaled * unit))
            grad[at] = lower
            grad_low[at] = lower.astype(bf16)
            return tuple(c + fold(v) for c, v in zip(carry, (upper * unit, upper, lower)))

        zero = jnp.zeros((8, width), f32)
        done = lax.fori_loop(0, rows // CHUNK, step, (zero,) * 3)
        for n in range(3):
            sums[n] = done[n]

    def pre(out_ref):
        for n in range(4):
            at = slice(n * tile, n * tile + tile)
            value = (dot(grad_low[...], down[i - 8, :, at], 1, 0) * slope[i - 8, :, at].astype(f32)).astype(bf16)
            out_ref[0, :, at] = value
            up_sums[0, :, at] = fold(value.astype(f32))

    pl.when(jnp.logical_and(i >= 8, i < 10))(lambda: pre(pre_near))
    pl.when(i >= 10)(lambda: pre(pre_far))


def mlp(place, low, weights, up_bias, normed, above, bias, gain, shift):
    rows, width = low.shape
    unit = weights.shape[2] // 2

    def still(*shape):
        return pl.BlockSpec(shape, lambda i, p: (0,) * len(shape), pipeline_mode=pl.Buffered(1))

    def block(group, first):
        def index(i, p):
            j = clamp(i, first, 4)
            return (group, lax.rem(p[3] + j % 2, 2), lax.rem(p[2] + j // 2, 2))

        return pl.BlockSpec((1, width, unit), index)

    def outs(first):
        return [pl.BlockSpec((1, rows, unit), lambda i, p, n=n: (clamp(i, n, 2), 0, 0)) for n in (first, first + 2)]

    def bias_index(i, p):
        j = clamp(i, 0, 4)
        return (lax.rem(p[3] + j % 2, 2) * 2 + lax.rem(p[2] + j // 2, 2), 0, 0)

    one, vector = still(rows, width), still(1, width)
    return pl.pallas_call(
        mlp_kernel,
        grid_spec=pltpu.PrefetchScalarGridSpec(
            num_scalar_prefetch=1,
            grid=(12,),
            in_specs=[one, block(0, 0), block(1, 4), pl.BlockSpec((1, 1, unit), bias_index), one, one, vector, vector, vector],
            out_specs=outs(0) + [one, one, one] + outs(8) + [still(3, 8, width), pl.BlockSpec((1, 8, unit), lambda i, p: (clamp(i, 8, 4), 0, 0))],
            scratch_shapes=[pltpu.VMEM((4, rows, unit), bf16)] * 2 + [pltpu.VMEM((4, width, unit), bf16), pltpu.VMEM((rows, width), f32)],
        ),
        out_shape=[jax.ShapeDtypeStruct(*o) for o in (
            [((2, rows, unit), bf16)] * 2
            + [((rows, width), bf16), ((rows, width), f32), ((rows, width), bf16)]
            + [((2, rows, unit), bf16)] * 2
            + [((3, 8, width), f32), ((4, 8, unit), f32)]
        )],
        compiler_params=pltpu.CompilerParams(vmem_limit_bytes=60 << 20),
        cost_estimate=cheap(),
        name="mlp",
    )(place, low, weights, weights, up_bias.reshape(4, 1, unit), normed, above, bias[None], gain[None], shift[None])


def mlp_back_kernel(place, near, far, weight, grad_two, unit_one, inverse, gain, out_near, out_far, grad, grad_low, near_context, far_context, sums, total):
    i = pl.program_id(0)

    @pl.when(i == 0)
    def _():
        total[...] = grad_two[...] + dot(near[0], weight[0], 1, 1)

    @pl.when(i == 1)
    def _():
        total[...] += dot(near[0], weight[0], 1, 1)

    @pl.when(i >= 2)
    def _():
        total[...] += dot(far[0], weight[0], 1, 1)

    @pl.when(i == 3)
    def _():
        def step(k, carry):
            at = pl.ds(pl.multiple_of(k * CHUNK, CHUNK), CHUNK)
            upper = total[at]
            unit = unit_one[at]
            scaled = upper * gain[...]
            down = inverse[at] * (scaled - mean(scaled) - unit * mean(scaled * unit))
            grad[at] = down
            grad_low[at] = down.astype(bf16)
            return tuple(c + fold(v) for c, v in zip(carry, (upper * unit, upper, down)))

        zero = jnp.zeros((8, grad.shape[1]), f32)
        done = lax.fori_loop(0, grad.shape[0] // CHUNK, step, (zero,) * 3)
        for n in range(3):
            sums[n] = done[n]
        near_context[...] = dot(grad_low[...], out_near[...], 1, 0).astype(bf16)
        far_context[...] = dot(grad_low[...], out_far[...], 1, 0).astype(bf16)


def mlp_back(place, near, far, weights, grad_two, unit_one, inverse, gain, out_near, out_far, after):
    rows, width = grad_two.shape
    unit = weights.shape[2] // 2
    part = out_near.shape[1]
    one = fixed(rows, width)

    def kernel(*refs):
        mlp_back_kernel(*refs[:10], *refs[10 + len(after) :])

    return call(
        kernel,
        place,
        4,
        (near, far, weights, grad_two, unit_one, inverse, gain[None], out_near, out_far, *after),
        block_ins(rows, unit) + [blocks_of(0, width, unit), one, one, fixed(rows, 1), fixed(1, width)] + [fixed(width, part)] * 2 + [pl.BlockSpec(memory_space=pl.ANY)] * len(after),
        [((rows, width), f32), ((rows, width), bf16)] + [((rows, part), bf16)] * 2 + [((3, 8, width), f32)],
        [one, one] + [fixed(rows, part)] * 2 + [fixed(3, 8, width)],
        [pltpu.VMEM((rows, width), f32)],
        "mlp_back",
    )


def over(axis, values):
    if axis == "t":
        return swap(values, "tp")
    if axis == "x":
        return swap_x(values)
    flip = 2 if axis == "l" else 4
    return lax.ppermute(values, "dp", [(i, i ^ flip) for i in range(8)])


def grad_kernel(kind, place, *refs):
    lefts = 2 if kind == "one" else 1
    sources = refs[: 2 * lefts]
    rights = refs[2 * lefts : 4 * lefts]
    outs = refs[4 * lefts : -lefts]
    turned = refs[-lefts:]
    i = pl.program_id(0)
    z, x = place[0], place[1]
    rows, width = sources[0].shape
    piece = width // 8

    @pl.when(i == 0)
    def _():
        for at in range(8):
            a, b, c = at // 4, (at // 2) % 2, at % 2
            far_x, low, high = (b, a, c) if kind == "one" else (a, b, c)
            block = (2 * lax.rem(z // 2 + high, 2) + lax.rem(z + low, 2)) * 2 + lax.rem(x + far_x, 2)
            cols = pl.ds(pl.multiple_of(block * piece, piece), piece)
            for n in range(lefts):
                for far in range(2):
                    turned[n][at * piece : (at + 1) * piece, far * rows : (far + 1) * rows] = sources[2 * n + far][:, cols].T

    def work(n):
        near, away = rights[2 * n], rights[2 * n + 1]
        pick = (lambda r: r[...]) if kind == "one" else (lambda r: r[0])
        out = dot(turned[n][...], jnp.concatenate([pick(near), pick(away)], 0), 1, 0).astype(bf16)
        if kind == "tp":
            out = out.reshape(2, 4 * piece, out.shape[1])
            pl.when(i < 2)(lambda: outs[0].__setitem__(..., out))
            pl.when(i >= 2)(lambda: outs[1].__setitem__(..., out))
        elif kind == "x":
            out = out.reshape(2, 2, 2, piece, out.shape[1])
            outs[0][:, :, 0] = out[0]
            outs[1][:, :, 0] = out[1]
        else:
            out = out.reshape(2, 2, 2 * piece, out.shape[1])
            pl.when(i < 4)(lambda: outs[0].__setitem__(..., out[0]))
            pl.when(i >= 4)(lambda: outs[1].__setitem__(..., out[0]))
            outs[2][0] = out[1, 0]
            outs[3][0] = out[1, 1]

    if lefts == 1:
        work(0)
    else:
        last = lax.rem(i, 4) == 3
        pl.when(jnp.logical_not(last))(lambda: work(0))
        pl.when(last)(lambda: work(1))


def weight_grad(place, pairs, kind):
    rows, width = pairs[0][0].shape
    piece = width // 8
    whole = pl.BlockSpec((rows, width), lambda i, p: (0, 0))
    tile = 256 if kind == "one" else 512
    steps = 1024 // tile
    first = lambda i: jnp.minimum(i, steps - 1)
    second = lambda i: jnp.maximum(i, steps) - steps
    if kind == "one":
        maps = [lambda i, p: (0, (i // 4) * 3 + jnp.minimum(i % 4, 2)), lambda i, p: (0, i // 4)]
        right_specs = [pl.BlockSpec((rows, 256), m) for m in maps for _ in range(2)]
        shapes = [(2, 2 * piece, 1024)] * 4
        out_specs = [
            pl.BlockSpec((2, 2 * piece, 256), lambda i, p: (0, 0, first(i))),
            pl.BlockSpec((2, 2 * piece, 256), lambda i, p: (0, 0, second(i))),
        ] + [pl.BlockSpec((1, 2 * piece, 256), lambda i, p: (i // 4, 0, i % 4))] * 2
    else:
        right_specs = [pl.BlockSpec((1, rows, tile), lambda i, p: (i // steps, 0, i % steps))] * 2
        if kind == "tp":
            shapes = [(2, 4 * piece, 1024)] * 2
            out_specs = [
                pl.BlockSpec((2, 4 * piece, tile), lambda i, p: (0, 0, first(i))),
                pl.BlockSpec((2, 4 * piece, tile), lambda i, p: (0, 0, second(i))),
            ]
        else:
            shapes = [(2, 2, 2, piece, 1024)] * 2
            out_specs = [pl.BlockSpec((2, 2, 1, piece, tile), lambda i, p: (0, 0, i // steps, 0, i % steps))] * 2
    lefts = [v for p in pairs for v in p[:2]]
    rights = [v for p in pairs for v in p[2:]]
    outs = pl.pallas_call(
        functools.partial(grad_kernel, kind),
        grid_spec=pltpu.PrefetchScalarGridSpec(
            num_scalar_prefetch=1,
            grid=(2 * steps,),
            in_specs=[whole] * len(lefts) + right_specs,
            out_specs=out_specs,
            scratch_shapes=[pltpu.VMEM((width, 2 * rows), bf16)] * len(pairs),
        ),
        out_shape=[jax.ShapeDtypeStruct(shape, bf16) for shape in shapes],
        compiler_params=pltpu.CompilerParams(vmem_limit_bytes=(60 if kind == "one" else 40) << 20),
        cost_estimate=cheap(),
        name="weight_grad_" + kind,
    )(place, *lefts, *rights)
    return [v.reshape(2, -1, 1024) for v in outs]


def halve_kernel(count, *refs):
    total = refs[0][...].astype(f32)
    for part in refs[1:count]:
        total += part[...].astype(f32)
    total = total.astype(bf16)
    if len(refs) == count + 1:
        refs[count][...] = total
    else:
        refs[count][...] = total[0]
        refs[count + 1][...] = total[1]


def halve(*parts, split=True):
    _, rows, cols = parts[0].shape
    tile = min(rows, 128)
    block = pl.BlockSpec((2, tile, cols), lambda i: (0, i, 0))
    half = pl.BlockSpec((tile, cols), lambda i: (i, 0))
    outs = pl.pallas_call(
        functools.partial(halve_kernel, len(parts)),
        grid=(rows // tile,),
        out_shape=[jax.ShapeDtypeStruct((rows, cols), bf16)] * 2 if split else [jax.ShapeDtypeStruct((2, rows, cols), bf16)],
        in_specs=[block] * len(parts),
        out_specs=[half] * 2 if split else [block],
        cost_estimate=cheap(),
        name="halve",
    )(*parts)
    if not split:
        return outs[0]
    if rows == tile:
        return outs
    return [v.reshape(2, rows // 2, cols) for v in outs]


def plain_sum(pairs):
    grads = []
    for left, left_far, right, right_far in pairs:
        both = jnp.concatenate([right, right_far], -2)
        if both.ndim == 3:
            both = jnp.concatenate([both[0], both[1]], 1)
        both = dot(jnp.concatenate([left, left_far], 0), both, 0, 0)
        grads.append(both.astype(bf16).reshape(both.shape[0], 2, -1))
    grads = jnp.concatenate(grads, 2)
    mine = add(grads[:, 0], swap(grads[:, 1], "tp"))
    return [lax.psum_scatter(mine, "dp", scatter_dimension=0, tiled=True)]


def close_kernel(place, *refs):
    parts, (mine, send) = refs[:-2], refs[-2:]
    total = parts[0][...].astype(f32)
    for part in parts[1:]:
        total += part[...].astype(f32)
    rows = mine.shape[0]
    for core in range(2):

        @pl.when(place[2] == core)
        def _(core=core):
            mine[...] = total[core * rows : (core + 1) * rows]
            send[...] = total[(1 - core) * rows : (2 - core) * rows]


def close(place, parts):
    rows, cols = parts[0].shape
    return pl.pallas_call(
        close_kernel,
        out_shape=[jax.ShapeDtypeStruct((rows // 2, cols), f32)] * 2,
        in_specs=[pl.BlockSpec(memory_space=pltpu.SMEM)] + [pl.BlockSpec(memory_space=pltpu.VMEM)] * len(parts),
        out_specs=[pl.BlockSpec(memory_space=pltpu.VMEM)] * 2,
        cost_estimate=cheap(),
        name="close",
    )(place, *parts)


def settle_kernel(place, mine, other, *outs):
    size = mine.shape[1] // len(outs)
    for core in range(2):

        @pl.when(place[2] == core)
        def _(core=core):
            for n, out in enumerate(outs):
                for part, at in ((mine, core), (other, 1 - core)):
                    out[:, at * size : (at + 1) * size] = part[:, n * size : (n + 1) * size]


def settle_columns(place, pair, count):
    mine, send = pair
    other = swap(send, "ctx")
    rows, cols = mine.shape
    return pl.pallas_call(
        settle_kernel,
        out_shape=[jax.ShapeDtypeStruct((rows, 2 * cols // count), f32)] * count,
        in_specs=[pl.BlockSpec(memory_space=pltpu.SMEM)] + [pl.BlockSpec(memory_space=pltpu.VMEM)] * 2,
        out_specs=[pl.BlockSpec(memory_space=pltpu.VMEM)] * count,
        cost_estimate=cheap(),
        name="settle_columns",
    )(place, mine, other)


def body(dp_count, tokens, segments, query_weight, key_weight, value_weight, out_weight, up_weight, down_weight, query_bias, value_bias, out_bias, up_bias, down_bias, attn_gain, attn_shift, mlp_gain, mlp_shift, cotangent):
    c = lax.axis_index("ctx")
    t = lax.axis_index("tp")
    d = lax.axis_index("dp")
    place = jnp.stack([d // 2, d % 2, c, t]).astype(jnp.int32)
    half, width = tokens.shape[1], tokens.shape[2]
    rows = 2 * half
    inner = 2 * query_bias.shape[0]
    ff = 2 * up_bias.shape[0]
    piece_rows = query_weight.shape[0]

    one = jnp.stack([query_weight, key_weight, value_weight, out_weight.T], 1)
    one = one.reshape(piece_rows, 4, 2, -1).transpose(2, 0, 1, 3).reshape(2, piece_rows, -1)
    one = one.astype(bf16)
    piece = order(c, take(one, c), swap(take(one, 1 - c), "ctx"), 0)
    unit = piece.shape[1]
    quarter = unit // 4
    qkv_mine, out_mine = gather_weights(piece, ((0, 3 * quarter), (3 * quarter, quarter)), place, dp_count)
    w_qkv = (qkv_mine, swap(qkv_mine, "ctx"))
    w_out = (out_mine, swap(out_mine, "ctx"))
    rest = jnp.stack([up_weight.astype(bf16), down_weight.T.astype(bf16)])
    rest = lax.all_gather(rest, ("tp", "dp", "ctx"), axis=1, tiled=True)

    biases = jnp.concatenate([query_bias, value_bias, up_bias])
    biases = jnp.stack([biases, swap(biases, "tp")])
    hin = inner // 2

    def near(values):
        values = values.reshape(2, 2, -1).transpose(1, 0, 2)
        return jnp.where(c == 0, values, values[::-1])

    bias_q, bias_v = near(biases[:, :hin]), near(biases[:, hin : 2 * hin])
    bias_up = jnp.where(t == 0, biases[:, 2 * hin :], biases[::-1, 2 * hin :])
    bias_qkv = jnp.stack([bias_q, jnp.zeros_like(bias_q), bias_v], 2).reshape(2, -1)

    seq = 2 * t + c
    other_seq = 2 * t + 1 - c
    pair_mine = jnp.stack([take(tokens, seq), take(cotangent, seq), take(tokens, other_seq)])
    pair_send = jnp.stack([take(tokens, other_seq), take(cotangent, other_seq), take(tokens, seq)])
    got = swap(pair_send, "ctx")
    flat = order(c, pair_mine[0], got[0], 0)
    flat_far = order(c, pair_mine[2], got[2], 0)
    grad_output = order(c, pair_mine[1], got[1], 0)
    flat = tie(flat, flat_far, grad_output)
    seg = take(segments, seq)

    def far(values):
        return swap(values, "ctx")

    qkv = [(dot(flat, w_qkv[r], 1, 0) + bias_qkv[r]).astype(bf16) for r in range(2)]
    attended = [attend(qkv[r], seg) for r in range(2)]
    context = [a[0] for a in attended]
    probs = [a[1] for a in attended]
    resid_one = flat.astype(f32) + dot(context[0], w_out[0], 1, 1) + dot(context[1], w_out[1], 1, 1) + out_bias
    normed_one, unit_one, inverse_one = norm_forward(resid_one, attn_gain, attn_shift)
    normed_low = normed_one.astype(bf16)
    normed_far, context_far = far(normed_low), far(context[1])
    normed_low = tie(normed_low, normed_far, context_far)
    hidden_near, hidden_far, output, grad_two, grad_mixed, pre_near, pre_far, sums_two, sums_pre = mlp(
        place, normed_low, rest, bias_up, normed_one, grad_output, down_bias, mlp_gain, mlp_shift
    )
    hidden_far, pre_got, grad_mixed_far = far(hidden_far), far(pre_far), far(grad_mixed)

    layer_all = lax.all_gather(output, ("tp", "ctx"), axis=0, tiled=False)
    grad_one, grad_attended, *grad_context, sums_one = mlp_back(
        place, pre_near, pre_far, rest, grad_two, unit_one, inverse_one, attn_gain, *w_out, ()
    )
    quick = dp_count == 8
    down_pairs = [(tie(grad_mixed, grad_attended), grad_mixed_far, hidden_near, hidden_far)]
    up_pairs = [(normed_low, normed_far, pre_near, pre_got)]
    if quick:
        down_keep, down_send = weight_grad(place, down_pairs, "x")
        up_keep, up_send = weight_grad(place, up_pairs, "tp")
        sent = (down_send, up_send)
    else:
        down_last, up_last, sent = plain_sum(down_pairs), plain_sum(up_pairs), ()
    back = [attend_back(qkv[r], probs[r], grad_context[r], sent) for r in range(2)]
    grad_qkv = [b[0] for b in back]
    sums = jnp.stack([b[1] for b in back])[:, :, :, 0]
    grad_qkv_far = far(grad_qkv[1])
    attended_far = far(grad_attended)
    one_pairs = [(flat, flat_far, grad_qkv[0], grad_qkv_far), (grad_attended, attended_far, context[0], context_far)]
    if quick:
        one_keep, one_send, two_keep, two_send = weight_grad(place, one_pairs, "one")
        down_keep, down_send = halve(tie(down_keep, one_send), over("x", down_send))
        one_got, two_got = over("t", one_send), over("x", two_send)
        up_keep, up_send = halve(tie(up_keep, two_got), over("t", up_send))
        up_got = over("x", up_send)
        down_got = over("l", down_send)
    else:
        one_last = plain_sum(one_pairs)
    if quick:
        grad_qkv = [tie(g, down_send) for g in grad_qkv]
    sent_back = dot(grad_qkv[0], w_qkv[0], 1, 1) + dot(grad_qkv[1], w_qkv[1], 1, 1)
    input_grad = (grad_one + sent_back).astype(bf16).reshape(2, half, width)
    got = swap(take(input_grad, 1 - c), "ctx")
    input_grad = order(c, take(input_grad, c)[None], got[None], 0)
    if quick:
        small_after = down_send
        two_keep, two_send = halve(tie(two_keep, down_got), two_got)
        one_keep, one_send = halve(one_keep, one_got)
        two_got, one_got = over("t", two_send), over("x", one_send)
        down_keep, down_send = halve(down_keep, down_got)
        down_got = over("h", down_send)
        low_got = over("l", halve(tie(two_keep, up_got), two_got, split=False))
        up_keep, up_send = halve(up_keep, up_got)
        up_got = over("l", up_send)
        down_keep, down_send = halve(down_keep, down_got)
        one_keep, one_send = halve(tie(one_keep, up_got), one_got, low_got)
        up_keep, up_send = halve(up_keep, up_got)
        up_last = (up_keep, over("h", up_send))
        down_last = (down_keep, over("t", down_send))
        one_last = (one_keep, over("h", one_send))
        sums_one, sums_two, sums_pre = (tie(v, small_after) for v in (sums_one, sums_two, sums_pre))
    input_grad = order(t, input_grad, swap(input_grad, "tp"), 0)
    sums_one, sums_two = jnp.sum(sums_one, 1), jnp.sum(sums_two, 1)

    def settle(values):
        values = jnp.where(c == 0, values, values[::-1])
        values = jnp.where(t == 0, values, values[:, ::-1])
        return values.transpose(1, 0, 2).reshape(-1)

    small = jnp.concatenate(
        [settle(sums[:, :, 0]), settle(sums[:, :, 1]), settle(jnp.sum(sums_pre, 1).reshape(2, 2, -1)), sums_one[2], sums_two[2], sums_one[0], sums_one[1], sums_two[0], sums_two[1]]
    )
    small = tie(small.reshape(-1, 128), layer_all)
    small = lax.all_gather(small, ("dp", "ctx", "tp"), axis=0, tiled=False)
    small = jnp.sum(small, axis=0).reshape(-1)

    def cut_tp(start, size):
        return lax.dynamic_slice_in_dim(small, start + t * (size // 2), size // 2)

    at = 2 * inner + ff
    vectors = [lax.slice_in_dim(small, at + i * width, at + (i + 1) * width) for i in range(6)]

    if quick:
        layer_all = tie(layer_all, down_last[0])
    layer_out = lax.dynamic_slice_in_dim(layer_all, c * half, half, 1)
    if quick:
        one_last = (tie(one_last[0], input_grad, small), one_last[1])
    (down_shard,) = settle_columns(place, close(place, down_last), 1)
    (up_shard,) = settle_columns(place, close(place, up_last), 1)
    one_shard = settle_columns(place, close(place, one_last), 4)
    return (
        layer_out,
        input_grad,
        *one_shard[:3],
        one_shard[3].T,
        up_shard,
        down_shard.T,
        cut_tp(0, inner),
        cut_tp(inner, inner),
        vectors[0],
        cut_tp(2 * inner, ff),
        *vectors[1:],
    )


def solution(mesh):
    weight_in, weight_out = P(("dp", "ctx"), "tp"), P("tp", ("dp", "ctx"))
    rows = P("dp", "ctx", None)
    weights = (weight_in, weight_in, weight_in, weight_out, weight_in, weight_out)
    vectors = (P("tp"), P("tp"), P(), P("tp"), P(), P(), P(), P(), P())
    dp_count = mesh.shape["dp"]

    def run(*args):
        return body(dp_count, *args)

    return jax.shard_map(
        run,
        mesh=mesh,
        in_specs=(rows, P("dp", None), *weights, *vectors, rows),
        out_specs=(rows, rows, *weights, *vectors),
        check_vma=False,
    )
```

```python
import functools

import jax
import jax.numpy as jnp
from jax import lax
from jax.experimental import pallas as pl
from jax.experimental.pallas import tpu as pltpu
from jax.sharding import PartitionSpec as P

HEAD_DIM = 64
LANES = 2 * HEAD_DIM

epsilon = 1e-12
root_half = 0.7071067811865476
inv_root_two_pi = 0.3989422804014327
bf16 = jnp.bfloat16
f32 = jnp.float32


def dot(left, right, left_dim, right_dim):
    return lax.dot_general(left, right, (((left_dim,), (right_dim,)), ((), ())), preferred_element_type=f32)


def norm_forward(values, gain, shift):
    centre = values - jnp.mean(values, axis=-1, keepdims=True)
    inverse = lax.rsqrt(jnp.mean(centre * centre, axis=-1, keepdims=True) + epsilon)
    normed = centre * inverse
    return (normed * gain + shift, normed, inverse)


def swap(values, axis):
    return lax.ppermute(values, axis, [(0, 1), (1, 0)])


def swap_x(values):
    return lax.ppermute(values, "dp", [(i, i ^ 1) for i in range(8)])


def shift_z(values, step):
    return lax.ppermute(values, "dp", [(i, (i + 2 * step) % 8) for i in range(8)])


def take(values, index, axis=0):
    return lax.dynamic_index_in_dim(values, index, axis, keepdims=False)


def add(left, right):
    return (left.astype(f32) + right.astype(f32)).astype(bf16)


def order(index, mine, other, axis):
    return jnp.where(index == 0, jnp.concatenate([mine, other], axis), jnp.concatenate([other, mine], axis))


def assemble_kernel(cuts, place, one, one_y, two, two_x, *rest):
    outs, sems = rest[: len(cuts)], rest[len(cuts)]
    z, x = place[0], place[1]
    rows = one.shape[2]
    copies = []
    for k in range(4):
        for far_x in range(2):
            block = lax.rem(z + 4 - k, 4) * 2 + lax.rem(x + far_x, 2)
            at = pl.ds(pl.multiple_of(block * rows, rows), rows)
            for far_t in range(2):
                if k < 2:
                    source = (one_y if far_t else one).at[far_x, k]
                else:
                    source = (two_x if far_x else two).at[far_t, k - 2]
                for n, (start, size) in enumerate(cuts):
                    copies.append(
                        pltpu.make_async_copy(
                            source.at[:, start : start + size],
                            outs[n].at[at, far_t * size : far_t * size + size],
                            sems.at[len(copies)],
                        )
                    )
                    copies[-1].start()
    for copy in copies:
        copy.wait()


def gather_weights(piece, cuts, place, dp_count):
    rows, cols = piece.shape
    total = dp_count * rows
    if dp_count != 8:
        t = lax.axis_index("tp")
        both = lax.all_gather(piece, ("tp", "dp"), axis=0, tiled=True).reshape(2, total, cols)
        first, second = take(both, t), take(both, 1 - t)
        return [
            jnp.concatenate([first[:, s : s + n], second[:, s : s + n]], 1) for s, n in cuts
        ]
    line = [piece] + [shift_z(piece, k) for k in range(1, 4)]
    one, two = jnp.stack(line[:2]), jnp.stack(line[2:])
    one_x, two_y = swap_x(one), swap(two, "tp")
    one, two = jnp.stack([one, one_x]), jnp.stack([two, two_y])
    one_y, two_x = swap(one, "tp"), swap_x(two)
    anyspace = pl.BlockSpec(memory_space=pl.ANY)


    return pl.pallas_call(
        functools.partial(assemble_kernel, cuts),
        out_shape=[jax.ShapeDtypeStruct((total, 2 * n), bf16) for _, n in cuts],
        in_specs=[pl.BlockSpec(memory_space=pltpu.SMEM)] + [anyspace] * 4,
        out_specs=[pl.BlockSpec(memory_space=pltpu.VMEM)] * len(cuts),
        scratch_shapes=[pltpu.SemaphoreType.DMA((16 * len(cuts),))],
        compiler_params=pltpu.CompilerParams(vmem_limit_bytes=24 << 20),
        name="assemble",
    )(place, one, one_y, two, two_x)


def tie_kernel(*refs):
    pass


def tie(value, *after):
    anyspace = pl.BlockSpec(memory_space=pl.ANY)
    return pl.pallas_call(
        tie_kernel,
        out_shape=jax.ShapeDtypeStruct(value.shape, value.dtype),
        in_specs=[anyspace] * (1 + len(after)),
        out_specs=anyspace,
        input_output_aliases={0: 0},
        name="tie",
    )(value, *after)


def attend_kernel(qkv, seg_keys, seg_queries, context, probs, bias):
    quarter = qkv.shape[1] // 3

    @pl.when(pl.program_id(0) == 0)
    def _():
        bias[...] = jnp.where(seg_keys[...] == seg_queries[...], 0.0, -1000000000.0)

    low = lax.broadcasted_iota(jnp.int32, (1, LANES), 1) < HEAD_DIM
    for pair in range(quarter // LANES):
        cols = slice(pair * LANES, pair * LANES + LANES)
        query = qkv[:, cols] * 0.125
        key = qkv[:, quarter + pair * LANES : quarter + pair * LANES + LANES]
        value_t = qkv[:, 2 * quarter + pair * LANES : 2 * quarter + pair * LANES + LANES].T
        parts = []
        for h in range(2):
            mine = jnp.where(low if h == 0 else ~low, query, jnp.zeros_like(query))
            scores = dot(key, mine, 1, 1) + bias[...]
            raised = jnp.exp(scores - jnp.max(scores, axis=0, keepdims=True))
            prob = (raised * (1.0 / jnp.sum(raised, axis=0, keepdims=True))).astype(bf16)
            probs[2 * pair + h] = prob
            parts.append(dot(value_t[h * HEAD_DIM : (h + 1) * HEAD_DIM], prob, 1, 0))
        context[:, cols] = jnp.concatenate(parts, 0).T.astype(bf16)


def attend(qkv, seg):
    rows, cols = qkv.shape
    half = cols // 2
    quarter = half // 3
    heads = quarter // HEAD_DIM
    return pl.pallas_call(
        attend_kernel,
        grid=(2,),
        out_shape=[jax.ShapeDtypeStruct((rows, 2 * quarter), bf16), jax.ShapeDtypeStruct((2 * heads, rows, rows), bf16)],
        in_specs=[
            pl.BlockSpec((rows, half), lambda i: (0, i)),
            pl.BlockSpec((rows, 1), lambda i: (0, 0)),
            pl.BlockSpec((1, rows), lambda i: (0, 0)),
        ],
        out_specs=[pl.BlockSpec((rows, quarter), lambda i: (0, i)), pl.BlockSpec((heads, rows, rows), lambda i: (i, 0, 0))],
        scratch_shapes=[pltpu.VMEM((rows, rows), f32)],
        compiler_params=pltpu.CompilerParams(vmem_limit_bytes=48 << 20),
        cost_estimate=pl.CostEstimate(flops=1024, bytes_accessed=1024, transcendentals=0),
        name="attend",
    )(qkv, seg.reshape(rows, 1), seg.reshape(1, rows))


def attend_back_kernel(qkv, probs, upstream, *rest):
    grads, sums = rest[-2:]
    quarter = qkv.shape[1] // 3
    low = lax.broadcasted_iota(jnp.int32, (1, LANES), 1) < HEAD_DIM
    for pair in range(quarter // LANES):
        cols = [slice(n * quarter + pair * LANES, n * quarter + pair * LANES + LANES) for n in range(3)]
        query, key, value = (qkv[:, c] for c in cols)
        key_t = key.T
        above = upstream[:, cols[0]]
        grad_q, grad_k, grad_v = [], [], []
        for h in range(2):
            mine = jnp.where(low if h == 0 else ~low, above, jnp.zeros_like(above))
            grad_p = dot(value, mine, 1, 1)
            prob_low = probs[2 * pair + h]
            prob = prob_low.astype(f32)
            weighted = prob * grad_p
            inner = jnp.sum(weighted, axis=0, keepdims=True)
            grad_s = (weighted - prob * inner).astype(bf16)
            grad_k.append(dot(grad_s, query, 1, 0))
            grad_v.append(dot(prob_low, above, 1, 0))
            grad_q.append(dot(key_t[h * HEAD_DIM : (h + 1) * HEAD_DIM], grad_s, 1, 0))
        out_q = (jnp.concatenate(grad_q, 0) * 0.125).T.astype(bf16)
        out_v = jnp.where(low, grad_v[0], grad_v[1]).astype(bf16)
        grads[:, cols[0]] = out_q
        grads[:, cols[1]] = (jnp.where(low, grad_k[0], grad_k[1]) * 0.125).astype(bf16)
        grads[:, cols[2]] = out_v
        for n, out in ((0, out_q), (1, out_v)):
            total = jnp.sum(out.astype(f32), axis=0, keepdims=True)
            sums[0, n, :, cols[0]] = jnp.broadcast_to(total, (8, LANES))


def attend_back(qkv, probs, upstream, after):
    rows, cols = qkv.shape
    half = cols // 2
    quarter = half // 3
    heads = quarter // HEAD_DIM
    return pl.pallas_call(
        attend_back_kernel,
        grid=(2,),
        out_shape=[jax.ShapeDtypeStruct((rows, cols), bf16), jax.ShapeDtypeStruct((2, 2, 8, quarter), f32)],
        in_specs=[
            pl.BlockSpec((rows, half), lambda i: (0, i)),
            pl.BlockSpec((heads, rows, rows), lambda i: (i, 0, 0)),
            pl.BlockSpec((rows, quarter), lambda i: (0, i)),
        ]
        + [pl.BlockSpec(memory_space=pl.ANY)] * len(after),
        out_specs=[pl.BlockSpec((rows, half), lambda i: (0, i)), pl.BlockSpec((1, 2, 8, quarter), lambda i: (i, 0, 0, 0))],
        compiler_params=pltpu.CompilerParams(vmem_limit_bytes=48 << 20),
        cost_estimate=pl.CostEstimate(flops=1024, bytes_accessed=1024, transcendentals=0),
        name="attend_back",
    )(qkv, probs, upstream, *after)


CHUNK = 128


def cheap():
    return pl.CostEstimate(flops=1024, bytes_accessed=1024, transcendentals=0)


def clamp(i, low, count):
    return jnp.clip(i - low, 0, count - 1)


def put(near, far, i, steps, value):
    @pl.when(i < steps)
    def _():
        near[0] = value

    @pl.when(i >= steps)
    def _():
        far[0] = value


def halves_of(group, width, unit):
    core = lambda i, p: lax.rem(p[2] + i // 4, 2)
    return pl.BlockSpec((1, width, unit // 2), lambda i, p: (group, (i // 2) % 2, core(i, p) * 2 + i % 2))


def blocks_of(group, width, unit):
    return pl.BlockSpec((1, width, unit), lambda i, p: (group, lax.rem(p[3] + i % 2, 2), lax.rem(p[2] + i // 2, 2)))


def half_outs(rows, unit):
    return [pl.BlockSpec((1, rows, unit // 2), lambda i, p, n=n: (clamp(i, n, 4) // 2, 0, clamp(i, n, 4) % 2)) for n in (0, 4)]


def block_ins(rows, unit):
    return [pl.BlockSpec((1, rows, unit), lambda i, p, n=n: (clamp(i, n, 2), 0, 0)) for n in (0, 2)]


def fixed(*shape):
    return pl.BlockSpec(shape, lambda i, p: (0,) * len(shape))


def call(kernel, place, grid, ins, in_specs, outs, out_specs, scratch, name):
    return pl.pallas_call(
        kernel,
        grid_spec=pltpu.PrefetchScalarGridSpec(num_scalar_prefetch=1, grid=(grid,), in_specs=in_specs, out_specs=out_specs, scratch_shapes=scratch),
        out_shape=[jax.ShapeDtypeStruct(*o) for o in outs],
        compiler_params=pltpu.CompilerParams(vmem_limit_bytes=48 << 20),
        cost_estimate=cheap(),
        name=name,
    )(place, *ins)


def mean(values):
    return jnp.sum(values, axis=-1, keepdims=True) * (1.0 / values.shape[-1])


def fold(values):
    return jnp.sum(values.reshape(-1, 8, values.shape[-1]), axis=0)


def mlp_kernel(place, low, up_weight, down_weight, up_bias, normed, above, bias, gain, shift, near, far, out, grad, grad_low, pre_near, pre_far, sums, up_sums, units, slope, down, total):
    i = pl.program_id(0)
    rows, width = low.shape
    cols = up_weight.shape[2]
    tile = cols // 4

    def up(out_ref):
        for n in range(4):
            at = slice(n * tile, n * tile + tile)
            pre = dot(low[...], up_weight[0, :, at], 1, 0) + up_bias[0, :, at]
            half = 0.5 * (1.0 + lax.erf(pre * root_half))
            value = (pre * half).astype(bf16)
            out_ref[0, :, at] = value
            units[i, :, at] = value
            slope[i, :, at] = (half + pre * jnp.exp(-0.5 * pre * pre) * inv_root_two_pi).astype(bf16)

    pl.when(i < 2)(lambda: up(near))
    pl.when(jnp.logical_and(i >= 2, i < 4))(lambda: up(far))

    @pl.when(i == 4)
    def _():
        total[...] = normed[...] + bias[...]

    @pl.when(jnp.logical_and(i >= 4, i < 8))
    def _():
        down[i - 4] = down_weight[0]
        total[...] += dot(units[i - 4], down_weight[0], 1, 1)

    @pl.when(i == 7)
    def _():
        def step(k, carry):
            at = pl.ds(pl.multiple_of(k * CHUNK, CHUNK), CHUNK)
            centre = total[at] - mean(total[at])
            inverse = lax.rsqrt(mean(centre * centre) + epsilon)
            unit = centre * inverse
            out[at] = (unit * gain[...] + shift[...]).astype(bf16)
            upper = above[at].astype(f32)
            scaled = upper * gain[...]
            lower = inverse * (scaled - mean(scaled) - unit * mean(scaled * unit))
            grad[at] = lower
            grad_low[at] = lower.astype(bf16)
            return tuple(c + fold(v) for c, v in zip(carry, (upper * unit, upper, lower)))

        zero = jnp.zeros((8, width), f32)
        done = lax.fori_loop(0, rows // CHUNK, step, (zero,) * 3)
        for n in range(3):
            sums[n] = done[n]

    def pre(out_ref):
        for n in range(4):
            at = slice(n * tile, n * tile + tile)
            value = (dot(grad_low[...], down[i - 8, :, at], 1, 0) * slope[i - 8, :, at].astype(f32)).astype(bf16)
            out_ref[0, :, at] = value
            up_sums[0, :, at] = fold(value.astype(f32))

    pl.when(jnp.logical_and(i >= 8, i < 10))(lambda: pre(pre_near))
    pl.when(i >= 10)(lambda: pre(pre_far))


def mlp(place, low, weights, up_bias, normed, above, bias, gain, shift):
    rows, width = low.shape
    unit = weights.shape[2] // 2

    def still(*shape):
        return pl.BlockSpec(shape, lambda i, p: (0,) * len(shape), pipeline_mode=pl.Buffered(1))

    def block(group, first):
        def index(i, p):
            j = clamp(i, first, 4)
            return (group, lax.rem(p[3] + j % 2, 2), lax.rem(p[2] + j // 2, 2))

        return pl.BlockSpec((1, width, unit), index)

    def outs(first):
        return [pl.BlockSpec((1, rows, unit), lambda i, p, n=n: (clamp(i, n, 2), 0, 0)) for n in (first, first + 2)]

    def bias_index(i, p):
        j = clamp(i, 0, 4)
        return (lax.rem(p[3] + j % 2, 2) * 2 + lax.rem(p[2] + j // 2, 2), 0, 0)

    one, vector = still(rows, width), still(1, width)
    return pl.pallas_call(
        mlp_kernel,
        grid_spec=pltpu.PrefetchScalarGridSpec(
            num_scalar_prefetch=1,
            grid=(12,),
            in_specs=[one, block(0, 0), block(1, 4), pl.BlockSpec((1, 1, unit), bias_index), one, one, vector, vector, vector],
            out_specs=outs(0) + [one, one, one] + outs(8) + [still(3, 8, width), pl.BlockSpec((1, 8, unit), lambda i, p: (clamp(i, 8, 4), 0, 0))],
            scratch_shapes=[pltpu.VMEM((4, rows, unit), bf16)] * 2 + [pltpu.VMEM((4, width, unit), bf16), pltpu.VMEM((rows, width), f32)],
        ),
        out_shape=[jax.ShapeDtypeStruct(*o) for o in (
            [((2, rows, unit), bf16)] * 2
            + [((rows, width), bf16), ((rows, width), f32), ((rows, width), bf16)]
            + [((2, rows, unit), bf16)] * 2
            + [((3, 8, width), f32), ((4, 8, unit), f32)]
        )],
        compiler_params=pltpu.CompilerParams(vmem_limit_bytes=60 << 20),
        cost_estimate=cheap(),
        name="mlp",
    )(place, low, weights, weights, up_bias.reshape(4, 1, unit), normed, above, bias[None], gain[None], shift[None])


def mlp_back_kernel(place, near, far, weight, grad_two, unit_one, inverse, gain, out_near, out_far, grad, grad_low, near_context, far_context, sums, total):
    i = pl.program_id(0)

    @pl.when(i == 0)
    def _():
        total[...] = grad_two[...] + dot(near[0], weight[0], 1, 1)

    @pl.when(i == 1)
    def _():
        total[...] += dot(near[0], weight[0], 1, 1)

    @pl.when(i >= 2)
    def _():
        total[...] += dot(far[0], weight[0], 1, 1)

    @pl.when(i == 3)
    def _():
        def step(k, carry):
            at = pl.ds(pl.multiple_of(k * CHUNK, CHUNK), CHUNK)
            upper = total[at]
            unit = unit_one[at]
            scaled = upper * gain[...]
            down = inverse[at] * (scaled - mean(scaled) - unit * mean(scaled * unit))
            grad[at] = down
            grad_low[at] = down.astype(bf16)
            return tuple(c + fold(v) for c, v in zip(carry, (upper * unit, upper, down)))

        zero = jnp.zeros((8, grad.shape[1]), f32)
        done = lax.fori_loop(0, grad.shape[0] // CHUNK, step, (zero,) * 3)
        for n in range(3):
            sums[n] = done[n]
        near_context[...] = dot(grad_low[...], out_near[...], 1, 0).astype(bf16)
        far_context[...] = dot(grad_low[...], out_far[...], 1, 0).astype(bf16)


def mlp_back(place, near, far, weights, grad_two, unit_one, inverse, gain, out_near, out_far, after):
    rows, width = grad_two.shape
    unit = weights.shape[2] // 2
    part = out_near.shape[1]
    one = fixed(rows, width)

    def kernel(*refs):
        mlp_back_kernel(*refs[:10], *refs[10 + len(after) :])

    return call(
        kernel,
        place,
        4,
        (near, far, weights, grad_two, unit_one, inverse, gain[None], out_near, out_far, *after),
        block_ins(rows, unit) + [blocks_of(0, width, unit), one, one, fixed(rows, 1), fixed(1, width)] + [fixed(width, part)] * 2 + [pl.BlockSpec(memory_space=pl.ANY)] * len(after),
        [((rows, width), f32), ((rows, width), bf16)] + [((rows, part), bf16)] * 2 + [((3, 8, width), f32)],
        [one, one] + [fixed(rows, part)] * 2 + [fixed(3, 8, width)],
        [pltpu.VMEM((rows, width), f32)],
        "mlp_back",
    )


def over(axis, values):
    if axis == "t":
        return swap(values, "tp")
    if axis == "x":
        return swap_x(values)
    flip = 2 if axis == "l" else 4
    return lax.ppermute(values, "dp", [(i, i ^ flip) for i in range(8)])


def grad_kernel(kind, place, *refs):
    lefts = 2 if kind == "one" else 1
    sources = refs[: 2 * lefts]
    rights = refs[2 * lefts : 4 * lefts]
    outs = refs[4 * lefts : -lefts]
    turned = refs[-lefts:]
    i = pl.program_id(0)
    z, x = place[0], place[1]
    rows, width = sources[0].shape
    piece = width // 8

    @pl.when(i == 0)
    def _():
        for at in range(8):
            a, b, c = at // 4, (at // 2) % 2, at % 2
            far_x, low, high = (b, a, c) if kind == "one" else (a, b, c)
            block = (2 * lax.rem(z // 2 + high, 2) + lax.rem(z + low, 2)) * 2 + lax.rem(x + far_x, 2)
            cols = pl.ds(pl.multiple_of(block * piece, piece), piece)
            for n in range(lefts):
                for far in range(2):
                    turned[n][at * piece : (at + 1) * piece, far * rows : (far + 1) * rows] = sources[2 * n + far][:, cols].T

    def work(n):
        near, away = rights[2 * n], rights[2 * n + 1]
        pick = (lambda r: r[...]) if kind == "one" else (lambda r: r[0])
        out = dot(turned[n][...], jnp.concatenate([pick(near), pick(away)], 0), 1, 0).astype(bf16)
        if kind == "tp":
            out = out.reshape(2, 4 * piece, out.shape[1])
            pl.when(i < 2)(lambda: outs[0].__setitem__(..., out))
            pl.when(i >= 2)(lambda: outs[1].__setitem__(..., out))
        elif kind == "x":
            out = out.reshape(2, 2, 2, piece, out.shape[1])
            outs[0][:, :, 0] = out[0]
            outs[1][:, :, 0] = out[1]
        else:
            out = out.reshape(2, 2, 2 * piece, out.shape[1])
            pl.when(i < 4)(lambda: outs[0].__setitem__(..., out[0]))
            pl.when(i >= 4)(lambda: outs[1].__setitem__(..., out[0]))
            outs[2][0] = out[1, 0]
            outs[3][0] = out[1, 1]

    if lefts == 1:
        work(0)
    else:
        last = lax.rem(i, 4) == 3
        pl.when(jnp.logical_not(last))(lambda: work(0))
        pl.when(last)(lambda: work(1))


def weight_grad(place, pairs, kind):
    rows, width = pairs[0][0].shape
    piece = width // 8
    whole = pl.BlockSpec((rows, width), lambda i, p: (0, 0))
    tile = 256 if kind == "one" else 512
    steps = 1024 // tile
    first = lambda i: jnp.minimum(i, steps - 1)
    second = lambda i: jnp.maximum(i, steps) - steps
    if kind == "one":
        maps = [lambda i, p: (0, (i // 4) * 3 + jnp.minimum(i % 4, 2)), lambda i, p: (0, i // 4)]
        right_specs = [pl.BlockSpec((rows, 256), m) for m in maps for _ in range(2)]
        shapes = [(2, 2 * piece, 1024)] * 4
        out_specs = [
            pl.BlockSpec((2, 2 * piece, 256), lambda i, p: (0, 0, first(i))),
            pl.BlockSpec((2, 2 * piece, 256), lambda i, p: (0, 0, second(i))),
        ] + [pl.BlockSpec((1, 2 * piece, 256), lambda i, p: (i // 4, 0, i % 4))] * 2
    else:
        right_specs = [pl.BlockSpec((1, rows, tile), lambda i, p: (i // steps, 0, i % steps))] * 2
        if kind == "tp":
            shapes = [(2, 4 * piece, 1024)] * 2
            out_specs = [
                pl.BlockSpec((2, 4 * piece, tile), lambda i, p: (0, 0, first(i))),
                pl.BlockSpec((2, 4 * piece, tile), lambda i, p: (0, 0, second(i))),
            ]
        else:
            shapes = [(2, 2, 2, piece, 1024)] * 2
            out_specs = [pl.BlockSpec((2, 2, 1, piece, tile), lambda i, p: (0, 0, i // steps, 0, i % steps))] * 2
    lefts = [v for p in pairs for v in p[:2]]
    rights = [v for p in pairs for v in p[2:]]
    outs = pl.pallas_call(
        functools.partial(grad_kernel, kind),
        grid_spec=pltpu.PrefetchScalarGridSpec(
            num_scalar_prefetch=1,
            grid=(2 * steps,),
            in_specs=[whole] * len(lefts) + right_specs,
            out_specs=out_specs,
            scratch_shapes=[pltpu.VMEM((width, 2 * rows), bf16)] * len(pairs),
        ),
        out_shape=[jax.ShapeDtypeStruct(shape, bf16) for shape in shapes],
        compiler_params=pltpu.CompilerParams(vmem_limit_bytes=(60 if kind == "one" else 40) << 20),
        cost_estimate=cheap(),
        name="weight_grad_" + kind,
    )(place, *lefts, *rights)
    return [v.reshape(2, -1, 1024) for v in outs]


def halve_kernel(count, *refs):
    total = refs[0][...].astype(f32)
    for part in refs[1:count]:
        total += part[...].astype(f32)
    total = total.astype(bf16)
    if len(refs) == count + 1:
        refs[count][...] = total
    else:
        refs[count][...] = total[0]
        refs[count + 1][...] = total[1]


def halve(*parts, split=True):
    _, rows, cols = parts[0].shape
    tile = min(rows, 128)
    block = pl.BlockSpec((2, tile, cols), lambda i: (0, i, 0))
    half = pl.BlockSpec((tile, cols), lambda i: (i, 0))
    outs = pl.pallas_call(
        functools.partial(halve_kernel, len(parts)),
        grid=(rows // tile,),
        out_shape=[jax.ShapeDtypeStruct((rows, cols), bf16)] * 2 if split else [jax.ShapeDtypeStruct((2, rows, cols), bf16)],
        in_specs=[block] * len(parts),
        out_specs=[half] * 2 if split else [block],
        cost_estimate=cheap(),
        name="halve",
    )(*parts)
    if not split:
        return outs[0]
    if rows == tile:
        return outs
    return [v.reshape(2, rows // 2, cols) for v in outs]


def plain_sum(pairs):
    grads = []
    for left, left_far, right, right_far in pairs:
        both = jnp.concatenate([right, right_far], -2)
        if both.ndim == 3:
            both = jnp.concatenate([both[0], both[1]], 1)
        both = dot(jnp.concatenate([left, left_far], 0), both, 0, 0)
        grads.append(both.astype(bf16).reshape(both.shape[0], 2, -1))
    grads = jnp.concatenate(grads, 2)
    mine = add(grads[:, 0], swap(grads[:, 1], "tp"))
    return [lax.psum_scatter(mine, "dp", scatter_dimension=0, tiled=True)]


def close_kernel(place, *refs):
    parts, (mine, send) = refs[:-2], refs[-2:]
    total = parts[0][...].astype(f32)
    for part in parts[1:]:
        total += part[...].astype(f32)
    rows = mine.shape[0]
    for core in range(2):

        @pl.when(place[2] == core)
        def _(core=core):
            mine[...] = total[core * rows : (core + 1) * rows]
            send[...] = total[(1 - core) * rows : (2 - core) * rows]


def close(place, parts):
    rows, cols = parts[0].shape
    return pl.pallas_call(
        close_kernel,
        out_shape=[jax.ShapeDtypeStruct((rows // 2, cols), f32)] * 2,
        in_specs=[pl.BlockSpec(memory_space=pltpu.SMEM)] + [pl.BlockSpec(memory_space=pltpu.VMEM)] * len(parts),
        out_specs=[pl.BlockSpec(memory_space=pltpu.VMEM)] * 2,
        cost_estimate=cheap(),
        name="close",
    )(place, *parts)


def settle_kernel(place, mine, other, *outs):
    size = mine.shape[1] // len(outs)
    for core in range(2):

        @pl.when(place[2] == core)
        def _(core=core):
            for n, out in enumerate(outs):
                for part, at in ((mine, core), (other, 1 - core)):
                    out[:, at * size : (at + 1) * size] = part[:, n * size : (n + 1) * size]


def settle_columns(place, pair, count):
    mine, send = pair
    other = swap(send, "ctx")
    rows, cols = mine.shape
    return pl.pallas_call(
        settle_kernel,
        out_shape=[jax.ShapeDtypeStruct((rows, 2 * cols // count), f32)] * count,
        in_specs=[pl.BlockSpec(memory_space=pltpu.SMEM)] + [pl.BlockSpec(memory_space=pltpu.VMEM)] * 2,
        out_specs=[pl.BlockSpec(memory_space=pltpu.VMEM)] * count,
        cost_estimate=cheap(),
        name="settle_columns",
    )(place, mine, other)


def body(dp_count, tokens, segments, query_weight, key_weight, value_weight, out_weight, up_weight, down_weight, query_bias, value_bias, out_bias, up_bias, down_bias, attn_gain, attn_shift, mlp_gain, mlp_shift, cotangent):
    c = lax.axis_index("ctx")
    t = lax.axis_index("tp")
    d = lax.axis_index("dp")
    place = jnp.stack([d // 2, d % 2, c, t]).astype(jnp.int32)
    half, width = tokens.shape[1], tokens.shape[2]
    rows = 2 * half
    inner = 2 * query_bias.shape[0]
    ff = 2 * up_bias.shape[0]
    piece_rows = query_weight.shape[0]

    one = jnp.stack([query_weight, key_weight, value_weight, out_weight.T], 1)
    one = one.reshape(piece_rows, 4, 2, -1).transpose(2, 0, 1, 3).reshape(2, piece_rows, -1)
    one = one.astype(bf16)
    piece = order(c, take(one, c), swap(take(one, 1 - c), "ctx"), 0)
    unit = piece.shape[1]
    quarter = unit // 4
    qkv_mine, out_mine = gather_weights(piece, ((0, 3 * quarter), (3 * quarter, quarter)), place, dp_count)
    w_qkv = (qkv_mine, swap(qkv_mine, "ctx"))
    w_out = (out_mine, swap(out_mine, "ctx"))
    rest = jnp.stack([up_weight.astype(bf16), down_weight.T.astype(bf16)])
    rest = lax.all_gather(rest, ("tp", "dp", "ctx"), axis=1, tiled=True)

    biases = jnp.concatenate([query_bias, value_bias, up_bias])
    biases = jnp.stack([biases, swap(biases, "tp")])
    hin = inner // 2

    def near(values):
        values = values.reshape(2, 2, -1).transpose(1, 0, 2)
        return jnp.where(c == 0, values, values[::-1])

    bias_q, bias_v = near(biases[:, :hin]), near(biases[:, hin : 2 * hin])
    bias_up = jnp.where(t == 0, biases[:, 2 * hin :], biases[::-1, 2 * hin :])
    bias_qkv = jnp.stack([bias_q, jnp.zeros_like(bias_q), bias_v], 2).reshape(2, -1)

    seq = 2 * t + c
    other_seq = 2 * t + 1 - c
    pair_mine = jnp.stack([take(tokens, seq), take(cotangent, seq), take(tokens, other_seq)])
    pair_send = jnp.stack([take(tokens, other_seq), take(cotangent, other_seq), take(tokens, seq)])
    got = swap(pair_send, "ctx")
    flat = order(c, pair_mine[0], got[0], 0)
    flat_far = order(c, pair_mine[2], got[2], 0)
    grad_output = order(c, pair_mine[1], got[1], 0)
    flat = tie(flat, flat_far, grad_output)
    seg = take(segments, seq)

    def far(values):
        return swap(values, "ctx")

    qkv = [(dot(flat, w_qkv[r], 1, 0) + bias_qkv[r]).astype(bf16) for r in range(2)]
    attended = [attend(qkv[r], seg) for r in range(2)]
    context = [a[0] for a in attended]
    probs = [a[1] for a in attended]
    resid_one = flat.astype(f32) + dot(context[0], w_out[0], 1, 1) + dot(context[1], w_out[1], 1, 1) + out_bias
    normed_one, unit_one, inverse_one = norm_forward(resid_one, attn_gain, attn_shift)
    normed_low = normed_one.astype(bf16)
    normed_far, context_far = far(normed_low), far(context[1])
    normed_low = tie(normed_low, normed_far, context_far)
    hidden_near, hidden_far, output, grad_two, grad_mixed, pre_near, pre_far, sums_two, sums_pre = mlp(
        place, normed_low, rest, bias_up, normed_one, grad_output, down_bias, mlp_gain, mlp_shift
    )
    hidden_far, pre_got, grad_mixed_far = far(hidden_far), far(pre_far), far(grad_mixed)

    layer_all = lax.all_gather(output, ("tp", "ctx"), axis=0, tiled=False)
    grad_one, grad_attended, *grad_context, sums_one = mlp_back(
        place, pre_near, pre_far, rest, grad_two, unit_one, inverse_one, attn_gain, *w_out, ()
    )
    quick = dp_count == 8
    down_pairs = [(tie(grad_mixed, grad_attended), grad_mixed_far, hidden_near, hidden_far)]
    up_pairs = [(normed_low, normed_far, pre_near, pre_got)]
    if quick:
        down_keep, down_send = weight_grad(place, down_pairs, "x")
        up_keep, up_send = weight_grad(place, up_pairs, "tp")
        sent = (down_send, up_send)
    else:
        down_last, up_last, sent = plain_sum(down_pairs), plain_sum(up_pairs), ()
    back = [attend_back(qkv[r], probs[r], grad_context[r], sent) for r in range(2)]
    grad_qkv = [b[0] for b in back]
    sums = jnp.stack([b[1] for b in back])[:, :, :, 0]
    grad_qkv_far = far(grad_qkv[1])
    attended_far = far(grad_attended)
    one_pairs = [(flat, flat_far, grad_qkv[0], grad_qkv_far), (grad_attended, attended_far, context[0], context_far)]
    if quick:
        one_keep, one_send, two_keep, two_send = weight_grad(place, one_pairs, "one")
        down_keep, down_send = halve(tie(down_keep, one_send), over("x", down_send))
        one_got, two_got = over("t", one_send), over("x", two_send)
        up_keep, up_send = halve(tie(up_keep, two_got), over("t", up_send))
        up_got = over("x", up_send)
        down_got = over("l", down_send)
    else:
        one_last = plain_sum(one_pairs)
    if quick:
        grad_qkv = [tie(g, down_send) for g in grad_qkv]
    sent_back = dot(grad_qkv[0], w_qkv[0], 1, 1) + dot(grad_qkv[1], w_qkv[1], 1, 1)
    input_grad = (grad_one + sent_back).astype(bf16).reshape(2, half, width)
    got = swap(take(input_grad, 1 - c), "ctx")
    input_grad = order(c, take(input_grad, c)[None], got[None], 0)
    if quick:
        small_after = down_send
        two_keep, two_send = halve(tie(two_keep, down_got), two_got)
        one_keep, one_send = halve(one_keep, one_got)
        two_got, one_got = over("t", two_send), over("x", one_send)
        down_keep, down_send = halve(down_keep, down_got)
        down_got = over("h", down_send)
        low_got = over("l", halve(tie(two_keep, up_got), two_got, split=False))
        up_keep, up_send = halve(up_keep, up_got)
        up_got = over("l", up_send)
        down_keep, down_send = halve(down_keep, down_got)
        one_keep, one_send = halve(tie(one_keep, up_got), one_got, low_got)
        up_keep, up_send = halve(up_keep, up_got)
        up_last = (up_keep, over("h", up_send))
        down_last = (down_keep, over("t", down_send))
        one_last = (one_keep, over("h", one_send))
        sums_one, sums_two, sums_pre = (tie(v, small_after) for v in (sums_one, sums_two, sums_pre))
    input_grad = order(t, input_grad, swap(input_grad, "tp"), 0)
    sums_one, sums_two = jnp.sum(sums_one, 1), jnp.sum(sums_two, 1)

    def settle(values):
        values = jnp.where(c == 0, values, values[::-1])
        values = jnp.where(t == 0, values, values[:, ::-1])
        return values.transpose(1, 0, 2).reshape(-1)

    small = jnp.concatenate(
        [settle(sums[:, :, 0]), settle(sums[:, :, 1]), settle(jnp.sum(sums_pre, 1).reshape(2, 2, -1)), sums_one[2], sums_two[2], sums_one[0], sums_one[1], sums_two[0], sums_two[1]]
    )
    small = tie(small.reshape(-1, 128), layer_all)
    small = lax.all_gather(small, ("dp", "ctx", "tp"), axis=0, tiled=False)
    small = jnp.sum(small, axis=0).reshape(-1)

    def cut_tp(start, size):
        return lax.dynamic_slice_in_dim(small, start + t * (size // 2), size // 2)

    at = 2 * inner + ff
    vectors = [lax.slice_in_dim(small, at + i * width, at + (i + 1) * width) for i in range(6)]

    if quick:
        layer_all = tie(layer_all, down_last[0])
    layer_out = lax.dynamic_slice_in_dim(layer_all, c * half, half, 1)
    if quick:
        one_last = (tie(one_last[0], input_grad, small), one_last[1])
    (down_shard,) = settle_columns(place, close(place, down_last), 1)
    (up_shard,) = settle_columns(place, close(place, up_last), 1)
    one_shard = settle_columns(place, close(place, one_last), 4)
    return (
        layer_out,
        input_grad,
        *one_shard[:3],
        one_shard[3].T,
        up_shard,
        down_shard.T,
        cut_tp(0, inner),
        cut_tp(inner, inner),
        vectors[0],
        cut_tp(2 * inner, ff),
        *vectors[1:],
    )


def solution(mesh):
    weight_in, weight_out = P(("dp", "ctx"), "tp"), P("tp", ("dp", "ctx"))
    rows = P("dp", "ctx", None)
    weights = (weight_in, weight_in, weight_in, weight_out, weight_in, weight_out)
    vectors = (P("tp"), P("tp"), P(), P("tp"), P(), P(), P(), P(), P())
    dp_count = mesh.shape["dp"]

    def run(*args):
        return body(dp_count, *args)

    return jax.shard_map(
        run,
        mesh=mesh,
        in_specs=(rows, P("dp", None), *weights, *vectors, rows),
        out_specs=(rows, rows, *weights, *vectors),
        check_vma=False,
    )
```

```python
import functools

import jax
import jax.numpy as jnp
from jax import lax
from jax.experimental import pallas as pl
from jax.experimental.pallas import tpu as pltpu
from jax.sharding import PartitionSpec as P

HEAD_DIM = 64
LANES = 2 * HEAD_DIM

epsilon = 1e-12
root_half = 0.7071067811865476
inv_root_two_pi = 0.3989422804014327
bf16 = jnp.bfloat16
f32 = jnp.float32


def dot(left, right, left_dim, right_dim):
    return lax.dot_general(left, right, (((left_dim,), (right_dim,)), ((), ())), preferred_element_type=f32)


def norm_forward(values, gain, shift):
    centre = values - jnp.mean(values, axis=-1, keepdims=True)
    inverse = lax.rsqrt(jnp.mean(centre * centre, axis=-1, keepdims=True) + epsilon)
    normed = centre * inverse
    return (normed * gain + shift, normed, inverse)


def swap(values, axis):
    return lax.ppermute(values, axis, [(0, 1), (1, 0)])


def swap_x(values):
    return lax.ppermute(values, "dp", [(i, i ^ 1) for i in range(8)])


def shift_z(values, step):
    return lax.ppermute(values, "dp", [(i, (i + 2 * step) % 8) for i in range(8)])


def take(values, index, axis=0):
    return lax.dynamic_index_in_dim(values, index, axis, keepdims=False)


def add(left, right):
    return (left.astype(f32) + right.astype(f32)).astype(bf16)


def order(index, mine, other, axis):
    return jnp.where(index == 0, jnp.concatenate([mine, other], axis), jnp.concatenate([other, mine], axis))


def assemble_kernel(cuts, place, one, one_y, two, two_x, *rest):
    outs, sems = rest[: len(cuts)], rest[len(cuts)]
    z, x = place[0], place[1]
    rows = one.shape[2]
    copies = []
    for k in range(4):
        for far_x in range(2):
            block = lax.rem(z + 4 - k, 4) * 2 + lax.rem(x + far_x, 2)
            at = pl.ds(pl.multiple_of(block * rows, rows), rows)
            for far_t in range(2):
                if k < 2:
                    source = (one_y if far_t else one).at[far_x, k]
                else:
                    source = (two_x if far_x else two).at[far_t, k - 2]
                for n, (start, size) in enumerate(cuts):
                    copies.append(
                        pltpu.make_async_copy(
                            source.at[:, start : start + size],
                            outs[n].at[at, far_t * size : far_t * size + size],
                            sems.at[len(copies)],
                        )
                    )
                    copies[-1].start()
    for copy in copies:
        copy.wait()


def gather_weights(piece, cuts, place, dp_count):
    rows, cols = piece.shape
    total = dp_count * rows
    if dp_count != 8:
        t = lax.axis_index("tp")
        both = lax.all_gather(piece, ("tp", "dp"), axis=0, tiled=True).reshape(2, total, cols)
        first, second = take(both, t), take(both, 1 - t)
        return [
            jnp.concatenate([first[:, s : s + n], second[:, s : s + n]], 1) for s, n in cuts
        ]
    line = [piece] + [shift_z(piece, k) for k in range(1, 4)]
    one, two = jnp.stack(line[:2]), jnp.stack(line[2:])
    one_x, two_y = swap_x(one), swap(two, "tp")
    one, two = jnp.stack([one, one_x]), jnp.stack([two, two_y])
    one_y, two_x = swap(one, "tp"), swap_x(two)
    anyspace = pl.BlockSpec(memory_space=pl.ANY)


    return pl.pallas_call(
        functools.partial(assemble_kernel, cuts),
        out_shape=[jax.ShapeDtypeStruct((total, 2 * n), bf16) for _, n in cuts],
        in_specs=[pl.BlockSpec(memory_space=pltpu.SMEM)] + [anyspace] * 4,
        out_specs=[pl.BlockSpec(memory_space=pltpu.VMEM)] * len(cuts),
        scratch_shapes=[pltpu.SemaphoreType.DMA((16 * len(cuts),))],
        compiler_params=pltpu.CompilerParams(vmem_limit_bytes=24 << 20),
        name="assemble",
    )(place, one, one_y, two, two_x)


def tie_kernel(*refs):
    pass


def tie(value, *after):
    anyspace = pl.BlockSpec(memory_space=pl.ANY)
    return pl.pallas_call(
        tie_kernel,
        out_shape=jax.ShapeDtypeStruct(value.shape, value.dtype),
        in_specs=[anyspace] * (1 + len(after)),
        out_specs=anyspace,
        input_output_aliases={0: 0},
        name="tie",
    )(value, *after)


def attend_kernel(qkv, seg_keys, seg_queries, context, probs, bias):
    quarter = qkv.shape[1] // 3

    @pl.when(pl.program_id(0) == 0)
    def _():
        bias[...] = jnp.where(seg_keys[...] == seg_queries[...], 0.0, -1000000000.0)

    low = lax.broadcasted_iota(jnp.int32, (1, LANES), 1) < HEAD_DIM
    for pair in range(quarter // LANES):
        cols = slice(pair * LANES, pair * LANES + LANES)
        query = qkv[:, cols] * 0.125
        key = qkv[:, quarter + pair * LANES : quarter + pair * LANES + LANES]
        value_t = qkv[:, 2 * quarter + pair * LANES : 2 * quarter + pair * LANES + LANES].T
        parts = []
        for h in range(2):
            mine = jnp.where(low if h == 0 else ~low, query, jnp.zeros_like(query))
            scores = dot(key, mine, 1, 1) + bias[...]
            raised = jnp.exp(scores - jnp.max(scores, axis=0, keepdims=True))
            prob = (raised * (1.0 / jnp.sum(raised, axis=0, keepdims=True))).astype(bf16)
            probs[2 * pair + h] = prob
            parts.append(dot(value_t[h * HEAD_DIM : (h + 1) * HEAD_DIM], prob, 1, 0))
        context[:, cols] = jnp.concatenate(parts, 0).T.astype(bf16)


def attend(qkv, seg):
    rows, cols = qkv.shape
    half = cols // 2
    quarter = half // 3
    heads = quarter // HEAD_DIM
    return pl.pallas_call(
        attend_kernel,
        grid=(2,),
        out_shape=[jax.ShapeDtypeStruct((rows, 2 * quarter), bf16), jax.ShapeDtypeStruct((2 * heads, rows, rows), bf16)],
        in_specs=[
            pl.BlockSpec((rows, half), lambda i: (0, i)),
            pl.BlockSpec((rows, 1), lambda i: (0, 0)),
            pl.BlockSpec((1, rows), lambda i: (0, 0)),
        ],
        out_specs=[pl.BlockSpec((rows, quarter), lambda i: (0, i)), pl.BlockSpec((heads, rows, rows), lambda i: (i, 0, 0))],
        scratch_shapes=[pltpu.VMEM((rows, rows), f32)],
        compiler_params=pltpu.CompilerParams(vmem_limit_bytes=48 << 20),
        cost_estimate=pl.CostEstimate(flops=1024, bytes_accessed=1024, transcendentals=0),
        name="attend",
    )(qkv, seg.reshape(rows, 1), seg.reshape(1, rows))


def attend_back_kernel(qkv, probs, upstream, *rest):
    grads, sums = rest[-2:]
    quarter = qkv.shape[1] // 3
    low = lax.broadcasted_iota(jnp.int32, (1, LANES), 1) < HEAD_DIM
    for pair in range(quarter // LANES):
        cols = [slice(n * quarter + pair * LANES, n * quarter + pair * LANES + LANES) for n in range(3)]
        query, key, value = (qkv[:, c] for c in cols)
        key_t = key.T
        above = upstream[:, cols[0]]
        grad_q, grad_k, grad_v = [], [], []
        for h in range(2):
            mine = jnp.where(low if h == 0 else ~low, above, jnp.zeros_like(above))
            grad_p = dot(value, mine, 1, 1)
            prob_low = probs[2 * pair + h]
            prob = prob_low.astype(f32)
            weighted = prob * grad_p
            inner = jnp.sum(weighted, axis=0, keepdims=True)
            grad_s = (weighted - prob * inner).astype(bf16)
            grad_k.append(dot(grad_s, query, 1, 0))
            grad_v.append(dot(prob_low, above, 1, 0))
            grad_q.append(dot(key_t[h * HEAD_DIM : (h + 1) * HEAD_DIM], grad_s, 1, 0))
        out_q = (jnp.concatenate(grad_q, 0) * 0.125).T.astype(bf16)
        out_v = jnp.where(low, grad_v[0], grad_v[1]).astype(bf16)
        grads[:, cols[0]] = out_q
        grads[:, cols[1]] = (jnp.where(low, grad_k[0], grad_k[1]) * 0.125).astype(bf16)
        grads[:, cols[2]] = out_v
        for n, out in ((0, out_q), (1, out_v)):
            total = jnp.sum(out.astype(f32), axis=0, keepdims=True)
            sums[0, n, :, cols[0]] = jnp.broadcast_to(total, (8, LANES))


def attend_back(qkv, probs, upstream, after):
    rows, cols = qkv.shape
    half = cols // 2
    quarter = half // 3
    heads = quarter // HEAD_DIM
    return pl.pallas_call(
        attend_back_kernel,
        grid=(2,),
        out_shape=[jax.ShapeDtypeStruct((rows, cols), bf16), jax.ShapeDtypeStruct((2, 2, 8, quarter), f32)],
        in_specs=[
            pl.BlockSpec((rows, half), lambda i: (0, i)),
            pl.BlockSpec((heads, rows, rows), lambda i: (i, 0, 0)),
            pl.BlockSpec((rows, quarter), lambda i: (0, i)),
        ]
        + [pl.BlockSpec(memory_space=pl.ANY)] * len(after),
        out_specs=[pl.BlockSpec((rows, half), lambda i: (0, i)), pl.BlockSpec((1, 2, 8, quarter), lambda i: (i, 0, 0, 0))],
        compiler_params=pltpu.CompilerParams(vmem_limit_bytes=48 << 20),
        cost_estimate=pl.CostEstimate(flops=1024, bytes_accessed=1024, transcendentals=0),
        name="attend_back",
    )(qkv, probs, upstream, *after)


CHUNK = 128


def cheap():
    return pl.CostEstimate(flops=1024, bytes_accessed=1024, transcendentals=0)


def clamp(i, low, count):
    return jnp.clip(i - low, 0, count - 1)


def put(near, far, i, steps, value):
    @pl.when(i < steps)
    def _():
        near[0] = value

    @pl.when(i >= steps)
    def _():
        far[0] = value


def halves_of(group, width, unit):
    core = lambda i, p: lax.rem(p[2] + i // 4, 2)
    return pl.BlockSpec((1, width, unit // 2), lambda i, p: (group, (i // 2) % 2, core(i, p) * 2 + i % 2))


def blocks_of(group, width, unit):
    return pl.BlockSpec((1, width, unit), lambda i, p: (group, lax.rem(p[3] + i % 2, 2), lax.rem(p[2] + i // 2, 2)))


def half_outs(rows, unit):
    return [pl.BlockSpec((1, rows, unit // 2), lambda i, p, n=n: (clamp(i, n, 4) // 2, 0, clamp(i, n, 4) % 2)) for n in (0, 4)]


def block_ins(rows, unit):
    return [pl.BlockSpec((1, rows, unit), lambda i, p, n=n: (clamp(i, n, 2), 0, 0)) for n in (0, 2)]


def fixed(*shape):
    return pl.BlockSpec(shape, lambda i, p: (0,) * len(shape))


def call(kernel, place, grid, ins, in_specs, outs, out_specs, scratch, name):
    return pl.pallas_call(
        kernel,
        grid_spec=pltpu.PrefetchScalarGridSpec(num_scalar_prefetch=1, grid=(grid,), in_specs=in_specs, out_specs=out_specs, scratch_shapes=scratch),
        out_shape=[jax.ShapeDtypeStruct(*o) for o in outs],
        compiler_params=pltpu.CompilerParams(vmem_limit_bytes=48 << 20),
        cost_estimate=cheap(),
        name=name,
    )(place, *ins)


def mean(values):
    return jnp.sum(values, axis=-1, keepdims=True) * (1.0 / values.shape[-1])


def fold(values):
    return jnp.sum(values.reshape(-1, 8, values.shape[-1]), axis=0)


def mlp_kernel(place, low, up_weight, down_weight, up_bias, normed, above, bias, gain, shift, near, far, out, grad, grad_low, pre_near, pre_far, sums, up_sums, units, slope, down, total):
    i = pl.program_id(0)
    rows, width = low.shape
    cols = up_weight.shape[2]
    tile = cols // 4

    def up(out_ref):
        for n in range(4):
            at = slice(n * tile, n * tile + tile)
            pre = dot(low[...], up_weight[0, :, at], 1, 0) + up_bias[0, :, at]
            half = 0.5 * (1.0 + lax.erf(pre * root_half))
            value = (pre * half).astype(bf16)
            out_ref[0, :, at] = value
            units[i, :, at] = value
            slope[i, :, at] = (half + pre * jnp.exp(-0.5 * pre * pre) * inv_root_two_pi).astype(bf16)

    pl.when(i < 2)(lambda: up(near))
    pl.when(jnp.logical_and(i >= 2, i < 4))(lambda: up(far))

    @pl.when(i == 4)
    def _():
        total[...] = normed[...] + bias[...]

    @pl.when(jnp.logical_and(i >= 4, i < 8))
    def _():
        down[i - 4] = down_weight[0]
        total[...] += dot(units[i - 4], down_weight[0], 1, 1)

    @pl.when(i == 7)
    def _():
        def step(k, carry):
            at = pl.ds(pl.multiple_of(k * CHUNK, CHUNK), CHUNK)
            centre = total[at] - mean(total[at])
            inverse = lax.rsqrt(mean(centre * centre) + epsilon)
            unit = centre * inverse
            out[at] = (unit * gain[...] + shift[...]).astype(bf16)
            upper = above[at].astype(f32)
            scaled = upper * gain[...]
            lower = inverse * (scaled - mean(scaled) - unit * mean(scaled * unit))
            grad[at] = lower
            grad_low[at] = lower.astype(bf16)
            return tuple(c + fold(v) for c, v in zip(carry, (upper * unit, upper, lower)))

        zero = jnp.zeros((8, width), f32)
        done = lax.fori_loop(0, rows // CHUNK, step, (zero,) * 3)
        for n in range(3):
            sums[n] = done[n]

    def pre(out_ref):
        for n in range(4):
            at = slice(n * tile, n * tile + tile)
            value = (dot(grad_low[...], down[i - 8, :, at], 1, 0) * slope[i - 8, :, at].astype(f32)).astype(bf16)
            out_ref[0, :, at] = value
            up_sums[0, :, at] = fold(value.astype(f32))

    pl.when(jnp.logical_and(i >= 8, i < 10))(lambda: pre(pre_near))
    pl.when(i >= 10)(lambda: pre(pre_far))


def mlp(place, low, weights, up_bias, normed, above, bias, gain, shift):
    rows, width = low.shape
    unit = weights.shape[2] // 2

    def still(*shape):
        return pl.BlockSpec(shape, lambda i, p: (0,) * len(shape), pipeline_mode=pl.Buffered(1))

    def block(group, first):
        def index(i, p):
            j = clamp(i, first, 4)
            return (group, lax.rem(p[3] + j % 2, 2), lax.rem(p[2] + j // 2, 2))

        return pl.BlockSpec((1, width, unit), index)

    def outs(first):
        return [pl.BlockSpec((1, rows, unit), lambda i, p, n=n: (clamp(i, n, 2), 0, 0)) for n in (first, first + 2)]

    def bias_index(i, p):
        j = clamp(i, 0, 4)
        return (lax.rem(p[3] + j % 2, 2) * 2 + lax.rem(p[2] + j // 2, 2), 0, 0)

    one, vector = still(rows, width), still(1, width)
    return pl.pallas_call(
        mlp_kernel,
        grid_spec=pltpu.PrefetchScalarGridSpec(
            num_scalar_prefetch=1,
            grid=(12,),
            in_specs=[one, block(0, 0), block(1, 4), pl.BlockSpec((1, 1, unit), bias_index), one, one, vector, vector, vector],
            out_specs=outs(0) + [one, one, one] + outs(8) + [still(3, 8, width), pl.BlockSpec((1, 8, unit), lambda i, p: (clamp(i, 8, 4), 0, 0))],
            scratch_shapes=[pltpu.VMEM((4, rows, unit), bf16)] * 2 + [pltpu.VMEM((4, width, unit), bf16), pltpu.VMEM((rows, width), f32)],
        ),
        out_shape=[jax.ShapeDtypeStruct(*o) for o in (
            [((2, rows, unit), bf16)] * 2
            + [((rows, width), bf16), ((rows, width), f32), ((rows, width), bf16)]
            + [((2, rows, unit), bf16)] * 2
            + [((3, 8, width), f32), ((4, 8, unit), f32)]
        )],
        compiler_params=pltpu.CompilerParams(vmem_limit_bytes=60 << 20),
        cost_estimate=cheap(),
        name="mlp",
    )(place, low, weights, weights, up_bias.reshape(4, 1, unit), normed, above, bias[None], gain[None], shift[None])


def mlp_back_kernel(place, near, far, weight, grad_two, unit_one, inverse, gain, out_near, out_far, grad, grad_low, near_context, far_context, sums, total):
    i = pl.program_id(0)

    @pl.when(i == 0)
    def _():
        total[...] = grad_two[...] + dot(near[0], weight[0], 1, 1)

    @pl.when(i == 1)
    def _():
        total[...] += dot(near[0], weight[0], 1, 1)

    @pl.when(i >= 2)
    def _():
        total[...] += dot(far[0], weight[0], 1, 1)

    @pl.when(i == 3)
    def _():
        def step(k, carry):
            at = pl.ds(pl.multiple_of(k * CHUNK, CHUNK), CHUNK)
            upper = total[at]
            unit = unit_one[at]
            scaled = upper * gain[...]
            down = inverse[at] * (scaled - mean(scaled) - unit * mean(scaled * unit))
            grad[at] = down
            grad_low[at] = down.astype(bf16)
            return tuple(c + fold(v) for c, v in zip(carry, (upper * unit, upper, down)))

        zero = jnp.zeros((8, grad.shape[1]), f32)
        done = lax.fori_loop(0, grad.shape[0] // CHUNK, step, (zero,) * 3)
        for n in range(3):
            sums[n] = done[n]
        near_context[...] = dot(grad_low[...], out_near[...], 1, 0).astype(bf16)
        far_context[...] = dot(grad_low[...], out_far[...], 1, 0).astype(bf16)


def mlp_back(place, near, far, weights, grad_two, unit_one, inverse, gain, out_near, out_far, after):
    rows, width = grad_two.shape
    unit = weights.shape[2] // 2
    part = out_near.shape[1]
    one = fixed(rows, width)

    def kernel(*refs):
        mlp_back_kernel(*refs[:10], *refs[10 + len(after) :])

    return call(
        kernel,
        place,
        4,
        (near, far, weights, grad_two, unit_one, inverse, gain[None], out_near, out_far, *after),
        block_ins(rows, unit) + [blocks_of(0, width, unit), one, one, fixed(rows, 1), fixed(1, width)] + [fixed(width, part)] * 2 + [pl.BlockSpec(memory_space=pl.ANY)] * len(after),
        [((rows, width), f32), ((rows, width), bf16)] + [((rows, part), bf16)] * 2 + [((3, 8, width), f32)],
        [one, one] + [fixed(rows, part)] * 2 + [fixed(3, 8, width)],
        [pltpu.VMEM((rows, width), f32)],
        "mlp_back",
    )


def over(axis, values):
    if axis == "t":
        return swap(values, "tp")
    if axis == "x":
        return swap_x(values)
    flip = 2 if axis == "l" else 4
    return lax.ppermute(values, "dp", [(i, i ^ flip) for i in range(8)])


def grad_kernel(kind, place, *refs):
    lefts = 2 if kind == "one" else 1
    sources = refs[: 2 * lefts]
    rights = refs[2 * lefts : 4 * lefts]
    outs = refs[4 * lefts : -lefts]
    turned = refs[-lefts:]
    i = pl.program_id(0)
    z, x = place[0], place[1]
    rows, width = sources[0].shape
    piece = width // 8

    @pl.when(i == 0)
    def _():
        for at in range(8):
            a, b, c = at // 4, (at // 2) % 2, at % 2
            far_x, low, high = (b, a, c) if kind == "one" else (a, b, c)
            block = (2 * lax.rem(z // 2 + high, 2) + lax.rem(z + low, 2)) * 2 + lax.rem(x + far_x, 2)
            cols = pl.ds(pl.multiple_of(block * piece, piece), piece)
            for n in range(lefts):
                for far in range(2):
                    turned[n][at * piece : (at + 1) * piece, far * rows : (far + 1) * rows] = sources[2 * n + far][:, cols].T

    def work(n):
        near, away = rights[2 * n], rights[2 * n + 1]
        pick = (lambda r: r[...]) if kind == "one" else (lambda r: r[0])
        out = dot(turned[n][...], jnp.concatenate([pick(near), pick(away)], 0), 1, 0).astype(bf16)
        if kind == "tp":
            out = out.reshape(2, 4 * piece, out.shape[1])
            pl.when(i < 2)(lambda: outs[0].__setitem__(..., out))
            pl.when(i >= 2)(lambda: outs[1].__setitem__(..., out))
        elif kind == "x":
            out = out.reshape(2, 2, 2, piece, out.shape[1])
            outs[0][:, :, 0] = out[0]
            outs[1][:, :, 0] = out[1]
        else:
            out = out.reshape(2, 2, 2 * piece, out.shape[1])
            pl.when(i < 4)(lambda: outs[0].__setitem__(..., out[0]))
            pl.when(i >= 4)(lambda: outs[1].__setitem__(..., out[0]))
            outs[2][0] = out[1, 0]
            outs[3][0] = out[1, 1]

    if lefts == 1:
        work(0)
    else:
        last = lax.rem(i, 4) == 3
        pl.when(jnp.logical_not(last))(lambda: work(0))
        pl.when(last)(lambda: work(1))


def weight_grad(place, pairs, kind):
    rows, width = pairs[0][0].shape
    piece = width // 8
    whole = pl.BlockSpec((rows, width), lambda i, p: (0, 0))
    tile = 256 if kind == "one" else 512
    steps = 1024 // tile
    first = lambda i: jnp.minimum(i, steps - 1)
    second = lambda i: jnp.maximum(i, steps) - steps
    if kind == "one":
        maps = [lambda i, p: (0, (i // 4) * 3 + jnp.minimum(i % 4, 2)), lambda i, p: (0, i // 4)]
        right_specs = [pl.BlockSpec((rows, 256), m) for m in maps for _ in range(2)]
        shapes = [(2, 2 * piece, 1024)] * 4
        out_specs = [
            pl.BlockSpec((2, 2 * piece, 256), lambda i, p: (0, 0, first(i))),
            pl.BlockSpec((2, 2 * piece, 256), lambda i, p: (0, 0, second(i))),
        ] + [pl.BlockSpec((1, 2 * piece, 256), lambda i, p: (i // 4, 0, i % 4))] * 2
    else:
        right_specs = [pl.BlockSpec((1, rows, tile), lambda i, p: (i // steps, 0, i % steps))] * 2
        if kind == "tp":
            shapes = [(2, 4 * piece, 1024)] * 2
            out_specs = [
                pl.BlockSpec((2, 4 * piece, tile), lambda i, p: (0, 0, first(i))),
                pl.BlockSpec((2, 4 * piece, tile), lambda i, p: (0, 0, second(i))),
            ]
        else:
            shapes = [(2, 2, 2, piece, 1024)] * 2
            out_specs = [pl.BlockSpec((2, 2, 1, piece, tile), lambda i, p: (0, 0, i // steps, 0, i % steps))] * 2
    lefts = [v for p in pairs for v in p[:2]]
    rights = [v for p in pairs for v in p[2:]]
    outs = pl.pallas_call(
        functools.partial(grad_kernel, kind),
        grid_spec=pltpu.PrefetchScalarGridSpec(
            num_scalar_prefetch=1,
            grid=(2 * steps,),
            in_specs=[whole] * len(lefts) + right_specs,
            out_specs=out_specs,
            scratch_shapes=[pltpu.VMEM((width, 2 * rows), bf16)] * len(pairs),
        ),
        out_shape=[jax.ShapeDtypeStruct(shape, bf16) for shape in shapes],
        compiler_params=pltpu.CompilerParams(vmem_limit_bytes=60 << 20),
        cost_estimate=cheap(),
        name="weight_grad_" + kind,
    )(place, *lefts, *rights)
    return [v.reshape(2, -1, 1024) for v in outs]


def halve_kernel(count, *refs):
    total = refs[0][...].astype(f32)
    for part in refs[1:count]:
        total += part[...].astype(f32)
    total = total.astype(bf16)
    if len(refs) == count + 1:
        refs[count][...] = total
    else:
        refs[count][...] = total[0]
        refs[count + 1][...] = total[1]


def halve(*parts, split=True):
    _, rows, cols = parts[0].shape
    tile = min(rows, 128)
    block = pl.BlockSpec((2, tile, cols), lambda i: (0, i, 0))
    half = pl.BlockSpec((tile, cols), lambda i: (i, 0))
    outs = pl.pallas_call(
        functools.partial(halve_kernel, len(parts)),
        grid=(rows // tile,),
        out_shape=[jax.ShapeDtypeStruct((rows, cols), bf16)] * 2 if split else [jax.ShapeDtypeStruct((2, rows, cols), bf16)],
        in_specs=[block] * len(parts),
        out_specs=[half] * 2 if split else [block],
        cost_estimate=cheap(),
        name="halve",
    )(*parts)
    if not split:
        return outs[0]
    if rows == tile:
        return outs
    return [v.reshape(2, rows // 2, cols) for v in outs]


def plain_sum(pairs):
    grads = []
    for left, left_far, right, right_far in pairs:
        both = jnp.concatenate([right, right_far], -2)
        if both.ndim == 3:
            both = jnp.concatenate([both[0], both[1]], 1)
        both = dot(jnp.concatenate([left, left_far], 0), both, 0, 0)
        grads.append(both.astype(bf16).reshape(both.shape[0], 2, -1))
    grads = jnp.concatenate(grads, 2)
    mine = add(grads[:, 0], swap(grads[:, 1], "tp"))
    return [lax.psum_scatter(mine, "dp", scatter_dimension=0, tiled=True)]


def close_kernel(place, *refs):
    parts, (mine, send) = refs[:-2], refs[-2:]
    total = parts[0][...].astype(f32)
    for part in parts[1:]:
        total += part[...].astype(f32)
    rows = mine.shape[0]
    for core in range(2):

        @pl.when(place[2] == core)
        def _(core=core):
            mine[...] = total[core * rows : (core + 1) * rows]
            send[...] = total[(1 - core) * rows : (2 - core) * rows]


def close(place, parts):
    rows, cols = parts[0].shape
    return pl.pallas_call(
        close_kernel,
        out_shape=[jax.ShapeDtypeStruct((rows // 2, cols), f32)] * 2,
        in_specs=[pl.BlockSpec(memory_space=pltpu.SMEM)] + [pl.BlockSpec(memory_space=pltpu.VMEM)] * len(parts),
        out_specs=[pl.BlockSpec(memory_space=pltpu.VMEM)] * 2,
        cost_estimate=cheap(),
        name="close",
    )(place, *parts)


def settle_kernel(place, mine, other, *outs):
    size = mine.shape[1] // len(outs)
    for core in range(2):

        @pl.when(place[2] == core)
        def _(core=core):
            for n, out in enumerate(outs):
                for part, at in ((mine, core), (other, 1 - core)):
                    out[:, at * size : (at + 1) * size] = part[:, n * size : (n + 1) * size]


def settle_columns(place, pair, count):
    mine, send = pair
    other = swap(send, "ctx")
    rows, cols = mine.shape
    return pl.pallas_call(
        settle_kernel,
        out_shape=[jax.ShapeDtypeStruct((rows, 2 * cols // count), f32)] * count,
        in_specs=[pl.BlockSpec(memory_space=pltpu.SMEM)] + [pl.BlockSpec(memory_space=pltpu.VMEM)] * 2,
        out_specs=[pl.BlockSpec(memory_space=pltpu.VMEM)] * count,
        cost_estimate=cheap(),
        name="settle_columns",
    )(place, mine, other)


def body(dp_count, tokens, segments, query_weight, key_weight, value_weight, out_weight, up_weight, down_weight, query_bias, value_bias, out_bias, up_bias, down_bias, attn_gain, attn_shift, mlp_gain, mlp_shift, cotangent):
    c = lax.axis_index("ctx")
    t = lax.axis_index("tp")
    d = lax.axis_index("dp")
    place = jnp.stack([d // 2, d % 2, c, t]).astype(jnp.int32)
    half, width = tokens.shape[1], tokens.shape[2]
    rows = 2 * half
    inner = 2 * query_bias.shape[0]
    ff = 2 * up_bias.shape[0]
    piece_rows = query_weight.shape[0]

    one = jnp.stack([query_weight, key_weight, value_weight, out_weight.T], 1)
    one = one.reshape(piece_rows, 4, 2, -1).transpose(2, 0, 1, 3).reshape(2, piece_rows, -1)
    one = one.astype(bf16)
    piece = order(c, take(one, c), swap(take(one, 1 - c), "ctx"), 0)
    unit = piece.shape[1]
    quarter = unit // 4
    qkv_mine, out_mine = gather_weights(piece, ((0, 3 * quarter), (3 * quarter, quarter)), place, dp_count)
    w_qkv = (qkv_mine, swap(qkv_mine, "ctx"))
    w_out = (out_mine, swap(out_mine, "ctx"))
    rest = jnp.stack([up_weight.astype(bf16), down_weight.T.astype(bf16)])
    rest = lax.all_gather(rest, ("tp", "dp", "ctx"), axis=1, tiled=True)

    biases = jnp.concatenate([query_bias, value_bias, up_bias])
    biases = jnp.stack([biases, swap(biases, "tp")])
    hin = inner // 2

    def near(values):
        values = values.reshape(2, 2, -1).transpose(1, 0, 2)
        return jnp.where(c == 0, values, values[::-1])

    bias_q, bias_v = near(biases[:, :hin]), near(biases[:, hin : 2 * hin])
    bias_up = jnp.where(t == 0, biases[:, 2 * hin :], biases[::-1, 2 * hin :])
    bias_qkv = jnp.stack([bias_q, jnp.zeros_like(bias_q), bias_v], 2).reshape(2, -1)

    seq = 2 * t + c
    other_seq = 2 * t + 1 - c
    pair_mine = jnp.stack([take(tokens, seq), take(cotangent, seq), take(tokens, other_seq)])
    pair_send = jnp.stack([take(tokens, other_seq), take(cotangent, other_seq), take(tokens, seq)])
    got = swap(pair_send, "ctx")
    flat = order(c, pair_mine[0], got[0], 0)
    flat_far = order(c, pair_mine[2], got[2], 0)
    grad_output = order(c, pair_mine[1], got[1], 0)
    flat = tie(flat, flat_far, grad_output)
    seg = take(segments, seq)

    def far(values):
        return swap(values, "ctx")

    qkv = [(dot(flat, w_qkv[r], 1, 0) + bias_qkv[r]).astype(bf16) for r in range(2)]
    attended = [attend(qkv[r], seg) for r in range(2)]
    context = [a[0] for a in attended]
    probs = [a[1] for a in attended]
    resid_one = flat.astype(f32) + dot(context[0], w_out[0], 1, 1) + dot(context[1], w_out[1], 1, 1) + out_bias
    normed_one, unit_one, inverse_one = norm_forward(resid_one, attn_gain, attn_shift)
    normed_low = normed_one.astype(bf16)
    normed_far, context_far = far(normed_low), far(context[1])
    normed_low = tie(normed_low, normed_far, context_far)
    hidden_near, hidden_far, output, grad_two, grad_mixed, pre_near, pre_far, sums_two, sums_pre = mlp(
        place, normed_low, rest, bias_up, normed_one, grad_output, down_bias, mlp_gain, mlp_shift
    )
    hidden_far, pre_got, grad_mixed_far = far(hidden_far), far(pre_far), far(grad_mixed)

    layer_all = lax.all_gather(output, ("tp", "ctx"), axis=0, tiled=False)
    grad_one, grad_attended, *grad_context, sums_one = mlp_back(
        place, pre_near, pre_far, rest, grad_two, unit_one, inverse_one, attn_gain, *w_out, ()
    )
    quick = dp_count == 8
    down_pairs = [(tie(grad_mixed, grad_attended), grad_mixed_far, hidden_near, hidden_far)]
    up_pairs = [(normed_low, normed_far, pre_near, pre_got)]
    if quick:
        down_keep, down_send = weight_grad(place, down_pairs, "x")
        up_keep, up_send = weight_grad(place, up_pairs, "tp")
        sent = (down_send, up_send)
    else:
        down_last, up_last, sent = plain_sum(down_pairs), plain_sum(up_pairs), ()
    back = [attend_back(qkv[r], probs[r], grad_context[r], sent) for r in range(2)]
    grad_qkv = [b[0] for b in back]
    sums = jnp.stack([b[1] for b in back])[:, :, :, 0]
    grad_qkv_far = far(grad_qkv[1])
    attended_far = far(grad_attended)
    one_pairs = [(flat, flat_far, grad_qkv[0], grad_qkv_far), (grad_attended, attended_far, context[0], context_far)]
    if quick:
        one_keep, one_send, two_keep, two_send = weight_grad(place, one_pairs, "one")
        down_keep, down_send = halve(tie(down_keep, one_send), over("x", down_send))
        one_got, two_got = over("t", one_send), over("x", two_send)
        up_keep, up_send = halve(tie(up_keep, two_got), over("t", up_send))
        up_got = over("x", up_send)
        down_got = over("l", down_send)
    else:
        one_last = plain_sum(one_pairs)
    if quick:
        grad_qkv = [tie(g, down_send) for g in grad_qkv]
    sent_back = dot(grad_qkv[0], w_qkv[0], 1, 1) + dot(grad_qkv[1], w_qkv[1], 1, 1)
    input_grad = (grad_one + sent_back).astype(bf16).reshape(2, half, width)
    got = swap(take(input_grad, 1 - c), "ctx")
    input_grad = order(c, take(input_grad, c)[None], got[None], 0)
    if quick:
        small_after = down_send
        two_keep, two_send = halve(tie(two_keep, down_got), two_got)
        one_keep, one_send = halve(one_keep, one_got)
        two_got, one_got = over("t", two_send), over("x", one_send)
        down_keep, down_send = halve(down_keep, down_got)
        down_got = over("h", down_send)
        low_got = over("l", halve(tie(two_keep, up_got), two_got, split=False))
        up_keep, up_send = halve(up_keep, up_got)
        up_got = over("l", up_send)
        down_keep, down_send = halve(down_keep, down_got)
        one_keep, one_send = halve(tie(one_keep, up_got), one_got, low_got)
        up_keep, up_send = halve(up_keep, up_got)
        up_last = (up_keep, over("h", up_send))
        down_last = (down_keep, over("t", down_send))
        one_last = (one_keep, over("h", one_send))
        down_last, up_last = ((tie(keep, one_send), got) for keep, got in (down_last, up_last))
        sums_one, sums_two, sums_pre = (tie(v, small_after) for v in (sums_one, sums_two, sums_pre))
    input_grad = order(t, input_grad, swap(input_grad, "tp"), 0)
    sums_one, sums_two = jnp.sum(sums_one, 1), jnp.sum(sums_two, 1)

    def settle(values):
        values = jnp.where(c == 0, values, values[::-1])
        values = jnp.where(t == 0, values, values[:, ::-1])
        return values.transpose(1, 0, 2).reshape(-1)

    small = jnp.concatenate(
        [settle(sums[:, :, 0]), settle(sums[:, :, 1]), settle(jnp.sum(sums_pre, 1).reshape(2, 2, -1)), sums_one[2], sums_two[2], sums_one[0], sums_one[1], sums_two[0], sums_two[1]]
    )
    small = tie(small.reshape(-1, 128), layer_all)
    small = lax.all_gather(small, ("dp", "ctx", "tp"), axis=0, tiled=False)
    small = jnp.sum(small, axis=0).reshape(-1)

    def cut_tp(start, size):
        return lax.dynamic_slice_in_dim(small, start + t * (size // 2), size // 2)

    at = 2 * inner + ff
    vectors = [lax.slice_in_dim(small, at + i * width, at + (i + 1) * width) for i in range(6)]

    if quick:
        layer_all = tie(layer_all, down_last[0])
    layer_out = lax.dynamic_slice_in_dim(layer_all, c * half, half, 1)
    if quick:
        one_last = (tie(one_last[0], input_grad, small), one_last[1])
    (down_shard,) = settle_columns(place, close(place, down_last), 1)
    (up_shard,) = settle_columns(place, close(place, up_last), 1)
    one_shard = settle_columns(place, close(place, one_last), 4)
    return (
        layer_out,
        input_grad,
        *one_shard[:3],
        one_shard[3].T,
        up_shard,
        down_shard.T,
        cut_tp(0, inner),
        cut_tp(inner, inner),
        vectors[0],
        cut_tp(2 * inner, ff),
        *vectors[1:],
    )


def solution(mesh):
    weight_in, weight_out = P(("dp", "ctx"), "tp"), P("tp", ("dp", "ctx"))
    rows = P("dp", "ctx", None)
    weights = (weight_in, weight_in, weight_in, weight_out, weight_in, weight_out)
    vectors = (P("tp"), P("tp"), P(), P("tp"), P(), P(), P(), P(), P())
    dp_count = mesh.shape["dp"]

    def run(*args):
        return body(dp_count, *args)

    return jax.shard_map(
        run,
        mesh=mesh,
        in_specs=(rows, P("dp", None), *weights, *vectors, rows),
        out_specs=(rows, rows, *weights, *vectors),
        check_vma=False,
    )
```

```python
import functools

import jax
import jax.numpy as jnp
from jax import lax
from jax.experimental import pallas as pl
from jax.experimental.pallas import tpu as pltpu
from jax.sharding import PartitionSpec as P

HEAD_DIM = 64
LANES = 2 * HEAD_DIM

epsilon = 1e-12
root_half = 0.7071067811865476
inv_root_two_pi = 0.3989422804014327
bf16 = jnp.bfloat16
f32 = jnp.float32


def dot(left, right, left_dim, right_dim):
    return lax.dot_general(left, right, (((left_dim,), (right_dim,)), ((), ())), preferred_element_type=f32)


def norm_forward(values, gain, shift):
    centre = values - jnp.mean(values, axis=-1, keepdims=True)
    inverse = lax.rsqrt(jnp.mean(centre * centre, axis=-1, keepdims=True) + epsilon)
    normed = centre * inverse
    return (normed * gain + shift, normed, inverse)


def swap(values, axis):
    return lax.ppermute(values, axis, [(0, 1), (1, 0)])


def swap_x(values):
    return lax.ppermute(values, "dp", [(i, i ^ 1) for i in range(8)])


def shift_z(values, step):
    return lax.ppermute(values, "dp", [(i, (i + 2 * step) % 8) for i in range(8)])


def take(values, index, axis=0):
    return lax.dynamic_index_in_dim(values, index, axis, keepdims=False)


def add(left, right):
    return (left.astype(f32) + right.astype(f32)).astype(bf16)


def order(index, mine, other, axis):
    return jnp.where(index == 0, jnp.concatenate([mine, other], axis), jnp.concatenate([other, mine], axis))


def assemble_kernel(cuts, place, one, one_y, two, two_x, *rest):
    outs, sems = rest[: len(cuts)], rest[len(cuts)]
    z, x = place[0], place[1]
    rows = one.shape[2]
    copies = []
    for k in range(4):
        for far_x in range(2):
            block = lax.rem(z + 4 - k, 4) * 2 + lax.rem(x + far_x, 2)
            at = pl.ds(pl.multiple_of(block * rows, rows), rows)
            for far_t in range(2):
                if k < 2:
                    source = (one_y if far_t else one).at[far_x, k]
                else:
                    source = (two_x if far_x else two).at[far_t, k - 2]
                for n, (start, size) in enumerate(cuts):
                    copies.append(
                        pltpu.make_async_copy(
                            source.at[:, start : start + size],
                            outs[n].at[at, far_t * size : far_t * size + size],
                            sems.at[len(copies)],
                        )
                    )
                    copies[-1].start()
    for copy in copies:
        copy.wait()


def gather_weights(piece, cuts, place, dp_count):
    rows, cols = piece.shape
    total = dp_count * rows
    if dp_count != 8:
        t = lax.axis_index("tp")
        both = lax.all_gather(piece, ("tp", "dp"), axis=0, tiled=True).reshape(2, total, cols)
        first, second = take(both, t), take(both, 1 - t)
        return [
            jnp.concatenate([first[:, s : s + n], second[:, s : s + n]], 1) for s, n in cuts
        ]
    line = [piece] + [shift_z(piece, k) for k in range(1, 4)]
    one, two = jnp.stack(line[:2]), jnp.stack(line[2:])
    one_x, two_y = swap_x(one), swap(two, "tp")
    one, two = jnp.stack([one, one_x]), jnp.stack([two, two_y])
    one_y, two_x = swap(one, "tp"), swap_x(two)
    anyspace = pl.BlockSpec(memory_space=pl.ANY)


    return pl.pallas_call(
        functools.partial(assemble_kernel, cuts),
        out_shape=[jax.ShapeDtypeStruct((total, 2 * n), bf16) for _, n in cuts],
        in_specs=[pl.BlockSpec(memory_space=pltpu.SMEM)] + [anyspace] * 4,
        out_specs=[pl.BlockSpec(memory_space=pltpu.VMEM)] * len(cuts),
        scratch_shapes=[pltpu.SemaphoreType.DMA((16 * len(cuts),))],
        compiler_params=pltpu.CompilerParams(vmem_limit_bytes=24 << 20),
        name="assemble",
    )(place, one, one_y, two, two_x)


def tie_kernel(*refs):
    pass


def tie(value, *after):
    anyspace = pl.BlockSpec(memory_space=pl.ANY)
    return pl.pallas_call(
        tie_kernel,
        out_shape=jax.ShapeDtypeStruct(value.shape, value.dtype),
        in_specs=[anyspace] * (1 + len(after)),
        out_specs=anyspace,
        input_output_aliases={0: 0},
        name="tie",
    )(value, *after)


def attend_kernel(qkv, seg_keys, seg_queries, context, probs, bias):
    quarter = qkv.shape[1] // 3

    @pl.when(pl.program_id(0) == 0)
    def _():
        bias[...] = jnp.where(seg_keys[...] == seg_queries[...], 0.0, -1000000000.0)

    low = lax.broadcasted_iota(jnp.int32, (1, LANES), 1) < HEAD_DIM
    for pair in range(quarter // LANES):
        cols = slice(pair * LANES, pair * LANES + LANES)
        query = qkv[:, cols] * 0.125
        key = qkv[:, quarter + pair * LANES : quarter + pair * LANES + LANES]
        value_t = qkv[:, 2 * quarter + pair * LANES : 2 * quarter + pair * LANES + LANES].T
        parts = []
        for h in range(2):
            mine = jnp.where(low if h == 0 else ~low, query, jnp.zeros_like(query))
            scores = dot(key, mine, 1, 1) + bias[...]
            raised = jnp.exp(scores - jnp.max(scores, axis=0, keepdims=True))
            prob = (raised * (1.0 / jnp.sum(raised, axis=0, keepdims=True))).astype(bf16)
            probs[2 * pair + h] = prob
            parts.append(dot(value_t[h * HEAD_DIM : (h + 1) * HEAD_DIM], prob, 1, 0))
        context[:, cols] = jnp.concatenate(parts, 0).T.astype(bf16)


def attend(qkv, seg):
    rows, cols = qkv.shape
    half = cols // 2
    quarter = half // 3
    heads = quarter // HEAD_DIM
    return pl.pallas_call(
        attend_kernel,
        grid=(2,),
        out_shape=[jax.ShapeDtypeStruct((rows, 2 * quarter), bf16), jax.ShapeDtypeStruct((2 * heads, rows, rows), bf16)],
        in_specs=[
            pl.BlockSpec((rows, half), lambda i: (0, i)),
            pl.BlockSpec((rows, 1), lambda i: (0, 0)),
            pl.BlockSpec((1, rows), lambda i: (0, 0)),
        ],
        out_specs=[pl.BlockSpec((rows, quarter), lambda i: (0, i)), pl.BlockSpec((heads, rows, rows), lambda i: (i, 0, 0))],
        scratch_shapes=[pltpu.VMEM((rows, rows), f32)],
        compiler_params=pltpu.CompilerParams(vmem_limit_bytes=48 << 20),
        cost_estimate=pl.CostEstimate(flops=1024, bytes_accessed=1024, transcendentals=0),
        name="attend",
    )(qkv, seg.reshape(rows, 1), seg.reshape(1, rows))


def attend_back_kernel(qkv, probs, upstream, *rest):
    grads, sums = rest[-2:]
    quarter = qkv.shape[1] // 3
    low = lax.broadcasted_iota(jnp.int32, (1, LANES), 1) < HEAD_DIM
    for pair in range(quarter // LANES):
        cols = [slice(n * quarter + pair * LANES, n * quarter + pair * LANES + LANES) for n in range(3)]
        query, key, value = (qkv[:, c] for c in cols)
        key_t = key.T
        above = upstream[:, cols[0]]
        grad_q, grad_k, grad_v = [], [], []
        for h in range(2):
            mine = jnp.where(low if h == 0 else ~low, above, jnp.zeros_like(above))
            grad_p = dot(value, mine, 1, 1)
            prob_low = probs[2 * pair + h]
            prob = prob_low.astype(f32)
            weighted = prob * grad_p
            inner = jnp.sum(weighted, axis=0, keepdims=True)
            grad_s = (weighted - prob * inner).astype(bf16)
            grad_k.append(dot(grad_s, query, 1, 0))
            grad_v.append(dot(prob_low, above, 1, 0))
            grad_q.append(dot(key_t[h * HEAD_DIM : (h + 1) * HEAD_DIM], grad_s, 1, 0))
        out_q = (jnp.concatenate(grad_q, 0) * 0.125).T.astype(bf16)
        out_v = jnp.where(low, grad_v[0], grad_v[1]).astype(bf16)
        grads[:, cols[0]] = out_q
        grads[:, cols[1]] = (jnp.where(low, grad_k[0], grad_k[1]) * 0.125).astype(bf16)
        grads[:, cols[2]] = out_v
        for n, out in ((0, out_q), (1, out_v)):
            total = jnp.sum(out.astype(f32), axis=0, keepdims=True)
            sums[0, n, :, cols[0]] = jnp.broadcast_to(total, (8, LANES))


def attend_back(qkv, probs, upstream, after):
    rows, cols = qkv.shape
    half = cols // 2
    quarter = half // 3
    heads = quarter // HEAD_DIM
    return pl.pallas_call(
        attend_back_kernel,
        grid=(2,),
        out_shape=[jax.ShapeDtypeStruct((rows, cols), bf16), jax.ShapeDtypeStruct((2, 2, 8, quarter), f32)],
        in_specs=[
            pl.BlockSpec((rows, half), lambda i: (0, i)),
            pl.BlockSpec((heads, rows, rows), lambda i: (i, 0, 0)),
            pl.BlockSpec((rows, quarter), lambda i: (0, i)),
        ]
        + [pl.BlockSpec(memory_space=pl.ANY)] * len(after),
        out_specs=[pl.BlockSpec((rows, half), lambda i: (0, i)), pl.BlockSpec((1, 2, 8, quarter), lambda i: (i, 0, 0, 0))],
        compiler_params=pltpu.CompilerParams(vmem_limit_bytes=48 << 20),
        cost_estimate=pl.CostEstimate(flops=1024, bytes_accessed=1024, transcendentals=0),
        name="attend_back",
    )(qkv, probs, upstream, *after)


CHUNK = 128


def cheap():
    return pl.CostEstimate(flops=1024, bytes_accessed=1024, transcendentals=0)


def clamp(i, low, count):
    return jnp.clip(i - low, 0, count - 1)


def put(near, far, i, steps, value):
    @pl.when(i < steps)
    def _():
        near[0] = value

    @pl.when(i >= steps)
    def _():
        far[0] = value


def halves_of(group, width, unit):
    core = lambda i, p: lax.rem(p[2] + i // 4, 2)
    return pl.BlockSpec((1, width, unit // 2), lambda i, p: (group, (i // 2) % 2, core(i, p) * 2 + i % 2))


def blocks_of(group, width, unit):
    return pl.BlockSpec((1, width, unit), lambda i, p: (group, lax.rem(p[3] + i % 2, 2), lax.rem(p[2] + i // 2, 2)))


def half_outs(rows, unit):
    return [pl.BlockSpec((1, rows, unit // 2), lambda i, p, n=n: (clamp(i, n, 4) // 2, 0, clamp(i, n, 4) % 2)) for n in (0, 4)]


def block_ins(rows, unit):
    return [pl.BlockSpec((1, rows, unit), lambda i, p, n=n: (clamp(i, n, 2), 0, 0)) for n in (0, 2)]


def fixed(*shape):
    return pl.BlockSpec(shape, lambda i, p: (0,) * len(shape))


def call(kernel, place, grid, ins, in_specs, outs, out_specs, scratch, name):
    return pl.pallas_call(
        kernel,
        grid_spec=pltpu.PrefetchScalarGridSpec(num_scalar_prefetch=1, grid=(grid,), in_specs=in_specs, out_specs=out_specs, scratch_shapes=scratch),
        out_shape=[jax.ShapeDtypeStruct(*o) for o in outs],
        compiler_params=pltpu.CompilerParams(vmem_limit_bytes=48 << 20),
        cost_estimate=cheap(),
        name=name,
    )(place, *ins)


def mean(values):
    return jnp.sum(values, axis=-1, keepdims=True) * (1.0 / values.shape[-1])


def fold(values):
    return jnp.sum(values.reshape(-1, 8, values.shape[-1]), axis=0)


def mlp_kernel(place, low, up_weight, down_weight, up_bias, normed, above, bias, gain, shift, near, far, out, grad, grad_low, pre_near, pre_far, sums, up_sums, units, slope, down, total):
    i = pl.program_id(0)
    rows, width = low.shape
    cols = up_weight.shape[2]
    tile = cols // 4

    def up(out_ref):
        for n in range(4):
            at = slice(n * tile, n * tile + tile)
            pre = dot(low[...], up_weight[0, :, at], 1, 0) + up_bias[0, :, at]
            half = 0.5 * (1.0 + lax.erf(pre * root_half))
            value = (pre * half).astype(bf16)
            out_ref[0, :, at] = value
            units[i, :, at] = value
            slope[i, :, at] = (half + pre * jnp.exp(-0.5 * pre * pre) * inv_root_two_pi).astype(bf16)

    pl.when(i < 2)(lambda: up(near))
    pl.when(jnp.logical_and(i >= 2, i < 4))(lambda: up(far))

    @pl.when(i == 4)
    def _():
        total[...] = normed[...] + bias[...]

    @pl.when(jnp.logical_and(i >= 4, i < 8))
    def _():
        down[i - 4] = down_weight[0]
        total[...] += dot(units[i - 4], down_weight[0], 1, 1)

    @pl.when(i == 7)
    def _():
        def step(k, carry):
            at = pl.ds(pl.multiple_of(k * CHUNK, CHUNK), CHUNK)
            centre = total[at] - mean(total[at])
            inverse = lax.rsqrt(mean(centre * centre) + epsilon)
            unit = centre * inverse
            out[at] = (unit * gain[...] + shift[...]).astype(bf16)
            upper = above[at].astype(f32)
            scaled = upper * gain[...]
            lower = inverse * (scaled - mean(scaled) - unit * mean(scaled * unit))
            grad[at] = lower
            grad_low[at] = lower.astype(bf16)
            return tuple(c + fold(v) for c, v in zip(carry, (upper * unit, upper, lower)))

        zero = jnp.zeros((8, width), f32)
        done = lax.fori_loop(0, rows // CHUNK, step, (zero,) * 3)
        for n in range(3):
            sums[n] = done[n]

    def pre(out_ref):
        for n in range(4):
            at = slice(n * tile, n * tile + tile)
            value = (dot(grad_low[...], down[i - 8, :, at], 1, 0) * slope[i - 8, :, at].astype(f32)).astype(bf16)
            out_ref[0, :, at] = value
            up_sums[0, :, at] = fold(value.astype(f32))

    pl.when(jnp.logical_and(i >= 8, i < 10))(lambda: pre(pre_near))
    pl.when(i >= 10)(lambda: pre(pre_far))


def mlp(place, low, weights, up_bias, normed, above, bias, gain, shift):
    rows, width = low.shape
    unit = weights.shape[2] // 2

    def still(*shape):
        return pl.BlockSpec(shape, lambda i, p: (0,) * len(shape), pipeline_mode=pl.Buffered(1))

    def block(group, first):
        def index(i, p):
            j = clamp(i, first, 4)
            return (group, lax.rem(p[3] + j % 2, 2), lax.rem(p[2] + j // 2, 2))

        return pl.BlockSpec((1, width, unit), index)

    def outs(first):
        return [pl.BlockSpec((1, rows, unit), lambda i, p, n=n: (clamp(i, n, 2), 0, 0)) for n in (first, first + 2)]

    def bias_index(i, p):
        j = clamp(i, 0, 4)
        return (lax.rem(p[3] + j % 2, 2) * 2 + lax.rem(p[2] + j // 2, 2), 0, 0)

    one, vector = still(rows, width), still(1, width)
    return pl.pallas_call(
        mlp_kernel,
        grid_spec=pltpu.PrefetchScalarGridSpec(
            num_scalar_prefetch=1,
            grid=(12,),
            in_specs=[one, block(0, 0), block(1, 4), pl.BlockSpec((1, 1, unit), bias_index), one, one, vector, vector, vector],
            out_specs=outs(0) + [one, one, one] + outs(8) + [still(3, 8, width), pl.BlockSpec((1, 8, unit), lambda i, p: (clamp(i, 8, 4), 0, 0))],
            scratch_shapes=[pltpu.VMEM((4, rows, unit), bf16)] * 2 + [pltpu.VMEM((4, width, unit), bf16), pltpu.VMEM((rows, width), f32)],
        ),
        out_shape=[jax.ShapeDtypeStruct(*o) for o in (
            [((2, rows, unit), bf16)] * 2
            + [((rows, width), bf16), ((rows, width), f32), ((rows, width), bf16)]
            + [((2, rows, unit), bf16)] * 2
            + [((3, 8, width), f32), ((4, 8, unit), f32)]
        )],
        compiler_params=pltpu.CompilerParams(vmem_limit_bytes=60 << 20),
        cost_estimate=cheap(),
        name="mlp",
    )(place, low, weights, weights, up_bias.reshape(4, 1, unit), normed, above, bias[None], gain[None], shift[None])


def mlp_back_kernel(place, near, far, weight, grad_two, unit_one, inverse, gain, out_near, out_far, grad, grad_low, near_context, far_context, sums, total):
    i = pl.program_id(0)

    @pl.when(i == 0)
    def _():
        total[...] = grad_two[...] + dot(near[0], weight[0], 1, 1)

    @pl.when(i == 1)
    def _():
        total[...] += dot(near[0], weight[0], 1, 1)

    @pl.when(i >= 2)
    def _():
        total[...] += dot(far[0], weight[0], 1, 1)

    @pl.when(i == 3)
    def _():
        def step(k, carry):
            at = pl.ds(pl.multiple_of(k * CHUNK, CHUNK), CHUNK)
            upper = total[at]
            unit = unit_one[at]
            scaled = upper * gain[...]
            down = inverse[at] * (scaled - mean(scaled) - unit * mean(scaled * unit))
            grad[at] = down
            grad_low[at] = down.astype(bf16)
            return tuple(c + fold(v) for c, v in zip(carry, (upper * unit, upper, down)))

        zero = jnp.zeros((8, grad.shape[1]), f32)
        done = lax.fori_loop(0, grad.shape[0] // CHUNK, step, (zero,) * 3)
        for n in range(3):
            sums[n] = done[n]
        near_context[...] = dot(grad_low[...], out_near[...], 1, 0).astype(bf16)
        far_context[...] = dot(grad_low[...], out_far[...], 1, 0).astype(bf16)


def mlp_back(place, near, far, weights, grad_two, unit_one, inverse, gain, out_near, out_far, after):
    rows, width = grad_two.shape
    unit = weights.shape[2] // 2
    part = out_near.shape[1]
    one = fixed(rows, width)

    def kernel(*refs):
        mlp_back_kernel(*refs[:10], *refs[10 + len(after) :])

    return call(
        kernel,
        place,
        4,
        (near, far, weights, grad_two, unit_one, inverse, gain[None], out_near, out_far, *after),
        block_ins(rows, unit) + [blocks_of(0, width, unit), one, one, fixed(rows, 1), fixed(1, width)] + [fixed(width, part)] * 2 + [pl.BlockSpec(memory_space=pl.ANY)] * len(after),
        [((rows, width), f32), ((rows, width), bf16)] + [((rows, part), bf16)] * 2 + [((3, 8, width), f32)],
        [one, one] + [fixed(rows, part)] * 2 + [fixed(3, 8, width)],
        [pltpu.VMEM((rows, width), f32)],
        "mlp_back",
    )


def over(axis, values):
    if axis == "t":
        return swap(values, "tp")
    if axis == "x":
        return swap_x(values)
    flip = 2 if axis == "l" else 4
    return lax.ppermute(values, "dp", [(i, i ^ flip) for i in range(8)])


def grad_kernel(kind, place, *refs):
    lefts = 2 if kind == "one" else 1
    sources = refs[: 2 * lefts]
    rights = refs[2 * lefts : 4 * lefts]
    outs = refs[4 * lefts : -lefts]
    turned = refs[-lefts:]
    i = pl.program_id(0)
    z, x = place[0], place[1]
    rows, width = sources[0].shape
    piece = width // 8

    @pl.when(i == 0)
    def _():
        for at in range(8):
            a, b, c = at // 4, (at // 2) % 2, at % 2
            far_x, low, high = (b, a, c) if kind == "one" else (a, b, c)
            block = (2 * lax.rem(z // 2 + high, 2) + lax.rem(z + low, 2)) * 2 + lax.rem(x + far_x, 2)
            cols = pl.ds(pl.multiple_of(block * piece, piece), piece)
            for n in range(lefts):
                for far in range(2):
                    turned[n][at * piece : (at + 1) * piece, far * rows : (far + 1) * rows] = sources[2 * n + far][:, cols].T

    def work(n):
        near, away = rights[2 * n], rights[2 * n + 1]
        pick = (lambda r: r[...]) if kind == "one" else (lambda r: r[0])
        out = dot(turned[n][...], jnp.concatenate([pick(near), pick(away)], 0), 1, 0).astype(bf16)
        if kind == "tp":
            out = out.reshape(2, 4 * piece, out.shape[1])
            pl.when(i < 2)(lambda: outs[0].__setitem__(..., out))
            pl.when(i >= 2)(lambda: outs[1].__setitem__(..., out))
        elif kind == "x":
            out = out.reshape(2, 2, 2, piece, out.shape[1])
            outs[0][:, :, 0] = out[0]
            outs[1][:, :, 0] = out[1]
        else:
            out = out.reshape(2, 2, 2 * piece, out.shape[1])
            pl.when(i < 4)(lambda: outs[0].__setitem__(..., out[0]))
            pl.when(i >= 4)(lambda: outs[1].__setitem__(..., out[0]))
            outs[2][0] = out[1, 0]
            outs[3][0] = out[1, 1]

    if lefts == 1:
        work(0)
    else:
        last = lax.rem(i, 4) == 3
        pl.when(jnp.logical_not(last))(lambda: work(0))
        pl.when(last)(lambda: work(1))


def weight_grad(place, pairs, kind):
    rows, width = pairs[0][0].shape
    piece = width // 8
    whole = pl.BlockSpec((rows, width), lambda i, p: (0, 0))
    tile = 256 if kind == "one" else 512
    steps = 1024 // tile
    first = lambda i: jnp.minimum(i, steps - 1)
    second = lambda i: jnp.maximum(i, steps) - steps
    if kind == "one":
        maps = [lambda i, p: (0, (i // 4) * 3 + jnp.minimum(i % 4, 2)), lambda i, p: (0, i // 4)]
        right_specs = [pl.BlockSpec((rows, 256), m) for m in maps for _ in range(2)]
        shapes = [(2, 2 * piece, 1024)] * 4
        out_specs = [
            pl.BlockSpec((2, 2 * piece, 256), lambda i, p: (0, 0, first(i))),
            pl.BlockSpec((2, 2 * piece, 256), lambda i, p: (0, 0, second(i))),
        ] + [pl.BlockSpec((1, 2 * piece, 256), lambda i, p: (i // 4, 0, i % 4))] * 2
    else:
        right_specs = [pl.BlockSpec((1, rows, tile), lambda i, p: (i // steps, 0, i % steps))] * 2
        if kind == "tp":
            shapes = [(2, 4 * piece, 1024)] * 2
            out_specs = [
                pl.BlockSpec((2, 4 * piece, tile), lambda i, p: (0, 0, first(i))),
                pl.BlockSpec((2, 4 * piece, tile), lambda i, p: (0, 0, second(i))),
            ]
        else:
            shapes = [(2, 2, 2, piece, 1024)] * 2
            out_specs = [pl.BlockSpec((2, 2, 1, piece, tile), lambda i, p: (0, 0, i // steps, 0, i % steps))] * 2
    lefts = [v for p in pairs for v in p[:2]]
    rights = [v for p in pairs for v in p[2:]]
    outs = pl.pallas_call(
        functools.partial(grad_kernel, kind),
        grid_spec=pltpu.PrefetchScalarGridSpec(
            num_scalar_prefetch=1,
            grid=(2 * steps,),
            in_specs=[whole] * len(lefts) + right_specs,
            out_specs=out_specs,
            scratch_shapes=[pltpu.VMEM((width, 2 * rows), bf16)] * len(pairs),
        ),
        out_shape=[jax.ShapeDtypeStruct(shape, bf16) for shape in shapes],
        compiler_params=pltpu.CompilerParams(vmem_limit_bytes=60 << 20),
        cost_estimate=cheap(),
        name="weight_grad_" + kind,
    )(place, *lefts, *rights)
    return [v.reshape(2, -1, 1024) for v in outs]


def halve_kernel(count, *refs):
    total = refs[0][...].astype(f32)
    for part in refs[1:count]:
        total += part[...].astype(f32)
    total = total.astype(bf16)
    if len(refs) == count + 1:
        refs[count][...] = total
    else:
        refs[count][...] = total[0]
        refs[count + 1][...] = total[1]


def halve(*parts, split=True):
    _, rows, cols = parts[0].shape
    tile = min(rows, 128)
    block = pl.BlockSpec((2, tile, cols), lambda i: (0, i, 0))
    half = pl.BlockSpec((tile, cols), lambda i: (i, 0))
    outs = pl.pallas_call(
        functools.partial(halve_kernel, len(parts)),
        grid=(rows // tile,),
        out_shape=[jax.ShapeDtypeStruct((rows, cols), bf16)] * 2 if split else [jax.ShapeDtypeStruct((2, rows, cols), bf16)],
        in_specs=[block] * len(parts),
        out_specs=[half] * 2 if split else [block],
        cost_estimate=cheap(),
        name="halve",
    )(*parts)
    if not split:
        return outs[0]
    if rows == tile:
        return outs
    return [v.reshape(2, rows // 2, cols) for v in outs]


def plain_sum(pairs):
    grads = []
    for left, left_far, right, right_far in pairs:
        both = jnp.concatenate([right, right_far], -2)
        if both.ndim == 3:
            both = jnp.concatenate([both[0], both[1]], 1)
        both = dot(jnp.concatenate([left, left_far], 0), both, 0, 0)
        grads.append(both.astype(bf16).reshape(both.shape[0], 2, -1))
    grads = jnp.concatenate(grads, 2)
    mine = add(grads[:, 0], swap(grads[:, 1], "tp"))
    return [lax.psum_scatter(mine, "dp", scatter_dimension=0, tiled=True)]


def close_kernel(place, *refs):
    parts, (mine, send) = refs[:-2], refs[-2:]
    total = parts[0][...].astype(f32)
    for part in parts[1:]:
        total += part[...].astype(f32)
    rows = mine.shape[0]
    for core in range(2):

        @pl.when(place[2] == core)
        def _(core=core):
            mine[...] = total[core * rows : (core + 1) * rows]
            send[...] = total[(1 - core) * rows : (2 - core) * rows]


def close(place, parts):
    rows, cols = parts[0].shape
    return pl.pallas_call(
        close_kernel,
        out_shape=[jax.ShapeDtypeStruct((rows // 2, cols), f32)] * 2,
        in_specs=[pl.BlockSpec(memory_space=pltpu.SMEM)] + [pl.BlockSpec(memory_space=pltpu.VMEM)] * len(parts),
        out_specs=[pl.BlockSpec(memory_space=pltpu.VMEM)] * 2,
        cost_estimate=cheap(),
        name="close",
    )(place, *parts)


def settle_kernel(place, mine, other, *outs):
    size = mine.shape[1] // len(outs)
    for core in range(2):

        @pl.when(place[2] == core)
        def _(core=core):
            for n, out in enumerate(outs):
                for part, at in ((mine, core), (other, 1 - core)):
                    out[:, at * size : (at + 1) * size] = part[:, n * size : (n + 1) * size]


def settle_columns(place, pair, count):
    mine, send = pair
    other = swap(send, "ctx")
    rows, cols = mine.shape
    return pl.pallas_call(
        settle_kernel,
        out_shape=[jax.ShapeDtypeStruct((rows, 2 * cols // count), f32)] * count,
        in_specs=[pl.BlockSpec(memory_space=pltpu.SMEM)] + [pl.BlockSpec(memory_space=pltpu.VMEM)] * 2,
        out_specs=[pl.BlockSpec(memory_space=pltpu.VMEM)] * count,
        cost_estimate=cheap(),
        name="settle_columns",
    )(place, mine, other)


def body(dp_count, tokens, segments, query_weight, key_weight, value_weight, out_weight, up_weight, down_weight, query_bias, value_bias, out_bias, up_bias, down_bias, attn_gain, attn_shift, mlp_gain, mlp_shift, cotangent):
    c = lax.axis_index("ctx")
    t = lax.axis_index("tp")
    d = lax.axis_index("dp")
    place = jnp.stack([d // 2, d % 2, c, t]).astype(jnp.int32)
    half, width = tokens.shape[1], tokens.shape[2]
    rows = 2 * half
    inner = 2 * query_bias.shape[0]
    ff = 2 * up_bias.shape[0]
    piece_rows = query_weight.shape[0]

    one = jnp.stack([query_weight, key_weight, value_weight, out_weight.T], 1)
    one = one.reshape(piece_rows, 4, 2, -1).transpose(2, 0, 1, 3).reshape(2, piece_rows, -1)
    one = one.astype(bf16)
    piece = order(c, take(one, c), swap(take(one, 1 - c), "ctx"), 0)
    unit = piece.shape[1]
    quarter = unit // 4
    qkv_mine, out_mine = gather_weights(piece, ((0, 3 * quarter), (3 * quarter, quarter)), place, dp_count)
    w_qkv = (qkv_mine, swap(qkv_mine, "ctx"))
    w_out = (out_mine, swap(out_mine, "ctx"))
    rest = jnp.stack([up_weight.astype(bf16), down_weight.T.astype(bf16)])
    rest = lax.all_gather(rest, ("tp", "dp", "ctx"), axis=1, tiled=True)

    biases = jnp.concatenate([query_bias, value_bias, up_bias])
    biases = jnp.stack([biases, swap(biases, "tp")])
    hin = inner // 2

    def near(values):
        values = values.reshape(2, 2, -1).transpose(1, 0, 2)
        return jnp.where(c == 0, values, values[::-1])

    bias_q, bias_v = near(biases[:, :hin]), near(biases[:, hin : 2 * hin])
    bias_up = jnp.where(t == 0, biases[:, 2 * hin :], biases[::-1, 2 * hin :])
    bias_qkv = jnp.stack([bias_q, jnp.zeros_like(bias_q), bias_v], 2).reshape(2, -1)

    seq = 2 * t + c
    other_seq = 2 * t + 1 - c
    pair_mine = jnp.stack([take(tokens, seq), take(cotangent, seq), take(tokens, other_seq)])
    pair_send = jnp.stack([take(tokens, other_seq), take(cotangent, other_seq), take(tokens, seq)])
    got = swap(pair_send, "ctx")
    flat = order(c, pair_mine[0], got[0], 0)
    flat_far = order(c, pair_mine[2], got[2], 0)
    grad_output = order(c, pair_mine[1], got[1], 0)
    flat = tie(flat, flat_far, grad_output)
    seg = take(segments, seq)

    def far(values):
        return swap(values, "ctx")

    qkv = [(dot(flat, w_qkv[r], 1, 0) + bias_qkv[r]).astype(bf16) for r in range(2)]
    attended = [attend(qkv[r], seg) for r in range(2)]
    context = [a[0] for a in attended]
    probs = [a[1] for a in attended]
    resid_one = flat.astype(f32) + dot(context[0], w_out[0], 1, 1) + dot(context[1], w_out[1], 1, 1) + out_bias
    normed_one, unit_one, inverse_one = norm_forward(resid_one, attn_gain, attn_shift)
    normed_low = normed_one.astype(bf16)
    normed_far, context_far = far(normed_low), far(context[1])
    normed_low = tie(normed_low, normed_far, context_far)
    hidden_near, hidden_far, output, grad_two, grad_mixed, pre_near, pre_far, sums_two, sums_pre = mlp(
        place, normed_low, rest, bias_up, normed_one, grad_output, down_bias, mlp_gain, mlp_shift
    )
    hidden_far, pre_got, grad_mixed_far = far(hidden_far), far(pre_far), far(grad_mixed)

    layer_all = lax.all_gather(output, ("tp", "ctx"), axis=0, tiled=False)
    grad_one, grad_attended, *grad_context, sums_one = mlp_back(
        place, pre_near, pre_far, rest, grad_two, unit_one, inverse_one, attn_gain, *w_out, ()
    )
    quick = dp_count == 8
    down_pairs = [(tie(grad_mixed, grad_attended), grad_mixed_far, hidden_near, hidden_far)]
    up_pairs = [(normed_low, normed_far, pre_near, pre_got)]
    if quick:
        down_keep, down_send = weight_grad(place, down_pairs, "x")
        up_keep, up_send = weight_grad(place, up_pairs, "tp")
        sent = (down_send, up_send)
    else:
        down_last, up_last, sent = plain_sum(down_pairs), plain_sum(up_pairs), ()
    back = [attend_back(qkv[r], probs[r], grad_context[r], sent) for r in range(2)]
    grad_qkv = [b[0] for b in back]
    sums = jnp.stack([b[1] for b in back])[:, :, :, 0]
    grad_qkv_far = far(grad_qkv[1])
    attended_far = far(grad_attended)
    one_pairs = [(flat, flat_far, grad_qkv[0], grad_qkv_far), (grad_attended, attended_far, context[0], context_far)]
    if quick:
        one_keep, one_send, two_keep, two_send = weight_grad(place, one_pairs, "one")
        down_keep, down_send = halve(tie(down_keep, one_send), over("x", down_send))
        one_got, two_got = over("t", one_send), over("x", two_send)
        up_keep, up_send = halve(tie(up_keep, two_got), over("t", up_send))
        up_got = over("x", up_send)
        down_got = over("l", down_send)
    else:
        one_last = plain_sum(one_pairs)
    if quick:
        grad_qkv = [tie(g, down_send) for g in grad_qkv]
    sent_back = dot(grad_qkv[0], w_qkv[0], 1, 1) + dot(grad_qkv[1], w_qkv[1], 1, 1)
    input_grad = (grad_one + sent_back).astype(bf16).reshape(2, half, width)
    got = swap(take(input_grad, 1 - c), "ctx")
    input_grad = order(c, take(input_grad, c)[None], got[None], 0)
    if quick:
        sums_one, sums_two, sums_pre = (tie(v, down_send) for v in (sums_one, sums_two, sums_pre))
    sums_one, sums_two = jnp.sum(sums_one, 1), jnp.sum(sums_two, 1)

    def settle(values):
        values = jnp.where(c == 0, values, values[::-1])
        values = jnp.where(t == 0, values, values[:, ::-1])
        return values.transpose(1, 0, 2).reshape(-1)

    small = jnp.concatenate(
        [settle(sums[:, :, 0]), settle(sums[:, :, 1]), settle(jnp.sum(sums_pre, 1).reshape(2, 2, -1)), sums_one[2], sums_two[2], sums_one[0], sums_one[1], sums_two[0], sums_two[1]]
    )
    small = tie(small.reshape(-1, 128), layer_all)
    small = lax.all_gather(small, ("dp", "ctx", "tp"), axis=0, tiled=False)
    small = jnp.sum(small, axis=0).reshape(-1)

    def cut_tp(start, size):
        return lax.dynamic_slice_in_dim(small, start + t * (size // 2), size // 2)

    at = 2 * inner + ff
    vectors = [lax.slice_in_dim(small, at + i * width, at + (i + 1) * width) for i in range(6)]

    if quick:
        two_keep, two_send = halve(tie(two_keep, down_got), two_got)
        one_keep, one_send = halve(one_keep, one_got)
        two_got, one_got = over("t", two_send), over("x", one_send)
        down_keep, down_send = halve(down_keep, down_got)
        down_got = over("h", down_send)
        low_got = over("l", halve(tie(two_keep, up_got), two_got, split=False))
        up_keep, up_send = halve(up_keep, up_got)
        up_got = over("l", up_send)
        down_keep, down_send = halve(down_keep, down_got)
        layer_out = lax.dynamic_slice_in_dim(tie(layer_all, two_send), c * half, half, 1)
        one_keep, one_send = halve(tie(one_keep, up_got, layer_out, small), one_got, low_got)
        up_keep, up_send = halve(up_keep, up_got)
        up_last = (up_keep, over("h", up_send))
        down_last = (down_keep, over("t", down_send))
        one_last = (one_keep, over("h", one_send))
        down_last, up_last = ((tie(keep, one_send), got) for keep, got in (down_last, up_last))
    input_grad = order(t, input_grad, swap(input_grad, "tp"), 0)
    if not quick:
        layer_out = lax.dynamic_slice_in_dim(layer_all, c * half, half, 1)
    if quick:
        one_last = (tie(one_last[0], input_grad), one_last[1])
    (down_shard,) = settle_columns(place, close(place, down_last), 1)
    (up_shard,) = settle_columns(place, close(place, up_last), 1)
    one_shard = settle_columns(place, close(place, one_last), 4)
    return (
        layer_out,
        input_grad,
        *one_shard[:3],
        one_shard[3].T,
        up_shard,
        down_shard.T,
        cut_tp(0, inner),
        cut_tp(inner, inner),
        vectors[0],
        cut_tp(2 * inner, ff),
        *vectors[1:],
    )


def solution(mesh):
    weight_in, weight_out = P(("dp", "ctx"), "tp"), P("tp", ("dp", "ctx"))
    rows = P("dp", "ctx", None)
    weights = (weight_in, weight_in, weight_in, weight_out, weight_in, weight_out)
    vectors = (P("tp"), P("tp"), P(), P("tp"), P(), P(), P(), P(), P())
    dp_count = mesh.shape["dp"]

    def run(*args):
        return body(dp_count, *args)

    return jax.shard_map(
        run,
        mesh=mesh,
        in_specs=(rows, P("dp", None), *weights, *vectors, rows),
        out_specs=(rows, rows, *weights, *vectors),
        check_vma=False,
    )
```
